32 devices in a mesh: dp: 16 (over z, x, core), mp: 2 (over y).
Axes of the slice: x: 2, y: 2, z: 4, core: 2. Of those that a mesh axis runs over, the one named last changes fastest.
Arguments:
- tokens: bfloat16 [2, 16, 1280, 1024], P(None, 'dp', 'mp'), may hold values from -6 to 6
- cotangent: bfloat16 [2, 16, 1280, 1024], P(None, 'dp', 'mp'), may hold values from -6 to 6
- patch_count: int32 [2, 16], P(None, 'dp'), may hold values from 256 to 576, as said below
- first_gain: float32 [1024], replicated, may hold values from 0.25 to 1.75
- first_shift: float32 [1024], replicated, may hold values from -1.75 to 1.75
- heads_weight: bfloat16 [1024, 3, 1024], P(None, None, 'mp'), may hold values from -0.1875 to 0.1875
- heads_bias: float32 [3, 1024], P(None, 'mp'), may hold values from -1.75 to 1.75
- merge_weight: bfloat16 [1024, 1024], P('mp'), may hold values from -3 to 3
- merge_bias: float32 [1024], replicated, may hold values from -1.75 to 1.75
- second_gain: float32 [1024], replicated, may hold values from 0.25 to 1.75
- second_shift: float32 [1024], replicated, may hold values from -1.75 to 1.75
- expand_weight: bfloat16 [1024, 4096], P(None, 'mp'), may hold values from -0.1875 to 0.1875
- expand_bias: float32 [4096], P('mp'), may hold values from -3 to 3
- reduce_weight: bfloat16 [4096, 1024], P('mp'), may hold values from -0.09375 to 0.09375
- reduce_bias: float32 [1024], replicated, may hold values from -1.75 to 1.75
Outputs:
- layer_out: bfloat16 [2, 16, 1280, 1024], P(None, 'dp', 'mp')
- tokens_grad: float32 [2, 16, 1280, 1024], P(None, 'dp', 'mp')
- first_gain_grad: float32 [1024], replicated
- first_shift_grad: float32 [1024], replicated
- heads_weight_grad: float32 [1024, 3, 1024], P(None, None, 'mp')
- heads_bias_grad: float32 [3, 1024], P(None, 'mp')
- merge_weight_grad: float32 [1024, 1024], P('mp')
- merge_bias_grad: float32 [1024], replicated
- second_gain_grad: float32 [1024], replicated
- second_shift_grad: float32 [1024], replicated
- expand_weight_grad: float32 [1024, 4096], P(None, 'mp')
- expand_bias_grad: float32 [4096], P('mp')
- reduce_weight_grad: float32 [4096, 1024], P('mp')
- reduce_bias_grad: float32 [1024], replicated
The draws below stay inside these ranges and needn't reach their ends.
Inputs may be any that keep to these rules, and one draw needn't show every extreme that they name: `patch_count`: each entry is 256 or 576, and exactly half of the entries are each.
All inputs are finite; a program needn't handle non-finite values.
Results may differ from the reference program's by a relative error of at most 0.017.
Values may be sent and summed in bfloat16 or wider, within the bound.
No kernel may reach another device: no remote copies, remote signals or barrier semaphores. Data moves between devices by JAX's collectives and lax.ppermute only.
A program may use at most 320 MiB of HBM per device.

```python
import math
import jax
import jax.numpy as jnp
from jax import lax

D = 1024
FF = 4096
HEADS = 16
HEAD_DIM = 64
FRAMES = 2
SIDE_SMALL = 16
SIDE_LARGE = 24
MB = 2
SLOTS = 1280
GROUPS = 16


def draw_patch_count(key, part):
    key = jax.random.fold_in(key, 11)
    ordering = jax.random.permutation(key, MB * GROUPS)
    large_count = SIDE_LARGE * SIDE_LARGE
    small_count = SIDE_SMALL * SIDE_SMALL
    return jnp.where(ordering % 2 == 0, large_count, small_count).astype(jnp.int32).reshape(MB, GROUPS)


def steps_of(rng, dims, cuts, low, largest):
    loudness = 1.0
    for dim, blocks in cuts:
        steps = jax.random.uniform(jax.random.fold_in(jax.random.fold_in(rng, 6), dim), (blocks,), jnp.float32, low / len(cuts), largest / len(cuts))
        loudness = loudness * jnp.repeat(jnp.exp(steps), dims[dim] // blocks).reshape((-1,) + (1,) * (len(dims) - 1 - dim))
    return loudness


def noise(rng, extent, scale, limit, split=(), kind=jnp.bfloat16):
    result = jax.random.normal(rng, extent, jnp.float32) * scale
    if len(split) > 0:
        result = steps_of(rng, extent, split, -0.22, 0.18) * result
    return jnp.clip(result, min=-limit, max=limit).astype(kind)


def setup_inputs(seed: int = 0) -> dict:
    splits = jax.random.split(jax.random.key(seed), 16)
    return {
        "tokens": noise(splits[0], (MB, GROUPS, SLOTS, D), 1.0, 6.0, ((1, 16), (2, 2))),
        "cotangent": noise(splits[1], (MB, GROUPS, SLOTS, D), 1.0, 6.0, ((1, 16), (2, 2))),
        "patch_count": draw_patch_count(jax.random.fold_in(splits[15], 71), 0),
        "first_gain": jnp.clip(1.0 + 0.15 * jax.random.normal(splits[3], (D,), jnp.float32), 0.25, 1.75),
        "first_shift": noise(splits[4], (D,), 0.3, 1.75, (), jnp.float32),
        "heads_weight": noise(splits[5], (D, 3, D), D ** -0.5, 0.1875, ((2, 2),)),
        "heads_bias": noise(splits[6], (3, D), 0.3, 1.75, ((1, 2),), jnp.float32),
        "merge_weight": noise(splits[7], (D, D), 4 ** -0.5, 3.0, ((0, 2),)),
        "merge_bias": noise(splits[8], (D,), 0.3, 1.75, (), jnp.float32),
        "second_gain": jnp.clip(1.0 + 0.15 * jax.random.normal(splits[9], (D,), jnp.float32), 0.25, 1.75),
        "second_shift": noise(splits[10], (D,), 0.3, 1.75, (), jnp.float32),
        "expand_weight": noise(splits[11], (D, FF), D ** -0.5, 0.1875, ((1, 2),)),
        "expand_bias": noise(splits[12], (FF,), 0.5, 3.0, ((0, 2),), jnp.float32),
        "reduce_weight": noise(splits[13], (FF, D), FF ** -0.5, 0.09375, ((0, 2),)),
        "reduce_bias": noise(splits[14], (D,), 0.3, 1.75, (), jnp.float32),
    }


EPSILON = 1e-06
MASKED = -1e+30
HIGHEST = lax.Precision.HIGHEST

@jax.custom_vjp
def low(v):
    return lax.optimization_barrier(v.astype(jnp.bfloat16)).astype(jnp.float32)

@jax.custom_vjp
def low_back(v):
    return v

def low_keep(v):
    return (low(v), None)

def low_pass(kept, grad):
    return (grad,)

def back_keep(v):
    return (v, None)

def back_low(kept, grad):
    return (low(grad),)
low.defvjp(low_keep, low_pass)
low_back.defvjp(back_keep, back_low)

def slot_layout(count_one, length):
    large_count = SIDE_LARGE * SIDE_LARGE
    grid_side = jnp.where(count_one == large_count, SIDE_LARGE, SIDE_SMALL).astype(jnp.int32)
    frame_len = grid_side * grid_side + 2
    clip_len = FRAMES * frame_len
    clip_total = jnp.where(count_one == large_count, 1, 2).astype(jnp.int32)
    slot_id = jnp.arange(length, dtype=jnp.int32)
    clip_id = jnp.minimum(slot_id // clip_len, clip_total)
    offset_in = slot_id - clip_id * clip_len
    frame_id = offset_in // frame_len
    place_in = offset_in - frame_id * frame_len - 2
    patch_id = jnp.maximum(place_in, 0)
    is_live = clip_id < clip_total
    is_patch = is_live & (place_in >= 0)
    frame_id = jnp.where(is_live, frame_id, 0)
    patch_row = jnp.where(is_patch, patch_id // grid_side, 0)
    column = jnp.where(is_patch, patch_id - patch_id // grid_side * grid_side, 0)
    return (clip_id, frame_id, patch_row, column)

def rotary_tables(frame_id, patch_row, column, head_width):
    segment = 2 * (head_width // 3 // 2)
    half_width = segment // 2
    dim_index = jnp.arange(head_width, dtype=jnp.int32)
    segment_id = dim_index // segment
    exponent = (dim_index % segment % half_width).astype(jnp.float32)
    frequency = jnp.exp(exponent * (-math.log(10000.0) / half_width))
    position = jnp.where(segment_id == 0, 1.0, 0.0).astype(jnp.float32)[None, :] * frame_id[:, None].astype(jnp.float32) + jnp.where(segment_id == 1, 1.0, 0.0).astype(jnp.float32)[None, :] * patch_row[:, None].astype(jnp.float32) + jnp.where(segment_id == 2, 1.0, 0.0).astype(jnp.float32)[None, :] * column[:, None].astype(jnp.float32)
    angles = position * frequency[None, :]
    return (jnp.cos(angles)[:, None, :], jnp.sin(angles)[:, None, :])

def partner(values_in):
    head_width = values_in.shape[-1]
    segment = 2 * (head_width // 3 // 2)
    half_width = segment // 2
    pieces_out = []
    for number in range(3):
        offset = number * segment
        pieces_out.append(-values_in[..., offset + half_width:offset + segment])
        pieces_out.append(values_in[..., offset:offset + half_width])
    pieces_out.append(jnp.zeros_like(values_in[..., 3 * segment:]))
    return jnp.concatenate(pieces_out, -1)

def rotate(values_in, cos_table, sin_table):
    return values_in * cos_table + partner(values_in) * sin_table

def standardize(values_in):
    row_mean = lax.optimization_barrier(jnp.mean(values_in, -1, keepdims=True))
    centred = values_in - row_mean
    norm_scale = lax.rsqrt(lax.optimization_barrier(jnp.mean(centred * centred, -1, keepdims=True)) + EPSILON)
    return (centred * norm_scale, norm_scale)

def product(left, right):
    return jnp.dot(left, right, precision=HIGHEST)

def head_attention(query_rows, key_rows, value_rows, allowed):
    scores = low_back(product(query_rows, key_rows.T) * HEAD_DIM ** (-0.5))
    scores = jnp.where(allowed, scores, MASKED)
    row_max = lax.optimization_barrier(jnp.max(scores, -1, keepdims=True))
    exp_scores = jnp.exp(scores - row_max)
    softmax_out = low(exp_scores / lax.optimization_barrier(jnp.sum(exp_scores, -1, keepdims=True)))
    return product(softmax_out, value_rows)

def forward(weights, stream, cos_table, sin_table, allowed):
    first_gain, first_shift, heads_weight, heads_bias, merge_weight, merge_bias, second_gain, second_shift, expand_weight, expand_bias, reduce_weight, reduce_bias = weights
    length = stream.shape[0]
    first_out = low(standardize(stream)[0] * first_gain + first_shift)
    head_proj = low_back(jnp.einsum('sd,dkf->skf', first_out, heads_weight, precision=HIGHEST) + heads_bias)
    head_proj = head_proj.reshape(length, 3, HEADS, HEAD_DIM)
    queries = low(rotate(head_proj[:, 0], cos_table, sin_table)).transpose(1, 0, 2)
    keys = low(rotate(head_proj[:, 1], cos_table, sin_table)).transpose(1, 0, 2)
    values = low(head_proj[:, 2]).transpose(1, 0, 2)

    def per_head(pieces):
        return head_attention(pieces[0], pieces[1], pieces[2], allowed)
    mixed_heads = lax.map(jax.checkpoint(per_head), (queries, keys, values))
    mixed_heads = low(low_back(mixed_heads.transpose(1, 0, 2).reshape(length, D)))
    residual = stream + low_back(product(mixed_heads, merge_weight) + merge_bias)
    second_out = low(standardize(residual)[0] * second_gain + second_shift)
    pre_gelu = low_back(product(second_out, expand_weight) + expand_bias)
    active = low(jax.nn.gelu(pre_gelu, approximate=False))
    return residual + low_back(product(active, reduce_weight) + reduce_bias)

def reference(tokens, cotangent, patch_count, first_gain, first_shift, heads_weight, heads_bias, merge_weight, merge_bias, second_gain, second_shift, expand_weight, expand_bias, reduce_weight, reduce_bias):
    params = (first_gain.astype(jnp.float32), first_shift.astype(jnp.float32), heads_weight.astype(jnp.float32), heads_bias.astype(jnp.float32), merge_weight.astype(jnp.float32), merge_bias.astype(jnp.float32), second_gain.astype(jnp.float32), second_shift.astype(jnp.float32), expand_weight.astype(jnp.float32), expand_bias.astype(jnp.float32), reduce_weight.astype(jnp.float32), reduce_bias.astype(jnp.float32))
    token_rows = tokens.reshape(MB * GROUPS, SLOTS, D)
    upstream = cotangent.reshape(MB * GROUPS, SLOTS, D)
    patch_counts = patch_count.reshape(MB * GROUPS)

    def buffer_step(grad_totals, pieces):
        stream = pieces[0].astype(jnp.float32)
        clip_id, frame_id, patch_row, column = slot_layout(pieces[2], SLOTS)
        cos_table, sin_table = rotary_tables(frame_id, patch_row, column, HEAD_DIM)
        allowed = (clip_id[:, None] == clip_id[None, :]) & (frame_id[None, :] <= frame_id[:, None])

        def apply_layer(weights, inputs):
            return forward(weights, inputs, cos_table, sin_table, allowed)
        layer_out, pullback = jax.vjp(apply_layer, params, stream)
        gradients, stream_grad = pullback(pieces[1].astype(jnp.float32))
        grad_totals = jax.tree.map(jnp.add, grad_totals, gradients)
        return (grad_totals, (layer_out.astype(jnp.bfloat16), stream_grad))
    initial = jax.tree.map(jnp.zeros_like, params)
    grad_totals, (outputs, stream_grads) = lax.scan(buffer_step, initial, (token_rows, upstream, patch_counts))
    return (outputs.reshape(MB, GROUPS, SLOTS, D), stream_grads.reshape(MB, GROUPS, SLOTS, D), grad_totals[0], grad_totals[1], grad_totals[2], grad_totals[3], grad_totals[4], grad_totals[5], grad_totals[6], grad_totals[7], grad_totals[8], grad_totals[9], grad_totals[10], grad_totals[11])
```

```python
import functools
import math

import jax
import jax.numpy as jnp
from jax import lax
from jax.experimental import pallas as pl
from jax.experimental.pallas import tpu as pltpu
from jax.sharding import PartitionSpec as P

HEAD_DIM = 64
FRAMES = 2
SIDE_SMALL = 16
SIDE_LARGE = 24
EPSILON = 1e-06
ROOT_HALF = 0.7071067811865476
GAUSS_NORM = 0.3989422804014327
MIB = 2**20

PAIR = 128
NEG = -1e30
STRIPS = ((0, 512, 592), (512, 640, 1168), (640, 1024, 1168), (1024, 1280, 1280))

def strips(bq):
    out = []
    for a, b, stop in STRIPS:
        for s in range(a, b, bq):
            out.append((s, min(s + bq, b), stop))
    return out

def fwd_kernel(bq, q_ref, k_ref, v_ref, lo_ref, hi_ref, o_ref, rl_ref, ea_ref, eb_ref):
    lane = lax.broadcasted_iota(jnp.int32, (1, PAIR), 1)
    c = (64 ** -0.5) * math.log2(math.e)
    vt = v_ref[...].T
    for (a, b, stop) in strips(bq):
        n = b - a
        q = q_ref[a:b, :]
        lo = lo_ref[:, a:b]
        hi = hi_ref[:, a:b]
        key = lax.broadcasted_iota(jnp.int32, (stop, n), 0)
        ok = (key >= lo) & (key < hi)
        outs, rls = [], []
        for h in range(2):
            qm = jnp.where((lane >= 64) == (h == 1), q, jnp.zeros_like(q))
            s = lax.dot_general(k_ref[0:stop, :], qm, (((1,), (1,)), ((), ())), preferred_element_type=jnp.float32)
            s = jnp.where(ok, s, NEG)
            m = jnp.max(s, 0, keepdims=True)
            e = jnp.exp2((s - m) * c)
            l = jnp.sum(e, 0, keepdims=True)
            eb16 = e.astype(jnp.bfloat16)
            if b <= 512:
                ea_ref[h, :, a:b] = eb16
            else:
                eb_ref[h, 0:stop, a - 512:b - 512] = eb16
            ot = lax.dot_general(vt[h * 64:(h + 1) * 64, 0:stop], eb16, (((1,), (0,)), ((), ())), preferred_element_type=jnp.float32)
            rl = 1.0 / l
            outs.append(ot * rl)
            rls.append(jnp.broadcast_to(rl, (64, n)))
        o_ref[a:b, :] = jnp.concatenate(outs, 0).T.astype(jnp.bfloat16)
        rl_ref[a:b, :] = jnp.concatenate(rls, 0).T

def attn_fwd(q, k, v, lo, hi, bq=256):
    rows, width = q.shape
    pairs = width // PAIR
    full = lambda i: (0, i)
    return pl.pallas_call(
        functools.partial(fwd_kernel, bq),
        grid=(pairs,),
        in_specs=[pl.BlockSpec((rows, PAIR), full)] * 3 + [pl.BlockSpec((1, rows), lambda i: (0, 0))] * 2,
        out_specs=[pl.BlockSpec((rows, PAIR), full), pl.BlockSpec((rows, PAIR), full),
                   pl.BlockSpec((2, 592, 512), lambda i: (i, 0, 0)), pl.BlockSpec((2, 1280, 768), lambda i: (i, 0, 0))],
        out_shape=[jax.ShapeDtypeStruct((rows, width), jnp.bfloat16), jax.ShapeDtypeStruct((rows, width), jnp.float32),
                   jax.ShapeDtypeStruct((2 * pairs, 592, 512), jnp.bfloat16), jax.ShapeDtypeStruct((2 * pairs, 1280, 768), jnp.bfloat16)],
        compiler_params=pltpu.CompilerParams(vmem_limit_bytes=50 * 2**20),
        name="attend",
    )(q, k, v, lo, hi)

def spin(x, cos, sa, sb):
    return x * cos + pltpu.roll(x, PAIR - 10, 1) * sa + pltpu.roll(x, 10, 1) * sb

def bwd_kernel(bq, q_ref, k_ref, v_ref, g_ref, o_ref, rl_ref, ea_ref, eb_ref, cos_ref, sa_ref, sb_ref,
               gq_ref, gk_ref, gv_ref, cs_ref, dk_acc, dv_acc, dqt_acc):
    lane = lax.broadcasted_iota(jnp.int32, (1, PAIR), 1)
    scale = 64 ** -0.5
    kt = k_ref[...].T
    rows = q_ref.shape[0]
    done = 0
    for (a, b, stop) in strips(bq)[::-1]:
        n = b - a
        q = q_ref[a:b, :]
        gf = g_ref[a:b, :].astype(jnp.float32) * rl_ref[a:b, :]
        go = (gf * o_ref[a:b, :].astype(jnp.float32)).T
        g = gf.astype(jnp.bfloat16)
        dk = dv = None
        for h in range(2):
            mask = (lane >= 64) == (h == 1)
            qm = jnp.where(mask, q, jnp.zeros_like(q))
            gm = jnp.where(mask, g, jnp.zeros_like(g))
            delta = jnp.sum(go[h * 64:(h + 1) * 64, :], 0, keepdims=True)
            dpt = lax.dot_general(v_ref[0:stop, :], gm, (((1,), (1,)), ((), ())), preferred_element_type=jnp.float32)
            e = ea_ref[h, :, a:b] if b <= 512 else eb_ref[h, 0:stop, a - 512:b - 512]
            ds = (e.astype(jnp.float32) * (dpt - delta)).astype(jnp.bfloat16)
            dqt_acc[h * 64:(h + 1) * 64, a:b] = lax.dot_general(kt[h * 64:(h + 1) * 64, 0:stop], ds, (((1,), (0,)), ((), ())), preferred_element_type=jnp.float32)
            dk_h = jnp.dot(ds, qm, preferred_element_type=jnp.float32)
            dv_h = jnp.dot(e, gm, preferred_element_type=jnp.float32)
            dk = dk_h if dk is None else dk + dk_h
            dv = dv_h if dv is None else dv + dv_h
        if done == 0:
            assert stop == rows
            dk_acc[...] = dk
            dv_acc[...] = dv
            done = 1
        else:
            dk_acc[0:stop, :] += dk
            dv_acc[0:stop, :] += dv
    cos, sa, sb = cos_ref[...], -sa_ref[...], -sb_ref[...]
    gq = spin(dqt_acc[...].T * scale, cos, sa, sb).astype(jnp.bfloat16)
    gk = spin(dk_acc[...] * scale, cos, sa, sb).astype(jnp.bfloat16)
    gv = dv_acc[...].astype(jnp.bfloat16)
    gq_ref[...] = gq
    gk_ref[...] = gk
    gv_ref[...] = gv
    f = lambda x: jnp.broadcast_to(jnp.sum(x.astype(jnp.float32), 0, keepdims=True), (8, PAIR))
    cs_ref[0] = f(gq)
    cs_ref[1] = f(gk)
    cs_ref[2] = f(gv)

def attn_bwd(q, k, v, g, o, rl, ea, eb, cos, sa, sb, bq=256):
    rows, width = q.shape
    pairs = width // PAIR
    full = lambda i: (0, i)
    blk = pl.BlockSpec((rows, PAIR), full)
    tab = pl.BlockSpec((rows, PAIR), lambda i: (0, 0))
    return pl.pallas_call(
        functools.partial(bwd_kernel, bq),
        grid=(pairs,),
        in_specs=[blk] * 6 + [pl.BlockSpec((2, 592, 512), lambda i: (i, 0, 0)), pl.BlockSpec((2, 1280, 768), lambda i: (i, 0, 0))] + [tab] * 3,
        out_specs=[blk] * 3 + [pl.BlockSpec((3, 8, PAIR), lambda i: (0, 0, i))],
        out_shape=[jax.ShapeDtypeStruct((rows, width), jnp.bfloat16)] * 3 + [jax.ShapeDtypeStruct((3, 8, width), jnp.float32)],
        scratch_shapes=[pltpu.VMEM((rows, PAIR), jnp.float32), pltpu.VMEM((rows, PAIR), jnp.float32), pltpu.VMEM((PAIR, rows), jnp.float32)],
        compiler_params=pltpu.CompilerParams(vmem_limit_bytes=56 * 2**20),
        name="attend_back",
    )(q, k, v, g, o, rl, ea, eb, cos, sa, sb)


def slot_layout(count_one, length):
    large_count = SIDE_LARGE * SIDE_LARGE
    grid_side = jnp.where(count_one == large_count, SIDE_LARGE, SIDE_SMALL).astype(jnp.int32)
    frame_len = grid_side * grid_side + 2
    clip_len = FRAMES * frame_len
    clip_total = jnp.where(count_one == large_count, 1, 2).astype(jnp.int32)
    slot_id = jnp.arange(length, dtype=jnp.int32)
    clip_id = jnp.minimum(slot_id // clip_len, clip_total)
    offset_in = slot_id - clip_id * clip_len
    frame_id = offset_in // frame_len
    place_in = offset_in - frame_id * frame_len - 2
    patch_id = jnp.maximum(place_in, 0)
    is_live = clip_id < clip_total
    is_patch = is_live & (place_in >= 0)
    frame_id = jnp.where(is_live, frame_id, 0)
    patch_row = jnp.where(is_patch, patch_id // grid_side, 0)
    column = jnp.where(is_patch, patch_id - patch_id // grid_side * grid_side, 0)
    first_key = clip_id * clip_len
    past_key = jnp.where(is_live, first_key + (frame_id + 1) * frame_len, length)
    return (first_key, past_key, frame_id, patch_row, column)


def rotary_tables(frame_id, patch_row, column):
    segment = 2 * (HEAD_DIM // 3 // 2)
    half_width = segment // 2
    dim_index = jnp.arange(PAIR, dtype=jnp.int32) % HEAD_DIM
    segment_id = dim_index // segment
    exponent = (dim_index % segment % half_width).astype(jnp.float32)
    frequency = jnp.exp(exponent * (-math.log(10000.0) / half_width))
    pick = lambda number: jnp.where(segment_id == number, 1.0, 0.0).astype(jnp.float32)[None, :]
    position = (
        pick(0) * frame_id[:, None].astype(jnp.float32)
        + pick(1) * patch_row[:, None].astype(jnp.float32)
        + pick(2) * column[:, None].astype(jnp.float32)
    )
    angles = position * frequency[None, :]
    lower = (dim_index % segment < half_width)[None, :]
    turning = (segment_id < 3)[None, :]
    sine = jnp.where(turning, jnp.sin(angles), 0.0)
    return (jnp.cos(angles), jnp.where(lower, -sine, 0.0), jnp.where(lower, 0.0, sine))


def project_kernel(x_ref, w_ref, b_ref, cos_ref, up_ref, down_ref, out_ref):
    y = jnp.dot(x_ref[...], w_ref[0], preferred_element_type=jnp.float32) + b_ref[0]
    part = pl.program_id(0)

    @pl.when(part == 2)
    def _():
        out_ref[0] = y.astype(jnp.bfloat16)

    @pl.when(part < 2)
    def _():
        cos, up, down = cos_ref[...], up_ref[...], down_ref[...]
        for at in range(0, y.shape[1], PAIR):
            out_ref[0, :, at : at + PAIR] = spin(y[:, at : at + PAIR], cos, up, down).astype(
                jnp.bfloat16
            )


def project(x, weight, bias, tables):
    rows, depth = x.shape
    width = weight.shape[2]
    table = pl.BlockSpec((rows, PAIR), lambda i: (0, 0))
    return pl.pallas_call(
        project_kernel,
        grid=(3,),
        in_specs=[
            pl.BlockSpec((rows, depth), lambda i: (0, 0)),
            pl.BlockSpec((1, depth, width), lambda i: (i, 0, 0)),
            pl.BlockSpec((1, 1, width), lambda i: (i, 0, 0)),
            table,
            table,
            table,
        ],
        out_specs=pl.BlockSpec((1, rows, width), lambda i: (i, 0, 0)),
        out_shape=jax.ShapeDtypeStruct((3, rows, width), jnp.bfloat16),
        compiler_params=pltpu.CompilerParams(vmem_limit_bytes=50 * MIB),
        name="project",
    )(x, weight, bias[:, None, :], *tables)


def standardize(values_in):
    row_mean = jnp.mean(values_in, -1, keepdims=True)
    centred = values_in - row_mean
    norm_scale = lax.rsqrt(jnp.mean(centred * centred, -1, keepdims=True) + EPSILON)
    return (centred * norm_scale, norm_scale)


def norm_back(grad_in, normed, norm_scale):
    return norm_scale * (
        grad_in
        - jnp.mean(grad_in, -1, keepdims=True)
        - normed * jnp.mean(grad_in * normed, -1, keepdims=True)
    )


def column_sums(matrix):
    unit_column = jnp.ones((matrix.shape[0],), matrix.dtype)
    return jnp.dot(unit_column, matrix, preferred_element_type=jnp.float32)


def dot(left, right):
    return jnp.dot(left, right, preferred_element_type=jnp.float32)


def dot_nt(left, right):
    return lax.dot_general(
        left, right, (((1,), (1,)), ((), ())), preferred_element_type=jnp.float32
    )


def dot_tn(left, right):
    return lax.dot_general(
        left, right, (((0,), (0,)), ((), ())), preferred_element_type=jnp.float32
    )


def low(array):
    return array.astype(jnp.bfloat16)


def wide(array):
    return array.astype(jnp.float32)


def on_device(
    spread,
    tokens,
    cotangent,
    patch_count,
    first_gain,
    first_shift,
    heads_weight,
    heads_bias,
    merge_weight,
    merge_bias,
    second_gain,
    second_shift,
    expand_weight,
    expand_bias,
    reduce_weight,
    reduce_bias,
):
    levels = spread.bit_length() - 1
    place = lax.axis_index("dp")
    side = lax.axis_index("mp")

    def bit(level):
        return (place >> level) & 1

    def swap(array, level):
        return lax.ppermute(array, "dp", [(i, i ^ (1 << level)) for i in range(spread)])

    def cross(array):
        return lax.ppermute(array, "mp", [(0, 1), (1, 0)])

    def ordered(flag, mine, theirs):
        return jnp.where(
            flag == 0,
            jnp.concatenate([mine, theirs], 0),
            jnp.concatenate([theirs, mine], 0),
        )

    def half_of(array, flag):
        size = array.shape[0] // 2
        return lax.dynamic_slice_in_dim(array, flag * size, size, 0)

    def scatter(array, levels_in):
        for level in levels_in:
            arrived = swap(half_of(array, 1 - bit(level)), level)
            array = low(wide(half_of(array, bit(level))) + wide(arrived))
        return array

    def gather(array, levels_in):
        for level in levels_in[::-1]:
            array = ordered(bit(level), array, swap(array, level))
        return array

    def fetch(array):
        near = list(range(min(3, levels)))
        piece = array
        for level in near:
            piece = half_of(piece, bit(level))
        return gather(cross(piece), near)

    def whole_rows(array):
        mine = lax.dynamic_index_in_dim(array[:, 0], side, 0, False)
        other = lax.dynamic_index_in_dim(array[:, 0], 1 - side, 0, False)
        return ordered(side, mine, cross(other))

    def give_back(array):
        size = array.shape[0] // 2
        mine = half_of(array, side)
        arrived = cross(half_of(array, 1 - side))
        return ordered(side, mine[None], arrived[None])[:, None]

    stream = whole_rows(tokens)
    length = stream.shape[0]
    heads_own = heads_weight.transpose(1, 0, 2)
    heads_width = heads_own.shape[2]
    heads_far = fetch(heads_own.reshape(-1, heads_width)).reshape(heads_own.shape)
    biases = jnp.concatenate([heads_bias.reshape(-1), expand_bias])
    biases_far = cross(biases)
    heads_biases = (heads_bias, biases_far[: heads_bias.size].reshape(heads_bias.shape))
    expand_biases = (expand_bias, biases_far[heads_bias.size :])
    merge_far = fetch(merge_weight)
    expand_far = fetch(expand_weight)
    reduce_far = fetch(reduce_weight)
    heads_both = (heads_own, heads_far)
    merge_both = (merge_weight, merge_far)
    expand_both = (expand_weight, expand_far)
    reduce_both = (reduce_weight, reduce_far)
    grad_two = whole_rows(cotangent)

    count_one = lax.dynamic_index_in_dim(patch_count[:, 0], side, 0, False)
    first_key, past_key, frame_id, patch_row, column = slot_layout(count_one, length)
    tables = rotary_tables(frame_id, patch_row, column)
    first_key, past_key = first_key[None], past_key[None]

    stream = wide(stream)
    first_norm, first_scale = standardize(stream)
    first_out = low(first_norm * first_gain + first_shift)
    parts = (0, 1)
    heads = [project(first_out, heads_both[p], heads_biases[p], tables) for p in parts]
    seen = [attn_fwd(heads[p][0], heads[p][1], heads[p][2], first_key, past_key, 512) for p in parts]
    mixed = [seen[p][0] for p in parts]
    residual = stream + (dot(mixed[0], merge_both[0]) + dot(mixed[1], merge_both[1]) + merge_bias)
    second_norm, second_scale = standardize(residual)
    second_out = low(second_norm * second_gain + second_shift)
    active, slope = [], []
    for p in parts:
        pre_gelu = dot(second_out, expand_both[p]) + expand_biases[p]
        below = 0.5 * (1.0 + lax.erf(pre_gelu * ROOT_HALF))
        active.append(low(pre_gelu * below))
        slope.append(low(below + pre_gelu * jnp.exp(-0.5 * pre_gelu * pre_gelu) * GAUSS_NORM))
    branch_two = dot(active[0], reduce_both[0]) + dot(active[1], reduce_both[1])
    layer_out = low(residual + (branch_two + reduce_bias))

    grad_pre = [low(dot_nt(grad_two, reduce_both[p]) * wide(slope[p])) for p in parts]
    reduce_grads = [low(dot_tn(active[p], grad_two)) for p in parts]
    expand_grads = [low(dot_tn(second_out, grad_pre[p])) for p in parts]
    grad_second = dot_nt(grad_pre[0], expand_both[0]) + dot_nt(grad_pre[1], expand_both[1])
    grad_residual = wide(grad_two) + norm_back(grad_second * second_gain, second_norm, second_scale)
    grad_one = low(grad_residual)
    merge_grads = [low(dot_tn(mixed[p], grad_one)) for p in parts]
    grad_mixed = [low(dot_nt(grad_one, merge_both[p])) for p in parts]
    heads_grads, grad_first, heads_bias_grads = [], 0.0, []
    for p in parts:
        _, root, early, late = seen[p]
        g_q, g_k, g_v, sums = attn_bwd(
            heads[p][0], heads[p][1], heads[p][2], grad_mixed[p], mixed[p], root, early, late, *tables, 512
        )
        heads_bias_grads.append(sums[:, 0].reshape(-1))
        heads_grads.append(
            jnp.concatenate([low(dot_tn(first_out, g)) for g in (g_q, g_k, g_v)], 0)
        )
        for number, g in enumerate((g_q, g_k, g_v)):
            grad_first = grad_first + dot_nt(g, heads_both[p][number])
    tokens_grad = grad_residual + norm_back(grad_first * first_gain, first_norm, first_scale)

    def reduced(grads):
        own, far = (scatter(g, [0]) for g in grads)
        piece = low(wide(own) + wide(cross(far)))
        rest = list(range(1, levels))
        return wide(gather(scatter(piece, rest), [0] + rest))

    reduce_total = reduced(reduce_grads)
    expand_total = reduced(expand_grads)
    merge_total = reduced(merge_grads)
    heads_total = reduced(heads_grads)

    far_sums = jnp.concatenate([heads_bias_grads[1], column_sums(grad_pre[1])])
    own_sums = jnp.concatenate([heads_bias_grads[0], column_sums(grad_pre[0])])
    both_sums = jnp.concatenate(
        [
            column_sums(grad_one),
            column_sums(grad_two),
            jnp.sum(grad_first * first_norm, 0),
            jnp.sum(grad_first, 0),
            jnp.sum(grad_second * second_norm, 0),
            jnp.sum(grad_second, 0),
        ]
    )
    arrived = cross(jnp.concatenate([far_sums, both_sums]))
    sums = jnp.concatenate([own_sums, both_sums]) + arrived
    for level in range(levels):
        sums = sums + swap(sums, level)
    bounds = [heads_bias.size, expand_bias.size] + [merge_bias.size] * 6
    cuts = [sum(bounds[:i]) for i in range(1, len(bounds))]
    (heads_bias_total, expand_bias_total, merge_bias_total, reduce_bias_total, first_gain_total,
     first_shift_total, second_gain_total, second_shift_total) = jnp.split(sums, cuts)
    return (
        give_back(layer_out),
        wide(give_back(low(tokens_grad))),
        first_gain_total,
        first_shift_total,
        heads_total.reshape(heads_own.shape).transpose(1, 0, 2),
        heads_bias_total.reshape(heads_bias.shape),
        merge_total,
        merge_bias_total,
        second_gain_total,
        second_shift_total,
        expand_total,
        expand_bias_total,
        reduce_total,
        reduce_bias_total,
    )


def solution(mesh):
    return jax.shard_map(
        functools.partial(on_device, mesh.shape["dp"]),
        mesh=mesh,
        in_specs=(
            P(None, "dp", "mp", None),
            P(None, "dp", "mp", None),
            P(None, "dp"),
            P(),
            P(),
            P(None, None, "mp"),
            P(None, "mp"),
            P("mp", None),
            P(),
            P(),
            P(),
            P(None, "mp"),
            P("mp"),
            P("mp", None),
            P(),
        ),
        out_specs=(
            P(None, "dp", "mp", None),
            P(None, "dp", "mp", None),
            P(),
            P(),
            P(None, None, "mp"),
            P(None, "mp"),
            P("mp", None),
            P(),
            P(),
            P(),
            P(None, "mp"),
            P("mp"),
            P("mp", None),
            P(),
        ),
        check_vma=False,
    )
```

```python
import functools
import math

import jax
import jax.numpy as jnp
from jax import lax
from jax.experimental import pallas as pl
from jax.experimental.pallas import tpu as pltpu
from jax.sharding import PartitionSpec as P

HEAD_DIM = 64
FRAMES = 2
SIDE_SMALL = 16
SIDE_LARGE = 24
EPSILON = 1e-06
ROOT_HALF = 0.7071067811865476
GAUSS_NORM = 0.3989422804014327
LOG2E = math.log2(math.e)
PAIR = 128
NEG = -1e30
STRIPS = ((0, 512, 592), (512, 640, 1168), (640, 1024, 1168), (1024, 1280, 1280))
EARLY = 512


def params(mib=50):
    return pltpu.CompilerParams(vmem_limit_bytes=mib * 2**20)


def takes(microseconds):
    return pl.CostEstimate(
        flops=int(microseconds * 1.1e9), bytes_accessed=int(microseconds * 1e6), transcendentals=0
    )


def low(array):
    return array.astype(jnp.bfloat16)


def wide(array):
    return array.astype(jnp.float32)


def dot(left, right):
    return jnp.dot(left, right, preferred_element_type=jnp.float32)


def dot_nt(left, right):
    return lax.dot_general(
        left, right, (((1,), (1,)), ((), ())), preferred_element_type=jnp.float32
    )


def dot_tn(left, right):
    return lax.dot_general(
        left, right, (((0,), (0,)), ((), ())), preferred_element_type=jnp.float32
    )


def slot_layout(count_one, length):
    large_count = SIDE_LARGE * SIDE_LARGE
    grid_side = jnp.where(count_one == large_count, SIDE_LARGE, SIDE_SMALL).astype(jnp.int32)
    frame_len = grid_side * grid_side + 2
    clip_len = FRAMES * frame_len
    clip_total = jnp.where(count_one == large_count, 1, 2).astype(jnp.int32)
    slot_id = jnp.arange(length, dtype=jnp.int32)
    clip_id = jnp.minimum(slot_id // clip_len, clip_total)
    offset_in = slot_id - clip_id * clip_len
    frame_id = offset_in // frame_len
    place_in = offset_in - frame_id * frame_len - 2
    patch_id = jnp.maximum(place_in, 0)
    is_live = clip_id < clip_total
    is_patch = is_live & (place_in >= 0)
    frame_id = jnp.where(is_live, frame_id, 0)
    patch_row = jnp.where(is_patch, patch_id // grid_side, 0)
    column = jnp.where(is_patch, patch_id - patch_id // grid_side * grid_side, 0)
    first_key = clip_id * clip_len
    past_key = jnp.where(is_live, first_key + (frame_id + 1) * frame_len, length)
    return (first_key, past_key, frame_id, patch_row, column)


def rotary_tables(frame_id, patch_row, column):
    segment = 2 * (HEAD_DIM // 3 // 2)
    half_width = segment // 2
    dim_index = jnp.arange(PAIR, dtype=jnp.int32) % HEAD_DIM
    segment_id = dim_index // segment
    exponent = (dim_index % segment % half_width).astype(jnp.float32)
    frequency = jnp.exp(exponent * (-math.log(10000.0) / half_width))
    pick = lambda number: wide(jnp.where(segment_id == number, 1.0, 0.0))[None, :]
    position = (
        pick(0) * wide(frame_id[:, None])
        + pick(1) * wide(patch_row[:, None])
        + pick(2) * wide(column[:, None])
    )
    angles = position * frequency[None, :]
    lower = (dim_index % segment < half_width)[None, :]
    sine = jnp.where((segment_id < 3)[None, :], jnp.sin(angles), 0.0)
    return (jnp.cos(angles), jnp.where(lower, -sine, 0.0), jnp.where(lower, 0.0, sine))


def spin(x, cos, up, down):
    turn = HEAD_DIM // 3 // 2
    return x * cos + pltpu.roll(x, PAIR - turn, 1) * up + pltpu.roll(x, turn, 1) * down


def standardize(values_in):
    row_mean = jnp.mean(values_in, -1, keepdims=True)
    centred = values_in - row_mean
    norm_scale = lax.rsqrt(jnp.mean(centred * centred, -1, keepdims=True) + EPSILON)
    return (centred * norm_scale, norm_scale)


def fold(x):
    return jnp.sum(x.reshape(x.shape[0] // 8, 8, x.shape[1]), 0)


def whole(array):
    return pl.BlockSpec(array.shape, lambda *_: (0,) * array.ndim, pipeline_mode=pl.Buffered(1))


def enter_kernel(side_ref, mine_ref, arrived_ref, gain_ref, shift_ref, stream_ref, out_ref):
    def step(rows):
        stream_ref[...] = rows
        normed, _ = standardize(wide(rows))
        out_ref[...] = low(normed * gain_ref[...] + shift_ref[...])

    @pl.when(pl.program_id(0) == 0)
    def _():
        step(mine_ref[0])

    @pl.when(pl.program_id(0) == 1)
    def _():
        step(arrived_ref[...])


def enter(side, tokens, arrived, gain, shift):
    _, half, depth = tokens.shape
    vector = pl.BlockSpec((1, depth), lambda i, side: (0, 0))
    out = pl.BlockSpec((half, depth), lambda i, side: (jnp.where(i == 0, side[0], 1 - side[0]), 0))
    return pl.pallas_call(
        enter_kernel,
        grid_spec=pltpu.PrefetchScalarGridSpec(
            num_scalar_prefetch=1,
            grid=(2,),
            in_specs=[
                pl.BlockSpec((1, half, depth), lambda i, side: (side[0], 0, 0)),
                pl.BlockSpec((half, depth), lambda i, side: (0, 0)),
                vector,
                vector,
            ],
            out_specs=[out, out],
        ),
        out_shape=[jax.ShapeDtypeStruct((2 * half, depth), jnp.bfloat16)] * 2,
        compiler_params=params(),
        cost_estimate=takes(5),
        name="enter",
    )(side, tokens, arrived, gain[None], shift[None])


def project_kernel(chunk, x_ref, w_ref, b_ref, cos_ref, up_ref, down_ref, out_ref):
    part = pl.program_id(0)
    for at in range(0, x_ref.shape[0], chunk):
        rows = slice(at, at + chunk)
        y = dot(x_ref[rows, :], w_ref[...]) + b_ref[...]

        @pl.when(part == 2)
        def _():
            out_ref[rows, :] = low(y)

        @pl.when(part < 2)
        def _():
            cos, up, down = cos_ref[rows, :], up_ref[rows, :], down_ref[rows, :]
            for lane in range(0, y.shape[1], PAIR):
                lanes = slice(lane, lane + PAIR)
                out_ref[rows, lanes] = low(spin(y[:, lanes], cos, up, down))


def project(x, weight, bias, tables):
    rows, depth = x.shape
    width = weight.shape[1] // 3
    return pl.pallas_call(
        functools.partial(project_kernel, rows),
        grid=(3,),
        in_specs=[
            whole(x),
            pl.BlockSpec((depth, width), lambda i: (0, i)),
            pl.BlockSpec((1, width), lambda i: (0, i)),
        ]
        + [whole(table) for table in tables],
        out_specs=pl.BlockSpec((rows, width), lambda i: (0, i)),
        out_shape=jax.ShapeDtypeStruct((rows, 3 * width), jnp.bfloat16),
        compiler_params=params(),
        cost_estimate=takes(7),
        name="project",
    )(x, weight, bias[None], *tables)


def attend_kernel(q_ref, k_ref, v_ref, lo_ref, hi_ref, out_ref, root_ref, early_ref, late_ref):
    lane = lax.broadcasted_iota(jnp.int32, (1, PAIR), 1)
    factor = HEAD_DIM**-0.5 * LOG2E
    values = v_ref[...].T
    for first, past, stop in STRIPS:
        count = past - first
        q = q_ref[first:past, :]
        key = lax.broadcasted_iota(jnp.int32, (stop, count), 0)
        allowed = (key >= lo_ref[:, first:past]) & (key < hi_ref[:, first:past])
        outs, roots = [], []
        for head in range(2):
            own = (lane >= HEAD_DIM) == (head == 1)
            scores = dot_nt(k_ref[0:stop, :], jnp.where(own, q, jnp.zeros_like(q)))
            scores = jnp.where(allowed, scores, NEG)
            powers = jnp.exp2((scores - jnp.max(scores, 0, keepdims=True)) * factor)
            root = 1.0 / jnp.sum(powers, 0, keepdims=True)
            powers = low(powers)
            if past <= EARLY:
                early_ref[head, :, first:past] = powers
            else:
                late_ref[head, 0:stop, first - EARLY : past - EARLY] = powers
            rows = slice(head * HEAD_DIM, (head + 1) * HEAD_DIM)
            outs.append(dot(values[rows, 0:stop], powers) * root)
            roots.append(jnp.broadcast_to(root, (HEAD_DIM, count)))
        out_ref[first:past, :] = low(jnp.concatenate(outs, 0).T)
        root_ref[first:past, :] = jnp.concatenate(roots, 0).T


def kept_specs(rows):
    return [
        pl.BlockSpec((2, STRIPS[0][2], EARLY), lambda i: (i, 0, 0)),
        pl.BlockSpec((2, rows, rows - EARLY), lambda i: (i, 0, 0)),
    ]


def attend(heads, first_key, past_key):
    rows, width = heads.shape[0], heads.shape[1] // 3
    pairs = width // PAIR
    block = pl.BlockSpec((rows, PAIR), lambda i: (0, i))
    part = lambda number: pl.BlockSpec((rows, PAIR), lambda i: (0, number * pairs + i))
    return pl.pallas_call(
        attend_kernel,
        grid=(pairs,),
        in_specs=[part(0), part(1), part(2), whole(first_key), whole(past_key)],
        out_specs=[block, block] + kept_specs(rows),
        out_shape=[
            jax.ShapeDtypeStruct((rows, width), jnp.bfloat16),
            jax.ShapeDtypeStruct((rows, width), jnp.float32),
            jax.ShapeDtypeStruct((2 * pairs, STRIPS[0][2], EARLY), jnp.bfloat16),
            jax.ShapeDtypeStruct((2 * pairs, rows, rows - EARLY), jnp.bfloat16),
        ],
        compiler_params=params(),
        cost_estimate=takes(17),
        name="attend",
    )(heads, heads, heads, first_key, past_key)


def attend_back_kernel(
    q_ref, k_ref, v_ref, g_ref, o_ref, root_ref, early_ref, late_ref, cos_ref, up_ref, down_ref,
    out_ref, sums_ref, keys_acc, values_acc, queries_acc,
):
    pair = pl.program_id(0)
    pairs = out_ref.shape[1] // (3 * PAIR)
    lane = lax.broadcasted_iota(jnp.int32, (1, PAIR), 1)
    scale = HEAD_DIM**-0.5
    keys = k_ref[...].T
    for first, past, stop in STRIPS[::-1]:
        q = q_ref[first:past, :]
        g = wide(g_ref[first:past, :]) * root_ref[first:past, :]
        inner = (g * wide(o_ref[first:past, :])).T
        g = low(g)
        for head in range(2):
            own = (lane >= HEAD_DIM) == (head == 1)
            rows = slice(head * HEAD_DIM, (head + 1) * HEAD_DIM)
            g_own = jnp.where(own, g, jnp.zeros_like(g))
            shift = jnp.sum(inner[rows, :], 0, keepdims=True)
            if past <= EARLY:
                powers = early_ref[head, :, first:past]
            else:
                powers = late_ref[head, 0:stop, first - EARLY : past - EARLY]
            g_scores = low(wide(powers) * (dot_nt(v_ref[0:stop, :], g_own) - shift))
            queries_acc[rows, first:past] = dot(keys[rows, 0:stop], g_scores)
            g_keys = dot(g_scores, jnp.where(own, q, jnp.zeros_like(q)))
            g_values = dot(powers, g_own)
            if head == 0:
                total_keys, total_values = g_keys, g_values
            else:
                total_keys, total_values = total_keys + g_keys, total_values + g_values
        if past == STRIPS[-1][1]:
            keys_acc[...] = total_keys
            values_acc[...] = total_values
        else:
            keys_acc[0:stop, :] += total_keys
            values_acc[0:stop, :] += total_values
    cos, up, down = cos_ref[...], -up_ref[...], -down_ref[...]
    grads = (
        low(spin(queries_acc[...].T * scale, cos, up, down)),
        low(spin(keys_acc[...] * scale, cos, up, down)),
        low(values_acc[...]),
    )
    for number, grad in enumerate(grads):
        lanes = pl.ds(pl.multiple_of((number * pairs + pair) * PAIR, PAIR), PAIR)
        out_ref[:, lanes] = grad
        sums_ref[:, lanes] = fold(wide(grad))


def attend_back(heads, g, out, root, early, late, tables):
    rows, width = g.shape
    pairs = width // PAIR
    block = pl.BlockSpec((rows, PAIR), lambda i: (0, i))
    part = lambda number: pl.BlockSpec((rows, PAIR), lambda i: (0, number * pairs + i))
    return pl.pallas_call(
        attend_back_kernel,
        grid=(pairs,),
        in_specs=[part(0), part(1), part(2), block, block, block]
        + kept_specs(rows)
        + [whole(table) for table in tables],
        out_specs=[
            pl.BlockSpec((rows, 3 * width), lambda i: (0, 0)),
            pl.BlockSpec((8, 3 * width), lambda i: (0, 0)),
        ],
        out_shape=[
            jax.ShapeDtypeStruct((rows, 3 * width), jnp.bfloat16),
            jax.ShapeDtypeStruct((8, 3 * width), jnp.float32),
        ],
        scratch_shapes=[
            pltpu.VMEM((rows, PAIR), jnp.float32),
            pltpu.VMEM((rows, PAIR), jnp.float32),
            pltpu.VMEM((PAIR, rows), jnp.float32),
        ],
        compiler_params=params(56),
        cost_estimate=takes(20),
        name="attend_back",
    )(heads, heads, heads, g, out, root, early, late, *tables)


def merge_kernel(count, *refs):
    rights, lefts = refs[:count], refs[count : 2 * count]
    x_ref, bias_ref, gain_ref, shift_ref, residual_ref, out_ref = refs[2 * count :]
    total = wide(x_ref[...]) + bias_ref[...]
    for left, right in zip(lefts, rights):
        total = total + dot(left[...], right[...])
    residual_ref[...] = total
    normed, _ = standardize(total)
    out_ref[...] = low(normed * gain_ref[...] + shift_ref[...])


def merge(lefts, rights, x, bias, gain, shift, block=256):
    rows, depth = x.shape
    row = lambda array: pl.BlockSpec((block, array.shape[1]), lambda i: (i, 0))
    vectors = (bias[None], gain[None], shift[None])
    return pl.pallas_call(
        functools.partial(merge_kernel, len(lefts)),
        grid=(rows // block,),
        in_specs=[whole(w) for w in rights]
        + [row(a) for a in lefts]
        + [row(x)]
        + [whole(v) for v in vectors],
        out_specs=[row(x), row(x)],
        out_shape=[
            jax.ShapeDtypeStruct((rows, depth), jnp.float32),
            jax.ShapeDtypeStruct((rows, depth), jnp.bfloat16),
        ],
        compiler_params=params(),
        cost_estimate=takes(8),
        name="merge",
    )(*rights, *lefts, x, *vectors)


def expand_kernel(chunk, x_ref, w_ref, b_ref, active_ref, slope_ref):
    for at in range(0, x_ref.shape[0], chunk):
        rows = slice(at, at + chunk)
        v = dot(x_ref[rows, :], w_ref[...]) + b_ref[...]
        below = 0.5 + 0.5 * lax.erf(v * ROOT_HALF)
        active_ref[rows, :] = low(v * below)
        slope_ref[rows, :] = low(below + v * jnp.exp(-0.5 * v * v) * GAUSS_NORM)


def expand(x, weight, bias, block=512, chunk=256):
    rows, depth = x.shape
    width = weight.shape[1]
    out = pl.BlockSpec((rows, block), lambda i: (0, i))
    return pl.pallas_call(
        functools.partial(expand_kernel, chunk),
        grid=(width // block,),
        in_specs=[
            whole(x),
            pl.BlockSpec((depth, block), lambda i: (0, i)),
            pl.BlockSpec((1, block), lambda i: (0, i)),
        ],
        out_specs=[out, out],
        out_shape=[jax.ShapeDtypeStruct((rows, width), jnp.bfloat16)] * 2,
        compiler_params=params(),
        cost_estimate=takes(8.5),
        name="expand",
    )(x, weight, bias[None])


def reduce_kernel(count, half, side_ref, *refs):
    rights, lefts = refs[:count], refs[count : 2 * count]
    x_ref, bias_ref, send_ref, keep_ref = refs[2 * count :]
    total = x_ref[...] + bias_ref[...]
    for left, right in zip(lefts, rights):
        total = total + dot(left[...], right[...])

    @pl.when(pl.program_id(0) < half)
    def _():
        send_ref[...] = low(total)

    @pl.when(pl.program_id(0) >= half)
    def _():
        keep_ref[...] = low(total)


def reduce_rows(side, lefts, rights, x, bias, block=320):
    rows, depth = x.shape
    half = rows // 2 // block
    at = lambda i, side: jnp.where(i < half, (1 - side[0]) * half + i, side[0] * half + i - half)
    row = lambda array: pl.BlockSpec((block, array.shape[1]), lambda i, side: (at(i, side), 0))
    return pl.pallas_call(
        functools.partial(reduce_kernel, len(lefts), half),
        grid_spec=pltpu.PrefetchScalarGridSpec(
            num_scalar_prefetch=1,
            grid=(2 * half,),
            in_specs=[whole(w) for w in rights]
            + [row(a) for a in lefts]
            + [row(x), whole(bias[None])],
            out_specs=[
                pl.BlockSpec((block, depth), lambda i, side: (jnp.minimum(i, half - 1), 0)),
                pl.BlockSpec((block, depth), lambda i, side: (jnp.maximum(i - half, 0), 0)),
            ],
        ),
        out_shape=[jax.ShapeDtypeStruct((rows // 2, depth), jnp.bfloat16)] * 2,
        compiler_params=params(),
        cost_estimate=takes(18),
        name="reduce_rows",
    )(side, *rights, *lefts, x, bias[None])


def back_kernel(count, at_ref, *refs):
    rights, lefts = refs[:count], refs[count : 2 * count]
    base_ref, above_ref, gain_ref, out_ref, sums_ref = refs[2 * count :]

    @pl.when(pl.program_id(0) == 0)
    def _():
        sums_ref[...] = jnp.zeros_like(sums_ref)

    g = dot_nt(lefts[0][...], rights[0][...])
    for left, right in zip(lefts[1:], rights[1:]):
        g = g + dot_nt(left[...], right[...])
    normed, scale = standardize(wide(base_ref[...]))
    u = g * gain_ref[...]
    above = wide(above_ref[...])
    inner = jnp.mean(u, -1, keepdims=True) + normed * jnp.mean(u * normed, -1, keepdims=True)
    out = low(above + scale * (u - inner))
    out_ref[...] = out
    sums_ref[0] += fold(g * normed)
    sums_ref[1] += fold(g)
    sums_ref[2] += fold(wide(out))
    sums_ref[3] += fold(above)


def back_norm(at, rows, lefts, rights, base, above, gain, block=320):
    depth = base.shape[1]
    row = lambda array: pl.BlockSpec((block, array.shape[1]), lambda i, at: (at[0] + i, 0))
    return pl.pallas_call(
        functools.partial(back_kernel, len(lefts)),
        grid_spec=pltpu.PrefetchScalarGridSpec(
            num_scalar_prefetch=1,
            grid=(rows // block,),
            in_specs=[whole(w) for w in rights]
            + [row(a) for a in lefts]
            + [row(base), row(above), whole(gain[None])],
            out_specs=[
                pl.BlockSpec((block, depth), lambda i, at: (i, 0)),
                pl.BlockSpec((4, 8, depth), lambda i, at: (0, 0, 0)),
            ],
        ),
        out_shape=[
            jax.ShapeDtypeStruct((rows, depth), jnp.bfloat16),
            jax.ShapeDtypeStruct((4, 8, depth), jnp.float32),
        ],
        compiler_params=params(),
        cost_estimate=takes(20 * rows / 1280),
        name="back_norm",
    )(at, *rights, *lefts, base, above, gain[None])


def place_kernel(steps, flag_ref, mine_ref, theirs_ref, out_ref):
    @pl.when(pl.program_id(0) < steps)
    def _():
        out_ref[...] = mine_ref[...].astype(out_ref.dtype).reshape(out_ref.shape)

    @pl.when(pl.program_id(0) >= steps)
    def _():
        out_ref[...] = theirs_ref[...].astype(out_ref.dtype).reshape(out_ref.shape)


def place(flag, mine, theirs, steps, in_block, in_index, out_shape, out_block, out_index, dtype):
    def target(i, flag):
        return out_index(jnp.where(i < steps, flag[0], 1 - flag[0]), jnp.where(i < steps, i, i - steps))

    return pl.pallas_call(
        functools.partial(place_kernel, steps),
        grid_spec=pltpu.PrefetchScalarGridSpec(
            num_scalar_prefetch=1,
            grid=(2 * steps,),
            in_specs=[
                pl.BlockSpec(in_block, lambda i, flag: in_index(jnp.minimum(i, steps - 1))),
                pl.BlockSpec(in_block, lambda i, flag: in_index(jnp.maximum(i - steps, 0))),
            ],
            out_specs=pl.BlockSpec(out_block, target),
        ),
        out_shape=jax.ShapeDtypeStruct(out_shape, dtype),
        compiler_params=params(),
        cost_estimate=takes(4),
        name="place",
    )(flag, mine, theirs)


def place_rows(flag, mine, theirs, steps, dtype):
    rows, width = mine.shape
    block = (rows // steps, width)
    return place(
        flag, mine, theirs, steps, block, lambda j: (j, 0),
        (2 * rows, width), block, lambda half, j: (half * steps + j, 0), dtype,
    )


def place_columns(flag, mine, theirs, steps, dtype):
    rows, width = mine.shape
    block = (rows // steps, width)
    return place(
        flag, mine, theirs, steps, block, lambda j: (j, 0),
        (rows, 2 * width), block, lambda half, j: (j, half), dtype,
    )


def place_heads(flag, mine, theirs, dtype):
    rows, width = mine.shape[0], mine.shape[1] // 3
    return place(
        flag, mine, theirs, 3, (rows, width), lambda j: (0, j),
        (3, rows, 2 * width), (1, rows, width), lambda half, j: (j, 0, half), dtype,
    )


def column_sums(matrix):
    unit_column = jnp.ones((matrix.shape[0],), matrix.dtype)
    return jnp.dot(unit_column, matrix, preferred_element_type=jnp.float32)


KEEP, SEND = 0, 1
OWN, FAR = 0, 1
QUARTERS = ((FAR, SEND), (FAR, KEEP), (OWN, SEND), (OWN, KEEP))


def on_device(
    spread,
    tokens,
    cotangent,
    patch_count,
    first_gain,
    first_shift,
    heads_weight,
    heads_bias,
    merge_weight,
    merge_bias,
    second_gain,
    second_shift,
    expand_weight,
    expand_bias,
    reduce_weight,
    reduce_bias,
):
    levels = spread.bit_length() - 1
    rest = list(range(1, levels))
    chunks = spread // 2
    location = lax.axis_index("dp")
    side = lax.axis_index("mp")
    sides = side[None].astype(jnp.int32)
    previous = []

    def bit(level):
        return (location >> level) & 1

    core = bit(0)[None].astype(jnp.int32)

    def tie(array, *others):
        return lax.optimization_barrier((array,) + others)[0] if others else array

    def after(array):
        return tie(array, *previous)

    def did(*arrays):
        previous[:] = arrays
        return arrays[0] if len(arrays) == 1 else arrays

    def swap(array, level):
        return lax.ppermute(array, "dp", [(i, i ^ (1 << level)) for i in range(spread)])

    def cross(array):
        return lax.ppermute(array, "mp", [(0, 1), (1, 0)])

    def half_of(array, flag, axis=0):
        size = array.shape[axis] // 2
        return lax.dynamic_slice_in_dim(array, flag * size, size, axis)

    def chunk_of(array):
        size = array.shape[0] // chunks
        return lax.dynamic_slice_in_dim(array, (location >> 1) * size, size, 0)

    def split(array, level):
        left = spread >> (level + 1)
        four = array.reshape(left, 2, -1, array.shape[1])
        part = lambda flag: lax.dynamic_index_in_dim(four, flag, 1, False).reshape(-1, array.shape[1])
        return part(bit(level)), part(1 - bit(level))

    def join(mine, theirs, level):
        left = spread >> (level + 1)
        four = lambda array: array.reshape(left, 1, -1, array.shape[1])
        pair = jnp.where(
            bit(level) == 0,
            jnp.concatenate([four(mine), four(theirs)], 1),
            jnp.concatenate([four(theirs), four(mine)], 1),
        )
        return pair.reshape(-1, mine.shape[1])

    def quarters_of(own, axis):
        return [half_of(own, bit(0), axis), half_of(own, 1 - bit(0), axis)]

    tokens, cotangent = tokens[:, 0], cotangent[:, 0]
    tokens_far = cross(lax.dynamic_index_in_dim(tokens, 1 - side, 0, False))
    heads_three = heads_weight.transpose(1, 0, 2)
    heads_own = [
        jnp.concatenate([half_of(heads_three[n], flag, 1) for n in range(3)], 1)
        for flag in (bit(0), 1 - bit(0))
    ]
    merge_own = quarters_of(merge_weight, 0)
    expand_own = quarters_of(expand_weight, 1)
    reduce_own = quarters_of(reduce_weight, 0)
    pack = lambda hb, eb: jnp.concatenate([hb.reshape(-1), eb])
    bias_own = [
        pack(half_of(heads_bias, flag, 1), half_of(expand_bias, flag)) for flag in (bit(0), 1 - bit(0))
    ]
    three = heads_bias.size // 2
    near = rest[:2]
    heads_piece = heads_own[KEEP]
    for level in near:
        heads_piece = split(heads_piece, level)[0]
    up_piece = jnp.concatenate([chunk_of(expand_own[KEEP]), chunk_of(merge_own[KEEP])])
    down_piece = chunk_of(reduce_own[KEEP])

    count_one = lax.dynamic_index_in_dim(patch_count[:, 0], side, 0, False)
    length = 2 * tokens.shape[1]
    first_key, past_key, frame_id, patch_row, column = slot_layout(count_one, length)
    tables = rotary_tables(frame_id, patch_row, column)
    first_key, past_key = first_key[None], past_key[None]

    heads_piece = cross(tie(heads_piece, tokens_far))
    up_piece = cross(tie(up_piece, tokens_far))
    bias_both = cross(tie(jnp.concatenate(bias_own), tokens_far))
    bias_far = [bias_both[: bias_both.size // 2], bias_both[bias_both.size // 2 :]]
    stream, first_out = did(*enter(sides, tokens, tokens_far, first_gain, first_shift))
    heads, seen = {}, {}
    heads_all = [heads_own, None]
    bias_all = (bias_own, bias_far)

    def look(p, c):
        heads[p, c] = did(project(after(first_out), heads_all[p][c], bias_all[p][c][:three], tables))

    def attention(p, c):
        seen[p, c] = did(*attend(after(heads[p, c]), first_key, past_key))

    def gathered(array, *splits):
        array = lax.all_gather(array, "dp", axis=0, tiled=True)
        array = array.reshape(chunks, 2, -1, array.shape[1])
        quarters, at = [], 0
        for size in splits:
            part = array[:, :, at : at + size]
            quarters.append(
                [
                    lax.dynamic_index_in_dim(part, flag, 1, False).reshape(-1, array.shape[3])
                    for flag in (bit(0), 1 - bit(0))
                ]
            )
            at += size
        return quarters

    look(OWN, KEEP)
    heads_piece = did(after(heads_piece))
    if len(near) > 1:
        heads_next = swap(heads_piece, near[1])
    look(OWN, SEND)
    up_sizes = (expand_own[0].shape[0] // chunks, merge_own[0].shape[0] // chunks)
    up_gathered = gathered(after(up_piece), *up_sizes)
    down_piece = cross(after(down_piece))
    if len(near) > 1:
        heads_piece = did(join(after(heads_piece), heads_next, near[1]))
    heads_next = swap(heads_piece, near[0])
    attention(OWN, KEEP)
    attention(OWN, SEND)
    heads_piece = did(join(after(heads_piece), heads_next, near[0]))
    heads_all[FAR] = [heads_piece, swap(heads_piece, 0)]
    cotangent_far = cross(after(lax.dynamic_index_in_dim(cotangent, 1 - side, 0, False)))
    (reduce_far,) = gathered(after(down_piece), down_piece.shape[0])
    look(FAR, KEEP)
    attention(FAR, KEEP)
    look(FAR, SEND)
    attention(FAR, SEND)
    expand_far, merge_far = ([after(q) for q in quarters] for quarters in up_gathered)
    merge_all = (merge_own, merge_far)
    expand_all = (expand_own, expand_far)
    reduce_all = (reduce_own, reduce_far)
    mixed = {q: seen[q][0] for q in QUARTERS}
    residual, second_out = did(
        *merge(
            [mixed[q] for q in QUARTERS], [merge_all[p][c] for p, c in QUARTERS],
            after(stream), merge_bias, second_gain, second_shift,
        )
    )
    cotangent_far = after(cotangent_far)
    grad_two = jnp.where(
        side == 0,
        jnp.concatenate([cotangent[0], cotangent_far]),
        jnp.concatenate([cotangent_far, cotangent[1]]),
    )

    active, slope, grad_pre = {}, {}, {}

    def widen(p, c):
        active[p, c], slope[p, c] = did(
            *expand(after(second_out), expand_all[p][c], bias_all[p][c][three:])
        )

    def back_active(p, c):
        grad_pre[p, c] = did(low(dot_nt(after(grad_two), reduce_all[p][c]) * wide(slope[p, c])))

    def product(left, right, *arrived):
        total = dot_tn(after(left), right)
        for array in arrived:
            total = total + wide(array)
        return did(low(total))

    def scattered(array, level):
        keep, send = split(after(array), level)
        did(send)
        return keep, swap(send, level)

    def summed(keep, arrived):
        return did(low(wide(after(keep)) + wide(arrived)))

    widen(FAR, SEND)
    widen(FAR, KEEP)
    sent = swap(product(active[FAR, SEND], grad_two), 0)
    widen(OWN, SEND)
    reduce_far_sum = product(active[FAR, KEEP], grad_two, sent)
    reduce_cross = cross(reduce_far_sum)
    widen(OWN, KEEP)
    sent = swap(product(active[OWN, SEND], grad_two), 0)
    back_active(FAR, SEND)
    reduce_sum = product(active[OWN, KEEP], grad_two, sent)
    back_active(FAR, KEEP)
    sent = swap(product(second_out, grad_pre[FAR, SEND]), 0)
    back_active(OWN, SEND)
    expand_far_sum = product(second_out, grad_pre[FAR, KEEP], sent)
    back_active(OWN, KEEP)
    sent = swap(product(second_out, grad_pre[OWN, SEND]), 0)
    reduce_sum = summed(reduce_sum, reduce_cross)
    expand_cross = cross(tie(expand_far_sum, reduce_cross))
    reduce_keep, reduce_next = scattered(reduce_sum, rest[0])
    layer_send, layer_keep = did(
        *reduce_rows(
            sides, [active[q] for q in QUARTERS], [reduce_all[p][c] for p, c in QUARTERS],
            after(residual), reduce_bias,
        )
    )
    expand_sum = product(second_out, grad_pre[OWN, KEEP], sent)
    zero = jnp.zeros((1,), jnp.int32)
    reduce_sum = summed(reduce_keep, reduce_next)
    reduce_keep, reduce_next = scattered(reduce_sum, rest[1])
    grad_one, second_sums = did(
        *back_norm(
            zero, length, [grad_pre[q] for q in QUARTERS], [expand_all[p][c] for p, c in QUARTERS],
            after(residual), grad_two, second_gain,
        )
    )
    reduce_sum = summed(reduce_keep, reduce_next)
    for level in rest[2:]:
        reduce_keep, reduce_next = scattered(reduce_sum, level)
        reduce_sum = low(wide(reduce_keep) + wide(reduce_next))

    grad_mixed, grad_heads, head_sums = {}, {}, {}

    def back_mixed(p, c):
        grad_mixed[p, c] = did(low(dot_nt(after(grad_one), merge_all[p][c])))

    def back_attention(q):
        out, root, early, late = seen[q]
        grad_heads[q], sums = did(
            *attend_back(heads[q], after(grad_mixed[q]), out, root, early, late, tables)
        )
        head_sums[q] = jnp.sum(sums, 0)

    sent_far = swap(product(mixed[FAR, SEND], grad_one), 0)
    sent_own = swap(product(mixed[OWN, SEND], grad_one), 0)
    for p, c in QUARTERS:
        back_mixed(p, c)
    merge_far_sum = product(mixed[FAR, KEEP], grad_one, sent_far)
    merge_sum = product(mixed[OWN, KEEP], grad_one, sent_own)
    expand_sum = summed(expand_sum, expand_cross)
    merge_cross = cross(tie(merge_far_sum, expand_cross))
    layer_far = cross(tie(layer_send, expand_cross))
    expand_keep, expand_next = scattered(expand_sum, rest[0])
    back_attention((FAR, SEND))
    reduce_total = lax.all_gather(after(reduce_sum), "dp", axis=0, tiled=True)
    expand_sum = summed(expand_keep, expand_next)
    expand_keep, expand_next = scattered(expand_sum, rest[1])
    sent = swap(product(first_out, grad_heads[FAR, SEND]), 0)
    merge_sum = summed(merge_sum, merge_cross)
    merge_keep, merge_next = scattered(merge_sum, rest[0])
    back_attention((FAR, KEEP))
    heads_far_sum = product(first_out, grad_heads[FAR, KEEP], sent)
    heads_cross = cross(heads_far_sum)
    expand_sum = summed(expand_keep, expand_next)
    merge_sum = summed(merge_keep, merge_next)
    merge_keep, merge_next = scattered(merge_sum, rest[1])
    for level in rest[2:]:
        expand_keep, expand_next = scattered(expand_sum, level)
        expand_sum = low(wide(expand_keep) + wide(expand_next))
    back_attention((OWN, SEND))
    merge_sum = summed(merge_keep, merge_next)
    for level in rest[2:]:
        merge_keep, merge_next = scattered(merge_sum, level)
        merge_sum = low(wide(merge_keep) + wide(merge_next))
    sent = swap(product(first_out, grad_heads[OWN, SEND]), 0)
    back_attention((OWN, KEEP))
    expand_total = lax.all_gather(
        after(jnp.concatenate([expand_sum, merge_sum])), "dp", axis=0, tiled=True
    )
    heads_sum = product(first_out, grad_heads[OWN, KEEP], sent, heads_cross)
    heads_keep, heads_next = scattered(heads_sum, rest[0])

    lefts = [grad_heads[q] for q in QUARTERS]
    rights = [heads_all[p][c] for p, c in QUARTERS]
    per_half = length // 2 // 320
    tokens_send, sums_a = did(
        *back_norm(
            (1 - sides) * per_half, length // 2, lefts, rights, stream, grad_one, after(first_gain)
        )
    )
    tokens_cross = cross(tokens_send)
    heads_sum = summed(heads_keep, heads_next)
    heads_keep, heads_next = scattered(heads_sum, rest[1])
    tokens_keep, sums_b = did(
        *back_norm(sides * per_half, length // 2, lefts, rights, stream, grad_one, after(first_gain))
    )
    first_sums = sums_a + sums_b
    heads_sum = summed(heads_keep, heads_next)
    for level in rest[2:]:
        heads_keep, heads_next = scattered(heads_sum, level)
        heads_sum = summed(heads_keep, heads_next)

    small = {q: jnp.concatenate([head_sums[q], column_sums(grad_pre[q])]) for q in QUARTERS}
    both = jnp.concatenate(
        [
            jnp.sum(part, 0)
            for part in (
                first_sums[0], first_sums[1], second_sums[0], second_sums[1], second_sums[2], second_sums[3],
            )
        ]
    )
    arrived = swap(jnp.concatenate([small[FAR, SEND], small[OWN, SEND], both]), 0)
    size = small[OWN, KEEP].size
    far = small[FAR, KEEP] + arrived[:size]
    mine = jnp.concatenate([small[OWN, KEEP], both]) + arrived[size:]
    mine = mine + cross(jnp.concatenate([far, mine[size:]]))
    for level in rest:
        mine = mine + swap(mine, level)
    both = mine[size:]
    mine = mine[:size]
    theirs = swap(mine, 0)
    first = jnp.where(bit(0) == 0, mine, theirs)
    second = jnp.where(bit(0) == 0, theirs, mine)
    heads_bias_total = jnp.concatenate([first[:three].reshape(3, -1), second[:three].reshape(3, -1)], 1)
    expand_bias_total = jnp.concatenate([first[three:], second[three:]])
    (first_gain_total, first_shift_total, second_gain_total, second_shift_total, merge_bias_total,
     reduce_bias_total) = both.reshape(6, -1)

    def rows_out(keep, arrived, dtype):
        return place_rows(sides, keep, arrived, 1, dtype).reshape(2, 1, length // 2, -1)

    def in_rows(array):
        return wide(array.transpose(1, 0, 2, 3).reshape(-1, array.shape[3]))

    reduce_total = reduce_total.reshape(chunks, 2, -1, reduce_total.shape[1])
    expand_total = expand_total.reshape(chunks, 2, -1, expand_total.shape[1])
    rows = expand_sum.shape[0]
    merge_total = expand_total[:, :, rows:]
    expand_total = expand_total[:, :, :rows]
    expand_total = jnp.concatenate(
        [expand_total[:, n].reshape(-1, expand_total.shape[3]) for n in range(2)], 1
    )
    layer_out = rows_out(after(layer_keep), layer_far, jnp.bfloat16)
    reduce_out = in_rows(reduce_total)
    for level in rest[::-1]:
        heads_sum = join(heads_sum, swap(heads_sum, level), level)
    heads_out = place_heads(core, heads_sum, swap(heads_sum, 0), jnp.float32)
    return (
        layer_out,
        rows_out(tokens_keep, tokens_cross, jnp.float32),
        first_gain_total,
        first_shift_total,
        heads_out.transpose(1, 0, 2),
        heads_bias_total,
        in_rows(merge_total),
        merge_bias_total,
        second_gain_total,
        second_shift_total,
        wide(expand_total),
        expand_bias_total,
        reduce_out,
        reduce_bias_total,
    )


def solution(mesh):
    rows = P(None, "dp", "mp", None)
    columns = P(None, "mp")
    heads = P(None, None, "mp")
    return jax.shard_map(
        functools.partial(on_device, mesh.shape["dp"]),
        mesh=mesh,
        in_specs=(
            rows, rows, P(None, "dp"), P(), P(), heads, columns, P("mp", None), P(), P(), P(), columns,
            P("mp"), P("mp", None), P(),
        ),
        out_specs=(
            rows, rows, P(), P(), heads, columns, P("mp", None), P(), P(), P(), columns, P("mp"),
            P("mp", None), P(),
        ),
        check_vma=False,
    )
```

```python
import functools
import math

import jax
import jax.numpy as jnp
from jax import lax
from jax.experimental import pallas as pl
from jax.experimental.pallas import tpu as pltpu
from jax.sharding import PartitionSpec as P

HEAD_DIM = 64
FRAMES = 2
SIDE_SMALL = 16
SIDE_LARGE = 24
EPSILON = 1e-06
ROOT_HALF = 0.7071067811865476
GAUSS_NORM = 0.3989422804014327
LOG2E = math.log2(math.e)
PAIR = 128
NEG = -1e30
STRIPS = ((0, 512, 592), (512, 640, 1168), (640, 1024, 1168), (1024, 1280, 1280))
EARLY = 512


def params(mib=50):
    return pltpu.CompilerParams(vmem_limit_bytes=mib * 2**20)


def takes(microseconds):
    return pl.CostEstimate(
        flops=int(microseconds * 4e9), bytes_accessed=int(microseconds * 4e6), transcendentals=0
    )


def low(array):
    return array.astype(jnp.bfloat16)


def wide(array):
    return array.astype(jnp.float32)


def dot(left, right):
    return jnp.dot(left, right, preferred_element_type=jnp.float32)


def dot_nt(left, right):
    return lax.dot_general(
        left, right, (((1,), (1,)), ((), ())), preferred_element_type=jnp.float32
    )


def dot_tn(left, right):
    return lax.dot_general(
        left, right, (((0,), (0,)), ((), ())), preferred_element_type=jnp.float32
    )


def slot_layout(count_one, length):
    large_count = SIDE_LARGE * SIDE_LARGE
    grid_side = jnp.where(count_one == large_count, SIDE_LARGE, SIDE_SMALL).astype(jnp.int32)
    frame_len = grid_side * grid_side + 2
    clip_len = FRAMES * frame_len
    clip_total = jnp.where(count_one == large_count, 1, 2).astype(jnp.int32)
    slot_id = jnp.arange(length, dtype=jnp.int32)
    clip_id = jnp.minimum(slot_id // clip_len, clip_total)
    offset_in = slot_id - clip_id * clip_len
    frame_id = offset_in // frame_len
    place_in = offset_in - frame_id * frame_len - 2
    patch_id = jnp.maximum(place_in, 0)
    is_live = clip_id < clip_total
    is_patch = is_live & (place_in >= 0)
    frame_id = jnp.where(is_live, frame_id, 0)
    patch_row = jnp.where(is_patch, patch_id // grid_side, 0)
    column = jnp.where(is_patch, patch_id - patch_id // grid_side * grid_side, 0)
    first_key = clip_id * clip_len
    past_key = jnp.where(is_live, first_key + (frame_id + 1) * frame_len, length)
    return (first_key, past_key, frame_id, patch_row, column)


def rotary_tables(frame_id, patch_row, column):
    segment = 2 * (HEAD_DIM // 3 // 2)
    half_width = segment // 2
    dim_index = jnp.arange(PAIR, dtype=jnp.int32) % HEAD_DIM
    segment_id = dim_index // segment
    exponent = (dim_index % segment % half_width).astype(jnp.float32)
    frequency = jnp.exp(exponent * (-math.log(10000.0) / half_width))
    pick = lambda number: wide(jnp.where(segment_id == number, 1.0, 0.0))[None, :]
    position = (
        pick(0) * wide(frame_id[:, None])
        + pick(1) * wide(patch_row[:, None])
        + pick(2) * wide(column[:, None])
    )
    angles = position * frequency[None, :]
    lower = (dim_index % segment < half_width)[None, :]
    sine = jnp.where((segment_id < 3)[None, :], jnp.sin(angles), 0.0)
    return (jnp.cos(angles), jnp.where(lower, -sine, 0.0), jnp.where(lower, 0.0, sine))


def spin(x, cos, up, down):
    turn = HEAD_DIM // 3 // 2
    return x * cos + pltpu.roll(x, PAIR - turn, 1) * up + pltpu.roll(x, turn, 1) * down


def standardize(values_in):
    row_mean = jnp.mean(values_in, -1, keepdims=True)
    centred = values_in - row_mean
    norm_scale = lax.rsqrt(jnp.mean(centred * centred, -1, keepdims=True) + EPSILON)
    return (centred * norm_scale, norm_scale)


def fold(x):
    return jnp.sum(x.reshape(x.shape[0] // 8, 8, x.shape[1]), 0)


def whole(array):
    return pl.BlockSpec(array.shape, lambda *_: (0,) * array.ndim, pipeline_mode=pl.Buffered(1))


def enter_kernel(side_ref, mine_ref, arrived_ref, gain_ref, shift_ref, stream_ref, out_ref):
    def step(rows):
        stream_ref[...] = rows
        normed, _ = standardize(wide(rows))
        out_ref[...] = low(normed * gain_ref[...] + shift_ref[...])

    @pl.when(pl.program_id(0) == 0)
    def _():
        step(mine_ref[0])

    @pl.when(pl.program_id(0) == 1)
    def _():
        step(arrived_ref[...])


def enter(side, tokens, arrived, gain, shift):
    _, half, depth = tokens.shape
    vector = pl.BlockSpec((1, depth), lambda i, side: (0, 0))
    out = pl.BlockSpec((half, depth), lambda i, side: (jnp.where(i == 0, side[0], 1 - side[0]), 0))
    return pl.pallas_call(
        enter_kernel,
        grid_spec=pltpu.PrefetchScalarGridSpec(
            num_scalar_prefetch=1,
            grid=(2,),
            in_specs=[
                pl.BlockSpec((1, half, depth), lambda i, side: (side[0], 0, 0)),
                pl.BlockSpec((half, depth), lambda i, side: (0, 0)),
                vector,
                vector,
            ],
            out_specs=[out, out],
        ),
        out_shape=[jax.ShapeDtypeStruct((2 * half, depth), jnp.bfloat16)] * 2,
        compiler_params=params(),
        cost_estimate=takes(5),
        name="enter",
    )(side, tokens, arrived, gain[None], shift[None])


def project_kernel(chunk, x_ref, w_ref, b_ref, cos_ref, up_ref, down_ref, out_ref):
    part = pl.program_id(0)
    for at in range(0, x_ref.shape[0], chunk):
        rows = slice(at, at + chunk)
        y = dot(x_ref[rows, :], w_ref[...]) + b_ref[...]

        @pl.when(part == 2)
        def _():
            out_ref[rows, :] = low(y)

        @pl.when(part < 2)
        def _():
            cos, up, down = cos_ref[rows, :], up_ref[rows, :], down_ref[rows, :]
            for lane in range(0, y.shape[1], PAIR):
                lanes = slice(lane, lane + PAIR)
                out_ref[rows, lanes] = low(spin(y[:, lanes], cos, up, down))


def project(x, weight, bias, tables):
    rows, depth = x.shape
    width = weight.shape[1] // 3
    return pl.pallas_call(
        functools.partial(project_kernel, rows),
        grid=(3,),
        in_specs=[
            whole(x),
            pl.BlockSpec((depth, width), lambda i: (0, i)),
            pl.BlockSpec((1, width), lambda i: (0, i)),
        ]
        + [whole(table) for table in tables],
        out_specs=pl.BlockSpec((rows, width), lambda i: (0, i)),
        out_shape=jax.ShapeDtypeStruct((rows, 3 * width), jnp.bfloat16),
        compiler_params=params(),
        cost_estimate=takes(7),
        name="project",
    )(x, weight, bias[None], *tables)


def attend_kernel(q_ref, k_ref, v_ref, lo_ref, hi_ref, out_ref, root_ref, early_ref, late_ref):
    lane = lax.broadcasted_iota(jnp.int32, (1, PAIR), 1)
    factor = HEAD_DIM**-0.5 * LOG2E
    values = v_ref[...].T
    for first, past, stop in STRIPS:
        count = past - first
        q = q_ref[first:past, :]
        key = lax.broadcasted_iota(jnp.int32, (stop, count), 0)
        allowed = (key >= lo_ref[:, first:past]) & (key < hi_ref[:, first:past])
        outs, roots = [], []
        for head in range(2):
            own = (lane >= HEAD_DIM) == (head == 1)
            scores = dot_nt(k_ref[0:stop, :], jnp.where(own, q, jnp.zeros_like(q)))
            scores = jnp.where(allowed, scores, NEG)
            powers = jnp.exp2((scores - jnp.max(scores, 0, keepdims=True)) * factor)
            root = 1.0 / jnp.sum(powers, 0, keepdims=True)
            powers = low(powers)
            if past <= EARLY:
                early_ref[head, :, first:past] = powers
            else:
                late_ref[head, 0:stop, first - EARLY : past - EARLY] = powers
            rows = slice(head * HEAD_DIM, (head + 1) * HEAD_DIM)
            outs.append(dot(values[rows, 0:stop], powers) * root)
            roots.append(jnp.broadcast_to(root, (HEAD_DIM, count)))
        out_ref[first:past, :] = low(jnp.concatenate(outs, 0).T)
        root_ref[first:past, :] = jnp.concatenate(roots, 0).T


def kept_specs(rows):
    return [
        pl.BlockSpec((2, STRIPS[0][2], EARLY), lambda i: (i, 0, 0)),
        pl.BlockSpec((2, rows, rows - EARLY), lambda i: (i, 0, 0)),
    ]


def attend(heads, first_key, past_key):
    rows, width = heads.shape[0], heads.shape[1] // 3
    pairs = width // PAIR
    block = pl.BlockSpec((rows, PAIR), lambda i: (0, i))
    part = lambda number: pl.BlockSpec((rows, PAIR), lambda i: (0, number * pairs + i))
    return pl.pallas_call(
        attend_kernel,
        grid=(pairs,),
        in_specs=[part(0), part(1), part(2), whole(first_key), whole(past_key)],
        out_specs=[block, block] + kept_specs(rows),
        out_shape=[
            jax.ShapeDtypeStruct((rows, width), jnp.bfloat16),
            jax.ShapeDtypeStruct((rows, width), jnp.float32),
            jax.ShapeDtypeStruct((2 * pairs, STRIPS[0][2], EARLY), jnp.bfloat16),
            jax.ShapeDtypeStruct((2 * pairs, rows, rows - EARLY), jnp.bfloat16),
        ],
        compiler_params=params(),
        cost_estimate=takes(17),
        name="attend",
    )(heads, heads, heads, first_key, past_key)


def attend_back_kernel(
    q_ref, k_ref, v_ref, g_ref, o_ref, root_ref, early_ref, late_ref, cos_ref, up_ref, down_ref,
    out_ref, sums_ref, keys_acc, values_acc, queries_acc,
):
    pair = pl.program_id(0)
    pairs = out_ref.shape[1] // (3 * PAIR)
    lane = lax.broadcasted_iota(jnp.int32, (1, PAIR), 1)
    scale = HEAD_DIM**-0.5
    keys = k_ref[...].T
    for first, past, stop in STRIPS[::-1]:
        q = q_ref[first:past, :]
        g = wide(g_ref[first:past, :]) * root_ref[first:past, :]
        inner = (g * wide(o_ref[first:past, :])).T
        g = low(g)
        for head in range(2):
            own = (lane >= HEAD_DIM) == (head == 1)
            rows = slice(head * HEAD_DIM, (head + 1) * HEAD_DIM)
            g_own = jnp.where(own, g, jnp.zeros_like(g))
            shift = jnp.sum(inner[rows, :], 0, keepdims=True)
            if past <= EARLY:
                powers = early_ref[head, :, first:past]
            else:
                powers = late_ref[head, 0:stop, first - EARLY : past - EARLY]
            g_scores = low(wide(powers) * (dot_nt(v_ref[0:stop, :], g_own) - shift))
            queries_acc[rows, first:past] = dot(keys[rows, 0:stop], g_scores)
            g_keys = dot(g_scores, jnp.where(own, q, jnp.zeros_like(q)))
            g_values = dot(powers, g_own)
            if head == 0:
                total_keys, total_values = g_keys, g_values
            else:
                total_keys, total_values = total_keys + g_keys, total_values + g_values
        if past == STRIPS[-1][1]:
            keys_acc[...] = total_keys
            values_acc[...] = total_values
        else:
            keys_acc[0:stop, :] += total_keys
            values_acc[0:stop, :] += total_values
    cos, up, down = cos_ref[...], -up_ref[...], -down_ref[...]
    grads = (
        low(spin(queries_acc[...].T * scale, cos, up, down)),
        low(spin(keys_acc[...] * scale, cos, up, down)),
        low(values_acc[...]),
    )
    for number, grad in enumerate(grads):
        lanes = pl.ds(pl.multiple_of((number * pairs + pair) * PAIR, PAIR), PAIR)
        out_ref[:, lanes] = grad
        sums_ref[:, lanes] = fold(wide(grad))


def attend_back(heads, g, out, root, early, late, tables):
    rows, width = g.shape
    pairs = width // PAIR
    block = pl.BlockSpec((rows, PAIR), lambda i: (0, i))
    part = lambda number: pl.BlockSpec((rows, PAIR), lambda i: (0, number * pairs + i))
    return pl.pallas_call(
        attend_back_kernel,
        grid=(pairs,),
        in_specs=[part(0), part(1), part(2), block, block, block]
        + kept_specs(rows)
        + [whole(table) for table in tables],
        out_specs=[
            pl.BlockSpec((rows, 3 * width), lambda i: (0, 0)),
            pl.BlockSpec((8, 3 * width), lambda i: (0, 0)),
        ],
        out_shape=[
            jax.ShapeDtypeStruct((rows, 3 * width), jnp.bfloat16),
            jax.ShapeDtypeStruct((8, 3 * width), jnp.float32),
        ],
        scratch_shapes=[
            pltpu.VMEM((rows, PAIR), jnp.float32),
            pltpu.VMEM((rows, PAIR), jnp.float32),
            pltpu.VMEM((PAIR, rows), jnp.float32),
        ],
        compiler_params=params(56),
        cost_estimate=takes(20),
        name="attend_back",
    )(heads, heads, heads, g, out, root, early, late, *tables)


def merge_kernel(count, *refs):
    rights, lefts = refs[:count], refs[count : 2 * count]
    x_ref, bias_ref, gain_ref, shift_ref, residual_ref, out_ref = refs[2 * count :]
    total = wide(x_ref[...]) + bias_ref[...]
    for left, right in zip(lefts, rights):
        total = total + dot(left[...], right[...])
    residual_ref[...] = total
    normed, _ = standardize(total)
    out_ref[...] = low(normed * gain_ref[...] + shift_ref[...])


def merge(lefts, rights, x, bias, gain, shift, block=256):
    rows, depth = x.shape
    row = lambda array: pl.BlockSpec((block, array.shape[1]), lambda i: (i, 0))
    vectors = (bias[None], gain[None], shift[None])
    return pl.pallas_call(
        functools.partial(merge_kernel, len(lefts)),
        grid=(rows // block,),
        in_specs=[whole(w) for w in rights]
        + [row(a) for a in lefts]
        + [row(x)]
        + [whole(v) for v in vectors],
        out_specs=[row(x), row(x)],
        out_shape=[
            jax.ShapeDtypeStruct((rows, depth), jnp.float32),
            jax.ShapeDtypeStruct((rows, depth), jnp.bfloat16),
        ],
        compiler_params=params(),
        cost_estimate=takes(8),
        name="merge",
    )(*rights, *lefts, x, *vectors)


def expand_kernel(chunk, x_ref, w_ref, b_ref, active_ref, slope_ref):
    for at in range(0, x_ref.shape[0], chunk):
        rows = slice(at, at + chunk)
        v = dot(x_ref[rows, :], w_ref[...]) + b_ref[...]
        below = 0.5 + 0.5 * lax.erf(v * ROOT_HALF)
        active_ref[rows, :] = low(v * below)
        slope_ref[rows, :] = low(below + v * jnp.exp(-0.5 * v * v) * GAUSS_NORM)


def expand(x, weight, bias, block=512, chunk=256):
    rows, depth = x.shape
    width = weight.shape[1]
    out = pl.BlockSpec((rows, block), lambda i: (0, i))
    return pl.pallas_call(
        functools.partial(expand_kernel, chunk),
        grid=(width // block,),
        in_specs=[
            whole(x),
            pl.BlockSpec((depth, block), lambda i: (0, i)),
            pl.BlockSpec((1, block), lambda i: (0, i)),
        ],
        out_specs=[out, out],
        out_shape=[jax.ShapeDtypeStruct((rows, width), jnp.bfloat16)] * 2,
        compiler_params=params(),
        cost_estimate=takes(8.5),
        name="expand",
    )(x, weight, bias[None])


def reduce_kernel(count, half, side_ref, *refs):
    rights, lefts = refs[:count], refs[count : 2 * count]
    x_ref, bias_ref, send_ref, keep_ref = refs[2 * count :]
    total = x_ref[...] + bias_ref[...]
    for left, right in zip(lefts, rights):
        total = total + dot(left[...], right[...])

    @pl.when(pl.program_id(0) < half)
    def _():
        send_ref[...] = low(total)

    @pl.when(pl.program_id(0) >= half)
    def _():
        keep_ref[...] = low(total)


def reduce_rows(side, lefts, rights, x, bias, block=320):
    rows, depth = x.shape
    half = rows // 2 // block
    at = lambda i, side: jnp.where(i < half, (1 - side[0]) * half + i, side[0] * half + i - half)
    row = lambda array: pl.BlockSpec((block, array.shape[1]), lambda i, side: (at(i, side), 0))
    return pl.pallas_call(
        functools.partial(reduce_kernel, len(lefts), half),
        grid_spec=pltpu.PrefetchScalarGridSpec(
            num_scalar_prefetch=1,
            grid=(2 * half,),
            in_specs=[whole(w) for w in rights]
            + [row(a) for a in lefts]
            + [row(x), whole(bias[None])],
            out_specs=[
                pl.BlockSpec((block, depth), lambda i, side: (jnp.minimum(i, half - 1), 0)),
                pl.BlockSpec((block, depth), lambda i, side: (jnp.maximum(i - half, 0), 0)),
            ],
        ),
        out_shape=[jax.ShapeDtypeStruct((rows // 2, depth), jnp.bfloat16)] * 2,
        compiler_params=params(),
        cost_estimate=takes(0.1),
        name="reduce_rows",
    )(side, *rights, *lefts, x, bias[None])


def back_kernel(count, at_ref, *refs):
    rights, lefts = refs[:count], refs[count : 2 * count]
    base_ref, above_ref, gain_ref, out_ref, sums_ref = refs[2 * count :]

    @pl.when(pl.program_id(0) == 0)
    def _():
        sums_ref[...] = jnp.zeros_like(sums_ref)

    g = dot_nt(lefts[0][...], rights[0][...])
    for left, right in zip(lefts[1:], rights[1:]):
        g = g + dot_nt(left[...], right[...])
    normed, scale = standardize(wide(base_ref[...]))
    u = g * gain_ref[...]
    above = wide(above_ref[...])
    inner = jnp.mean(u, -1, keepdims=True) + normed * jnp.mean(u * normed, -1, keepdims=True)
    out = low(above + scale * (u - inner))
    out_ref[...] = out
    sums_ref[0] += fold(g * normed)
    sums_ref[1] += fold(g)
    sums_ref[2] += fold(wide(out))
    sums_ref[3] += fold(above)


def back_norm(at, rows, lefts, rights, base, above, gain, block=320):
    depth = base.shape[1]
    row = lambda array: pl.BlockSpec((block, array.shape[1]), lambda i, at: (at[0] + i, 0))
    return pl.pallas_call(
        functools.partial(back_kernel, len(lefts)),
        grid_spec=pltpu.PrefetchScalarGridSpec(
            num_scalar_prefetch=1,
            grid=(rows // block,),
            in_specs=[whole(w) for w in rights]
            + [row(a) for a in lefts]
            + [row(base), row(above), whole(gain[None])],
            out_specs=[
                pl.BlockSpec((block, depth), lambda i, at: (i, 0)),
                pl.BlockSpec((4, 8, depth), lambda i, at: (0, 0, 0)),
            ],
        ),
        out_shape=[
            jax.ShapeDtypeStruct((rows, depth), jnp.bfloat16),
            jax.ShapeDtypeStruct((4, 8, depth), jnp.float32),
        ],
        compiler_params=params(),
        cost_estimate=takes(0.1 if rows == base.shape[0] else 10),
        name="back_norm",
    )(at, *rights, *lefts, base, above, gain[None])


def place_kernel(steps, flag_ref, mine_ref, theirs_ref, out_ref):
    @pl.when(pl.program_id(0) < steps)
    def _():
        out_ref[...] = mine_ref[...].astype(out_ref.dtype).reshape(out_ref.shape)

    @pl.when(pl.program_id(0) >= steps)
    def _():
        out_ref[...] = theirs_ref[...].astype(out_ref.dtype).reshape(out_ref.shape)


def place(flag, mine, theirs, steps, in_block, in_index, out_shape, out_block, out_index, dtype):
    def target(i, flag):
        return out_index(jnp.where(i < steps, flag[0], 1 - flag[0]), jnp.where(i < steps, i, i - steps))

    return pl.pallas_call(
        functools.partial(place_kernel, steps),
        grid_spec=pltpu.PrefetchScalarGridSpec(
            num_scalar_prefetch=1,
            grid=(2 * steps,),
            in_specs=[
                pl.BlockSpec(in_block, lambda i, flag: in_index(jnp.minimum(i, steps - 1))),
                pl.BlockSpec(in_block, lambda i, flag: in_index(jnp.maximum(i - steps, 0))),
            ],
            out_specs=pl.BlockSpec(out_block, target),
        ),
        out_shape=jax.ShapeDtypeStruct(out_shape, dtype),
        compiler_params=params(),
        cost_estimate=takes(4),
        name="place",
    )(flag, mine, theirs)


def place_rows(flag, mine, theirs, steps, dtype):
    rows, width = mine.shape
    block = (rows // steps, width)
    return place(
        flag, mine, theirs, steps, block, lambda j: (j, 0),
        (2 * rows, width), block, lambda half, j: (half * steps + j, 0), dtype,
    )


def place_columns(flag, mine, theirs, steps, dtype):
    rows, width = mine.shape
    block = (rows // steps, width)
    return place(
        flag, mine, theirs, steps, block, lambda j: (j, 0),
        (rows, 2 * width), block, lambda half, j: (j, half), dtype,
    )


def place_heads(flag, mine, theirs, dtype):
    rows, width = mine.shape[0], mine.shape[1] // 3
    return place(
        flag, mine, theirs, 3, (rows, width), lambda j: (0, j),
        (3, rows, 2 * width), (1, rows, width), lambda half, j: (j, 0, half), dtype,
    )


def column_sums(matrix):
    unit_column = jnp.ones((matrix.shape[0],), matrix.dtype)
    return jnp.dot(unit_column, matrix, preferred_element_type=jnp.float32)


KEEP, SEND = 0, 1
OWN, FAR = 0, 1
QUARTERS = ((FAR, SEND), (FAR, KEEP), (OWN, SEND), (OWN, KEEP))


def on_device(
    spread,
    tokens,
    cotangent,
    patch_count,
    first_gain,
    first_shift,
    heads_weight,
    heads_bias,
    merge_weight,
    merge_bias,
    second_gain,
    second_shift,
    expand_weight,
    expand_bias,
    reduce_weight,
    reduce_bias,
):
    levels = spread.bit_length() - 1
    rest = list(range(1, levels))
    chunks = spread // 2
    location = lax.axis_index("dp")
    side = lax.axis_index("mp")
    sides = side[None].astype(jnp.int32)
    previous = []

    def bit(level):
        return (location >> level) & 1

    core = bit(0)[None].astype(jnp.int32)

    def tie(array, *others):
        return lax.optimization_barrier((array,) + others)[0] if others else array

    def after(array):
        return tie(array, *previous)

    def did(*arrays):
        previous[:] = arrays
        return arrays[0] if len(arrays) == 1 else arrays

    def swap(array, level):
        return lax.ppermute(array, "dp", [(i, i ^ (1 << level)) for i in range(spread)])

    def cross(array):
        return lax.ppermute(array, "mp", [(0, 1), (1, 0)])

    def half_of(array, flag, axis=0):
        size = array.shape[axis] // 2
        return lax.dynamic_slice_in_dim(array, flag * size, size, axis)

    def chunk_of(array):
        size = array.shape[0] // chunks
        return lax.dynamic_slice_in_dim(array, (location >> 1) * size, size, 0)

    def split(array, level, open_levels=None):
        left = 1 << sum(other > level for other in (open_levels or rest))
        four = array.reshape(left, 2, -1, array.shape[1])
        part = lambda flag: lax.dynamic_index_in_dim(four, flag, 1, False).reshape(-1, array.shape[1])
        return part(bit(level)), part(1 - bit(level))

    def join(mine, theirs, level, open_levels=None):
        left = 1 << sum(other > level for other in (open_levels or rest))
        four = lambda array: array.reshape(left, 1, -1, array.shape[1])
        pair = jnp.where(
            bit(level) == 0,
            jnp.concatenate([four(mine), four(theirs)], 1),
            jnp.concatenate([four(theirs), four(mine)], 1),
        )
        return pair.reshape(-1, mine.shape[1])

    def quarters_of(own, axis):
        return [half_of(own, bit(0), axis), half_of(own, 1 - bit(0), axis)]

    tokens, cotangent = tokens[:, 0], cotangent[:, 0]
    tokens_far = cross(lax.dynamic_index_in_dim(tokens, 1 - side, 0, False))
    heads_three = heads_weight.transpose(1, 0, 2)
    heads_own = [
        jnp.concatenate([half_of(heads_three[n], flag, 1) for n in range(3)], 1)
        for flag in (bit(0), 1 - bit(0))
    ]
    merge_own = quarters_of(merge_weight, 0)
    expand_own = quarters_of(expand_weight, 1)
    reduce_own = quarters_of(reduce_weight, 0)
    pack = lambda hb, eb: jnp.concatenate([hb.reshape(-1), eb])
    bias_own = [
        pack(half_of(heads_bias, flag, 1), half_of(expand_bias, flag)) for flag in (bit(0), 1 - bit(0))
    ]
    three = heads_bias.size // 2
    near = rest[:2]
    heads_piece = heads_own[KEEP]
    for n, level in enumerate(near):
        heads_piece = split(heads_piece, level, near[n:])[0]
    up_piece = jnp.concatenate([chunk_of(expand_own[KEEP]), chunk_of(merge_own[KEEP])])
    down_piece = chunk_of(reduce_own[KEEP])

    count_one = lax.dynamic_index_in_dim(patch_count[:, 0], side, 0, False)
    length = 2 * tokens.shape[1]
    first_key, past_key, frame_id, patch_row, column = slot_layout(count_one, length)
    tables = rotary_tables(frame_id, patch_row, column)
    first_key, past_key = first_key[None], past_key[None]

    did(heads_piece, up_piece, down_piece, *heads_own, *merge_own, *expand_own, *reduce_own, *tables)
    heads_piece = cross(tie(heads_piece, tokens_far))
    up_piece = cross(tie(up_piece, tokens_far))
    bias_both = cross(tie(jnp.concatenate(bias_own), tokens_far))
    bias_far = [bias_both[: bias_both.size // 2], bias_both[bias_both.size // 2 :]]
    stream, first_out = did(*enter(sides, after(tokens), tokens_far, first_gain, first_shift))
    heads, seen = {}, {}
    heads_all = [heads_own, None]
    bias_all = (bias_own, bias_far)

    def look(p, c):
        heads[p, c] = did(project(after(first_out), heads_all[p][c], bias_all[p][c][:three], tables))

    def attention(p, c):
        seen[p, c] = did(*attend(after(heads[p, c]), first_key, past_key))

    def gathered(array, *splits):
        array = lax.all_gather(array, "dp", axis=0, tiled=True)
        array = array.reshape(chunks, 2, -1, array.shape[1])
        quarters, at = [], 0
        for size in splits:
            part = array[:, :, at : at + size]
            quarters.append(
                [
                    lax.dynamic_index_in_dim(part, flag, 1, False).reshape(-1, array.shape[3])
                    for flag in (bit(0), 1 - bit(0))
                ]
            )
            at += size
        return quarters

    look(OWN, KEEP)
    look(OWN, SEND)
    heads_piece = did(after(heads_piece))
    if len(near) > 1:
        heads_next = swap(heads_piece, near[1])
    attention(OWN, KEEP)
    up_sizes = (expand_own[0].shape[0] // chunks, merge_own[0].shape[0] // chunks)
    up_gathered = gathered(after(up_piece), *up_sizes)
    down_piece = cross(after(down_piece))
    if len(near) > 1:
        heads_piece = did(join(after(heads_piece), heads_next, near[1], near[1:]))
    heads_next = swap(heads_piece, near[0])
    attention(OWN, SEND)
    heads_piece = did(join(after(heads_piece), heads_next, near[0], near))
    heads_all[FAR] = [heads_piece, swap(heads_piece, 0)]
    cotangent_far = cross(after(lax.dynamic_index_in_dim(cotangent, 1 - side, 0, False)))
    (reduce_far,) = gathered(after(down_piece), down_piece.shape[0])
    look(FAR, KEEP)
    attention(FAR, KEEP)
    look(FAR, SEND)
    attention(FAR, SEND)
    expand_far, merge_far = ([after(q) for q in quarters] for quarters in up_gathered)
    merge_all = (merge_own, merge_far)
    expand_all = (expand_own, expand_far)
    reduce_all = (reduce_own, reduce_far)
    mixed = {q: seen[q][0] for q in QUARTERS}
    residual, second_out = did(
        *merge(
            [mixed[q] for q in QUARTERS], [merge_all[p][c] for p, c in QUARTERS],
            after(stream), merge_bias, second_gain, second_shift,
        )
    )
    cotangent_far = after(cotangent_far)
    grad_two = jnp.where(
        side == 0,
        jnp.concatenate([cotangent[0], cotangent_far]),
        jnp.concatenate([cotangent_far, cotangent[1]]),
    )

    active, slope, grad_pre = {}, {}, {}

    def widen(p, c):
        active[p, c], slope[p, c] = did(
            *expand(after(second_out), expand_all[p][c], bias_all[p][c][three:])
        )

    def back_active(p, c):
        grad_pre[p, c] = did(low(dot_nt(after(grad_two), reduce_all[p][c]) * wide(slope[p, c])))

    def product(left, right, *arrived):
        total = dot_tn(after(left), right)
        for array in arrived:
            total = total + wide(array)
        return did(low(total))

    def scattered(array, level, open_levels=None):
        keep, send = split(after(array), level, open_levels or rest[rest.index(level) :])
        did(send)
        return keep, swap(send, level)

    def summed(keep, arrived):
        return did(low(wide(after(keep)) + wide(arrived)))

    def rows_out(keep, arrived, dtype):
        return place_rows(sides, keep, arrived, 1, dtype).reshape(2, 1, length // 2, -1)

    widen(FAR, SEND)
    widen(FAR, KEEP)
    sent = swap(product(active[FAR, SEND], grad_two), 0)
    widen(OWN, SEND)
    reduce_far_sum = product(active[FAR, KEEP], grad_two, sent)
    reduce_cross = cross(reduce_far_sum)
    widen(OWN, KEEP)
    sent = swap(product(active[OWN, SEND], grad_two), 0)
    back_active(FAR, SEND)
    reduce_sum = product(active[OWN, KEEP], grad_two, sent)
    back_active(FAR, KEEP)
    sent = swap(product(second_out, grad_pre[FAR, SEND]), 0)
    layer_send, layer_keep = did(
        *reduce_rows(
            sides, [active[q] for q in QUARTERS], [reduce_all[p][c] for p, c in QUARTERS],
            after(residual), reduce_bias,
        )
    )
    back_active(OWN, SEND)
    expand_far_sum = product(second_out, grad_pre[FAR, KEEP], sent)
    back_active(OWN, KEEP)
    sent = swap(product(second_out, grad_pre[OWN, SEND]), 0)
    reduce_sum = summed(reduce_sum, reduce_cross)
    expand_cross = cross(tie(expand_far_sum, reduce_cross))
    reduce_keep, reduce_next = scattered(reduce_sum, rest[0])
    expand_sum = product(second_out, grad_pre[OWN, KEEP], sent)
    zero = jnp.zeros((1,), jnp.int32)
    grad_one, second_sums = did(
        *back_norm(
            zero, length, [grad_pre[q] for q in QUARTERS], [expand_all[p][c] for p, c in QUARTERS],
            after(residual), grad_two, second_gain,
        )
    )
    reduce_sum = summed(reduce_keep, reduce_next)
    reduce_keep, reduce_next = scattered(reduce_sum, rest[1])

    grad_mixed, grad_heads, head_sums = {}, {}, {}

    def back_mixed(p, c):
        grad_mixed[p, c] = did(low(dot_nt(after(grad_one), merge_all[p][c])))

    def back_attention(q):
        out, root, early, late = seen[q]
        grad_heads[q], sums = did(
            *attend_back(heads[q], after(grad_mixed[q]), out, root, early, late, tables)
        )
        head_sums[q] = jnp.sum(sums, 0)

    sent_far = swap(product(mixed[FAR, SEND], grad_one), 0)
    sent_own = swap(product(mixed[OWN, SEND], grad_one), 0)
    for p, c in QUARTERS:
        back_mixed(p, c)
    merge_far_sum = product(mixed[FAR, KEEP], grad_one, sent_far)
    merge_sum = product(mixed[OWN, KEEP], grad_one, sent_own)
    expand_sum = summed(expand_sum, expand_cross)
    merge_cross = cross(tie(merge_far_sum, expand_cross))
    layer_far = cross(tie(layer_send, expand_cross))
    expand_keep, expand_next = scattered(expand_sum, rest[0])
    reduce_sum = summed(reduce_keep, reduce_next)
    for level in rest[2:]:
        reduce_keep, reduce_next = scattered(reduce_sum, level)
        reduce_sum = low(wide(reduce_keep) + wide(reduce_next))
    back_attention((FAR, SEND))
    reduce_total = lax.all_gather(after(reduce_sum), "dp", axis=0, tiled=True)
    expand_sum = summed(expand_keep, expand_next)
    expand_keep, expand_next = scattered(expand_sum, rest[1])
    sent = swap(product(first_out, grad_heads[FAR, SEND]), 0)
    merge_sum = summed(merge_sum, merge_cross)
    merge_keep, merge_next = scattered(merge_sum, rest[0])
    back_attention((FAR, KEEP))
    heads_far_sum = product(first_out, grad_heads[FAR, KEEP], sent)
    heads_cross = cross(heads_far_sum)
    expand_sum = summed(expand_keep, expand_next)
    merge_sum = summed(merge_keep, merge_next)
    merge_keep, merge_next = scattered(merge_sum, rest[1])
    for level in rest[2:]:
        expand_keep, expand_next = scattered(expand_sum, level)
        expand_sum = low(wide(expand_keep) + wide(expand_next))
    back_attention((OWN, SEND))
    merge_sum = summed(merge_keep, merge_next)
    layer_out = rows_out(after(layer_keep), layer_far, jnp.bfloat16)
    merge_sum, layer_out = lax.optimization_barrier((merge_sum, layer_out))
    for level in rest[2:]:
        merge_keep, merge_next = scattered(merge_sum, level)
        merge_sum = low(wide(merge_keep) + wide(merge_next))
    sent = swap(product(first_out, grad_heads[OWN, SEND]), 0)
    back_attention((OWN, KEEP))
    expand_total = lax.all_gather(
        after(jnp.concatenate([expand_sum, merge_sum])), "dp", axis=0, tiled=True
    )
    heads_sum = product(first_out, grad_heads[OWN, KEEP], sent, heads_cross)
    orders = [rest, rest[1:2] + rest[:1] + rest[2:]]
    middle = heads_sum.shape[1] // 2
    heads_sums = [heads_sum[:, :middle], heads_sum[:, middle:]]

    def both_scattered(n):
        return [scattered(total, order[n], order[n:]) for total, order in zip(heads_sums, orders)]

    def both_summed(pairs):
        return [summed(*pair) for pair in pairs]

    def in_rows(array):
        return wide(array.transpose(1, 0, 2, 3).reshape(-1, array.shape[3]))

    reduce_total = reduce_total.reshape(chunks, 2, -1, reduce_total.shape[1])
    expand_total = expand_total.reshape(chunks, 2, -1, expand_total.shape[1])
    rows = expand_sum.shape[0]

    pairs = both_scattered(0)
    lefts = [grad_heads[q] for q in QUARTERS]
    rights = [heads_all[p][c] for p, c in QUARTERS]
    per_half = length // 2 // 320
    tokens_send, sums_a = did(
        *back_norm(
            (1 - sides) * per_half, length // 2, lefts, rights, stream, grad_one, after(first_gain)
        )
    )
    tokens_cross = cross(tokens_send)
    heads_sums = both_summed(pairs)
    pairs = both_scattered(1)
    tokens_keep, sums_b = did(
        *back_norm(sides * per_half, length // 2, lefts, rights, stream, grad_one, after(first_gain))
    )
    first_sums = sums_a + sums_b

    small = {q: jnp.concatenate([head_sums[q], column_sums(grad_pre[q])]) for q in QUARTERS}
    both = jnp.concatenate(
        [
            jnp.sum(part, 0)
            for part in (
                first_sums[0], first_sums[1], second_sums[0], second_sums[1], second_sums[2], second_sums[3],
            )
        ]
    )
    far_send, own_send, both = did(*(after(v) for v in (small[FAR, SEND], small[OWN, SEND], both)))
    arrived = swap(jnp.concatenate([far_send, own_send, both]), 0)
    size = own_send.size
    heads_sums = both_summed(pairs)
    mine = jnp.concatenate([small[FAR, KEEP] + arrived[:size], small[OWN, KEEP], both])
    mine = did(
        jnp.concatenate([mine[:size], mine[size:] + after(arrived)[size:]])
    )
    for n in range(2, len(rest)):
        pairs = both_scattered(n)
        small_next = swap(mine, rest[n])
        if n == 2:
            reduce_out = in_rows(after(reduce_total))
            mine, reduce_out = lax.optimization_barrier((mine, reduce_out))
            did(mine)
        heads_sums = both_summed(pairs)
        mine = did(mine + after(small_next))
    for n in range(len(rest))[::-1]:
        arrived = [swap(total, order[n]) for total, order in zip(heads_sums, orders)]
        small_next = swap(mine, rest[n]) if n < 2 else None
        if n == len(rest) - 1:
            expand_out = wide(
                jnp.concatenate(
                    [
                        after(expand_total)[:, n, :rows].reshape(-1, expand_total.shape[3])
                        for n in range(2)
                    ],
                    1,
                )
            )
            mine, expand_out = lax.optimization_barrier((mine, expand_out))
            did(mine)
        if n == 0:
            tokens_out = rows_out(after(tokens_keep), tokens_cross, jnp.float32)
            mine, tokens_out = lax.optimization_barrier((mine, tokens_out))
            did(mine)
        heads_sums = [
            did(join(after(total), other, order[n], order[n:]))
            for total, other, order in zip(heads_sums, arrived, orders)
        ]
        if n < 2:
            mine = did(mine + after(small_next))
    heads_sum = jnp.concatenate(heads_sums, 1)
    heads_next = swap(heads_sum, 0)
    arrived = cross(jnp.concatenate([mine[:size], mine[2 * size :]]))
    both = mine[2 * size :] + arrived[size:]
    mine = mine[size : 2 * size] + arrived[:size]
    theirs = swap(mine, 0)
    first = jnp.where(bit(0) == 0, mine, theirs)
    second = jnp.where(bit(0) == 0, theirs, mine)
    heads_bias_total = jnp.concatenate([first[:three].reshape(3, -1), second[:three].reshape(3, -1)], 1)
    expand_bias_total = jnp.concatenate([first[three:], second[three:]])
    (first_gain_total, first_shift_total, second_gain_total, second_shift_total, merge_bias_total,
     reduce_bias_total) = both.reshape(6, -1)
    heads_out = place_heads(core, heads_sum, heads_next, jnp.float32)
    return (
        layer_out,
        tokens_out,
        first_gain_total,
        first_shift_total,
        heads_out.transpose(1, 0, 2),
        heads_bias_total,
        in_rows(expand_total[:, :, rows:]),
        merge_bias_total,
        second_gain_total,
        second_shift_total,
        expand_out,
        expand_bias_total,
        reduce_out,
        reduce_bias_total,
    )


def solution(mesh):
    rows = P(None, "dp", "mp", None)
    columns = P(None, "mp")
    heads = P(None, None, "mp")
    return jax.shard_map(
        functools.partial(on_device, mesh.shape["dp"]),
        mesh=mesh,
        in_specs=(
            rows, rows, P(None, "dp"), P(), P(), heads, columns, P("mp", None), P(), P(), P(), columns,
            P("mp"), P("mp", None), P(),
        ),
        out_specs=(
            rows, rows, P(), P(), heads, columns, P("mp", None), P(), P(), P(), columns, P("mp"),
            P("mp", None), P(),
        ),
        check_vma=False,
    )
```

```python
import functools
import math

import jax
import jax.numpy as jnp
from jax import lax
from jax.experimental import pallas as pl
from jax.experimental.pallas import tpu as pltpu
from jax.sharding import PartitionSpec as P

HEAD_DIM = 64
FRAMES = 2
SIDE_SMALL = 16
SIDE_LARGE = 24
EPSILON = 1e-06
ROOT_HALF = 0.7071067811865476
GAUSS_NORM = 0.3989422804014327
LOG2E = math.log2(math.e)
PAIR = 128
NEG = -1e30
STRIPS = ((0, 512, 592), (512, 1024, 1168), (1024, 1280, 1280))
EARLY = 512


def params(mib=50):
    return pltpu.CompilerParams(vmem_limit_bytes=mib * 2**20)


def takes(microseconds):
    return pl.CostEstimate(
        flops=int(microseconds * 4e9), bytes_accessed=int(microseconds * 4e6), transcendentals=0
    )


def low(array):
    return array.astype(jnp.bfloat16)


def wide(array):
    return array.astype(jnp.float32)


def dot(left, right):
    return jnp.dot(left, right, preferred_element_type=jnp.float32)


def dot_nt(left, right):
    return lax.dot_general(
        left, right, (((1,), (1,)), ((), ())), preferred_element_type=jnp.float32
    )


def dot_tn(left, right):
    return lax.dot_general(
        left, right, (((0,), (0,)), ((), ())), preferred_element_type=jnp.float32
    )


def slot_layout(count_one, length):
    large_count = SIDE_LARGE * SIDE_LARGE
    grid_side = jnp.where(count_one == large_count, SIDE_LARGE, SIDE_SMALL).astype(jnp.int32)
    frame_len = grid_side * grid_side + 2
    clip_len = FRAMES * frame_len
    clip_total = jnp.where(count_one == large_count, 1, 2).astype(jnp.int32)
    slot_id = jnp.arange(length, dtype=jnp.int32)
    clip_id = jnp.minimum(slot_id // clip_len, clip_total)
    offset_in = slot_id - clip_id * clip_len
    frame_id = offset_in // frame_len
    place_in = offset_in - frame_id * frame_len - 2
    patch_id = jnp.maximum(place_in, 0)
    is_live = clip_id < clip_total
    is_patch = is_live & (place_in >= 0)
    frame_id = jnp.where(is_live, frame_id, 0)
    patch_row = jnp.where(is_patch, patch_id // grid_side, 0)
    column = jnp.where(is_patch, patch_id - patch_id // grid_side * grid_side, 0)
    first_key = clip_id * clip_len
    past_key = jnp.where(is_live, first_key + (frame_id + 1) * frame_len, length)
    segment = FRAMES * clip_id + frame_id
    starts = [n * frame_len for n in range(FRAMES * 2 + 1)]
    return (first_key, past_key, frame_id, patch_row, column, segment, starts)


def rotary_tables(frame_id, patch_row, column):
    segment = 2 * (HEAD_DIM // 3 // 2)
    half_width = segment // 2
    dim_index = jnp.arange(PAIR, dtype=jnp.int32) % HEAD_DIM
    segment_id = dim_index // segment
    exponent = (dim_index % segment % half_width).astype(jnp.float32)
    frequency = jnp.exp(exponent * (-math.log(10000.0) / half_width))
    pick = lambda number: wide(jnp.where(segment_id == number, 1.0, 0.0))[None, :]
    position = (
        pick(0) * wide(frame_id[:, None])
        + pick(1) * wide(patch_row[:, None])
        + pick(2) * wide(column[:, None])
    )
    angles = position * frequency[None, :]
    lower = (dim_index % segment < half_width)[None, :]
    sine = jnp.where((segment_id < 3)[None, :], jnp.sin(angles), 0.0)
    return (jnp.cos(angles), jnp.where(lower, -sine, 0.0), jnp.where(lower, 0.0, sine))


def spin(x, cos, up, down):
    turn = HEAD_DIM // 3 // 2
    return x * cos + pltpu.roll(x, PAIR - turn, 1) * up + pltpu.roll(x, turn, 1) * down


def standardize(values_in):
    row_mean = jnp.mean(values_in, -1, keepdims=True)
    centred = values_in - row_mean
    norm_scale = lax.rsqrt(jnp.mean(centred * centred, -1, keepdims=True) + EPSILON)
    return (centred * norm_scale, norm_scale)


def fold(x):
    return jnp.sum(x.reshape(x.shape[0] // 8, 8, x.shape[1]), 0)


def whole(array):
    return pl.BlockSpec(array.shape, lambda *_: (0,) * array.ndim, pipeline_mode=pl.Buffered(1))


def enter_kernel(side_ref, mine_ref, arrived_ref, gain_ref, shift_ref, stream_ref, out_ref):
    def step(rows):
        stream_ref[...] = rows
        normed, _ = standardize(wide(rows))
        out_ref[...] = low(normed * gain_ref[...] + shift_ref[...])

    @pl.when(pl.program_id(0) == 0)
    def _():
        step(mine_ref[0])

    @pl.when(pl.program_id(0) == 1)
    def _():
        step(arrived_ref[...])


def enter(side, tokens, arrived, gain, shift):
    _, half, depth = tokens.shape
    vector = pl.BlockSpec((1, depth), lambda i, side: (0, 0))
    out = pl.BlockSpec((half, depth), lambda i, side: (jnp.where(i == 0, side[0], 1 - side[0]), 0))
    return pl.pallas_call(
        enter_kernel,
        grid_spec=pltpu.PrefetchScalarGridSpec(
            num_scalar_prefetch=1,
            grid=(2,),
            in_specs=[
                pl.BlockSpec((1, half, depth), lambda i, side: (side[0], 0, 0)),
                pl.BlockSpec((half, depth), lambda i, side: (0, 0)),
                vector,
                vector,
            ],
            out_specs=[out, out],
        ),
        out_shape=[jax.ShapeDtypeStruct((2 * half, depth), jnp.bfloat16)] * 2,
        compiler_params=params(),
        cost_estimate=takes(5),
        name="enter",
    )(side, tokens, arrived, gain[None], shift[None])


def project_kernel(chunk, count, x_ref, *refs):
    weights, biases, outs = refs[:count], refs[count : 2 * count], refs[2 * count + 3]
    tables = refs[2 * count : 2 * count + 3]
    for at in range(0, x_ref.shape[0], chunk):
        rows = slice(at, at + chunk)
        cos, up, down = (table[rows, :] for table in tables)
        for number, (w_ref, b_ref) in enumerate(zip(weights, biases)):
            base, width = number * w_ref.shape[1], w_ref.shape[1] // 3
            y = dot(x_ref[rows, :], w_ref[...]) + b_ref[...]
            for lane in range(0, 2 * width, PAIR):
                turned = spin(y[:, lane : lane + PAIR], cos, up, down)
                outs[rows, base + lane : base + lane + PAIR] = low(turned)
            outs[rows, base + 2 * width : base + 3 * width] = low(y[:, 2 * width :])


def project(x, weights, biases, tables, block=640, chunk=320):
    rows, depth = x.shape
    width = weights[0].shape[1] * len(weights)
    biases = [bias[None] for bias in biases]
    row = lambda array: pl.BlockSpec((block, array.shape[1]), lambda i: (i, 0))
    return pl.pallas_call(
        functools.partial(project_kernel, chunk, len(weights)),
        grid=(rows // block,),
        in_specs=[row(x)] + [whole(a) for a in (*weights, *biases)] + [row(t) for t in tables],
        out_specs=pl.BlockSpec((block, width), lambda i: (i, 0)),
        out_shape=jax.ShapeDtypeStruct((rows, width), jnp.bfloat16),
        compiler_params=params(),
        cost_estimate=takes(9),
        name="project",
    )(x, *weights, *biases, *tables)


SEGMENTS = 5
BOUND_LANE = SEGMENTS


def segment_lanes(first_key, past_key, segment, starts):
    lane = jnp.arange(PAIR, dtype=jnp.int32)[None, :] % HEAD_DIM
    start = sum(jnp.where(lane == n, starts[n], 0) for n in range(SEGMENTS))
    inside = (start >= first_key[:, None]) & (start < past_key[:, None])
    for_query = jnp.where((lane < SEGMENTS) & ~inside, NEG, 0.0)
    for_key = jnp.where((lane == segment[:, None]) | (lane == BOUND_LANE), 1.0, 0.0)
    return low(for_query), low(for_key)


def own_lanes(head):
    lane = lax.broadcasted_iota(jnp.int32, (1, PAIR), 1)
    return (lane >= HEAD_DIM) == (head == 1), lane % HEAD_DIM


def attend_strips(shifted, v_ref, out_ref, root_ref, early_ref, late_ref):
    values = v_ref[...].T
    least = None
    for strip in STRIPS:
        first, past, stop = strip
        outs, roots = [], []
        for head in range(2):
            powers = jnp.exp2(shifted(head, strip))
            total = jnp.sum(powers, 0, keepdims=True)
            least = jnp.min(total) if least is None else jnp.minimum(least, jnp.min(total))
            root = 1.0 / total
            powers = low(powers)
            if past <= EARLY:
                early_ref[head, :, first:past] = powers
            else:
                late_ref[head, 0:stop, first - EARLY : past - EARLY] = powers
            rows = slice(head * HEAD_DIM, (head + 1) * HEAD_DIM)
            outs.append(dot(values[rows, 0:stop], powers) * root)
            roots.append(jnp.broadcast_to(root, (HEAD_DIM, past - first)))
        out_ref[first:past, :] = low(jnp.concatenate(outs, 0).T)
        root_ref[first:past, :] = jnp.concatenate(roots, 0).T
    return least


def attend_kernel(
    q_ref, k_ref, v_ref, query_ref, key_ref, lo_ref, hi_ref, out_ref, root_ref, early_ref, late_ref
):
    factor = HEAD_DIM**-0.5 * LOG2E
    squares = wide(k_ref[...]) * wide(k_ref[...])
    keys, longest = [], []
    for head in range(2):
        own, _ = own_lanes(head)
        keys.append(jnp.where(own, k_ref[...], key_ref[...]))
        length = jnp.sum(jnp.where(own, squares, 0.0), 1, keepdims=True)
        longest.append(jnp.max(length, 0, keepdims=True))

    def below_bound(head, strip):
        first, past, stop = strip
        own, lane = own_lanes(head)
        q = q_ref[first:past, :]
        length = jnp.sum(jnp.where(own, wide(q) * wide(q), 0.0), 1, keepdims=True)
        bound = jnp.sqrt(length * longest[head]) * 1.01
        beside = jnp.where(lane == BOUND_LANE, low(-bound), query_ref[first:past, :])
        return dot_nt(keys[head][0:stop], jnp.where(own, q, beside)) * factor

    outs = (v_ref, out_ref, root_ref, early_ref, late_ref)
    least = attend_strips(below_bound, *outs)

    @pl.when(jnp.logical_not(least > 1e-20))
    def _():
        def below_maximum(head, strip):
            first, past, stop = strip
            own, _ = own_lanes(head)
            q = q_ref[first:past, :]
            scores = dot_nt(k_ref[0:stop, :], jnp.where(own, q, jnp.zeros_like(q)))
            key = lax.broadcasted_iota(jnp.int32, scores.shape, 0)
            allowed = (key >= lo_ref[:, first:past]) & (key < hi_ref[:, first:past])
            scores = jnp.where(allowed, scores, NEG)
            return (scores - jnp.max(scores, 0, keepdims=True)) * factor

        attend_strips(below_maximum, *outs)


def kept_specs(rows, base):
    return [
        pl.BlockSpec((2, STRIPS[0][2], EARLY), lambda i: (base + i, 0, 0)),
        pl.BlockSpec((2, rows, rows - EARLY), lambda i: (base + i, 0, 0)),
    ]


QUARTER_PAIRS = 2


def head_specs(rows, base):
    pair = lambda i: (base + i) // QUARTER_PAIRS * 3 * QUARTER_PAIRS + (base + i) % QUARTER_PAIRS
    part = lambda number: pl.BlockSpec((rows, PAIR), lambda i: (0, pair(i) + number * QUARTER_PAIRS))
    return [part(0), part(1), part(2)], pl.BlockSpec((rows, PAIR), lambda i: (0, base + i))


def attend(heads, lanes, first_key, past_key):
    rows, width = heads.shape[0], heads.shape[1] // 3
    pairs = width // PAIR
    parts, block = head_specs(rows, 0)
    beside = (*lanes, first_key, past_key)
    return pl.pallas_call(
        attend_kernel,
        grid=(pairs,),
        in_specs=parts + [whole(array) for array in beside],
        out_specs=[block, block] + kept_specs(rows, 0),
        out_shape=[
            jax.ShapeDtypeStruct((rows, width), jnp.bfloat16),
            jax.ShapeDtypeStruct((rows, width), jnp.float32),
            jax.ShapeDtypeStruct((2 * pairs, STRIPS[0][2], EARLY), jnp.bfloat16),
            jax.ShapeDtypeStruct((2 * pairs, rows, rows - EARLY), jnp.bfloat16),
        ],
        compiler_params=params(),
        cost_estimate=takes(20),
        name="attend",
    )(heads, heads, heads, *beside)


def attend_back_kernel(
    q_ref, k_ref, v_ref, g_ref, o_ref, root_ref, early_ref, late_ref, cos_ref, up_ref, down_ref,
    out_ref, sums_ref, keys_acc, values_acc, queries_acc,
):
    pair = pl.program_id(0)
    pairs = out_ref.shape[1] // (3 * PAIR)
    scale = HEAD_DIM**-0.5
    keys = k_ref[...].T
    values = []
    for head in range(2):
        own, lane = own_lanes(head)
        values.append(jnp.where(own, v_ref[...], low(jnp.where(lane < 3, 1.0, 0.0))))
    for first, past, stop in STRIPS[::-1]:
        q = q_ref[first:past, :]
        g = wide(g_ref[first:past, :]) * root_ref[first:past, :]
        inner = g * wide(o_ref[first:past, :])
        g = low(g)
        zero = jnp.zeros_like(g)
        for head in range(2):
            own, lane = own_lanes(head)
            rows = slice(head * HEAD_DIM, (head + 1) * HEAD_DIM)
            shift = -jnp.sum(jnp.where(own, inner, 0.0), 1, keepdims=True)
            beside = zero
            for number in range(3):
                part = low(shift)
                shift = shift - wide(part)
                beside = jnp.where(lane == number, part, beside)
            if past <= EARLY:
                powers = early_ref[head, :, first:past]
            else:
                powers = late_ref[head, 0:stop, first - EARLY : past - EARLY]
            g_scores = low(wide(powers) * dot_nt(values[head][0:stop], jnp.where(own, g, beside)))
            queries_acc[rows, first:past] = dot(keys[rows, 0:stop], g_scores)
            g_keys = dot(g_scores, jnp.where(own, q, zero))
            g_values = dot(powers, jnp.where(own, g, zero))
            if head == 0:
                total_keys, total_values = g_keys, g_values
            else:
                total_keys, total_values = total_keys + g_keys, total_values + g_values
        if past == STRIPS[-1][1]:
            keys_acc[...] = total_keys
            values_acc[...] = total_values
        else:
            keys_acc[0:stop, :] += total_keys
            values_acc[0:stop, :] += total_values
    cos, up, down = cos_ref[...], -up_ref[...], -down_ref[...]
    grads = (
        low(spin(queries_acc[...].T * scale, cos, up, down)),
        low(spin(keys_acc[...] * scale, cos, up, down)),
        low(values_acc[...]),
    )
    for number, grad in enumerate(grads):
        lanes = pl.ds(pl.multiple_of((number * pairs + pair) * PAIR, PAIR), PAIR)
        out_ref[:, lanes] = grad
        sums_ref[:, lanes] = fold(wide(grad))


def attend_back(quarter, heads, g, out, root, early, late, tables):
    rows, width = g.shape
    pairs = width // PAIR
    parts, block = head_specs(rows, quarter * pairs)
    return pl.pallas_call(
        attend_back_kernel,
        grid=(pairs,),
        in_specs=parts
        + [pl.BlockSpec((rows, PAIR), lambda i: (0, i)), block, block]
        + kept_specs(rows, quarter * pairs)
        + [whole(table) for table in tables],
        out_specs=[
            pl.BlockSpec((rows, 3 * width), lambda i: (0, 0)),
            pl.BlockSpec((8, 3 * width), lambda i: (0, 0)),
        ],
        out_shape=[
            jax.ShapeDtypeStruct((rows, 3 * width), jnp.bfloat16),
            jax.ShapeDtypeStruct((8, 3 * width), jnp.float32),
        ],
        scratch_shapes=[
            pltpu.VMEM((rows, PAIR), jnp.float32),
            pltpu.VMEM((rows, PAIR), jnp.float32),
            pltpu.VMEM((PAIR, rows), jnp.float32),
        ],
        compiler_params=params(56),
        cost_estimate=takes(16),
        name="attend_back",
    )(heads, heads, heads, g, out, root, early, late, *tables)


def merge_kernel(count, *refs):
    rights, lefts = refs[: 2 * count], refs[2 * count : 3 * count]
    x_ref, bias_ref, gain_ref, shift_ref, residual_ref, out_ref = refs[3 * count :]
    total = wide(x_ref[...]) + bias_ref[...]
    for number, right in enumerate(rights):
        left, width = lefts[number // 2], right.shape[0]
        total = total + dot(left[:, number % 2 * width : (number % 2 + 1) * width], right[...])
    residual_ref[...] = total
    normed, _ = standardize(total)
    out_ref[...] = low(normed * gain_ref[...] + shift_ref[...])


def merge(lefts, rights, x, bias, gain, shift, block=320):
    rows, depth = x.shape
    row = lambda array: pl.BlockSpec((block, array.shape[1]), lambda i: (i, 0))
    vectors = (bias[None], gain[None], shift[None])
    return pl.pallas_call(
        functools.partial(merge_kernel, len(lefts)),
        grid=(rows // block,),
        in_specs=[whole(w) for w in rights]
        + [row(a) for a in lefts]
        + [row(x)]
        + [whole(v) for v in vectors],
        out_specs=[row(x), row(x)],
        out_shape=[
            jax.ShapeDtypeStruct((rows, depth), jnp.float32),
            jax.ShapeDtypeStruct((rows, depth), jnp.bfloat16),
        ],
        compiler_params=params(),
        cost_estimate=takes(8),
        name="merge",
    )(*rights, *lefts, x, *vectors)


def expand_kernel(chunk, x_ref, w_ref, b_ref, active_ref, slope_ref):
    for at in range(0, x_ref.shape[0], chunk):
        rows = slice(at, at + chunk)
        v = dot(x_ref[rows, :], w_ref[...]) + b_ref[...]
        below = 0.5 + 0.5 * lax.erf(v * ROOT_HALF)
        active_ref[rows, :] = low(v * below)
        slope_ref[rows, :] = low(below + v * jnp.exp(-0.5 * v * v) * GAUSS_NORM)


def expand(x, weight, bias, block=512, chunk=256):
    rows, depth = x.shape
    width = weight.shape[1]
    out = pl.BlockSpec((rows, block), lambda i: (0, i))
    return pl.pallas_call(
        functools.partial(expand_kernel, chunk),
        grid=(width // block,),
        in_specs=[
            whole(x),
            pl.BlockSpec((depth, block), lambda i: (0, i)),
            pl.BlockSpec((1, block), lambda i: (0, i)),
        ],
        out_specs=[out, out],
        out_shape=[jax.ShapeDtypeStruct((rows, width), jnp.bfloat16)] * 2,
        compiler_params=params(),
        cost_estimate=takes(8.5),
        name="expand",
    )(x, weight, bias[None])


def reduce_kernel(count, half, side_ref, *refs):
    rights, lefts = refs[:count], refs[count : 2 * count]
    x_ref, bias_ref, send_ref, keep_ref = refs[2 * count :]
    total = x_ref[...] + bias_ref[...]
    for left, right in zip(lefts, rights):
        total = total + dot(left[...], right[...])

    @pl.when(pl.program_id(0) < half)
    def _():
        send_ref[...] = low(total)

    @pl.when(pl.program_id(0) >= half)
    def _():
        keep_ref[...] = low(total)


def reduce_rows(side, lefts, rights, x, bias, block=320):
    rows, depth = x.shape
    half = rows // 2 // block
    at = lambda i, side: jnp.where(i < half, (1 - side[0]) * half + i, side[0] * half + i - half)
    row = lambda array: pl.BlockSpec((block, array.shape[1]), lambda i, side: (at(i, side), 0))
    return pl.pallas_call(
        functools.partial(reduce_kernel, len(lefts), half),
        grid_spec=pltpu.PrefetchScalarGridSpec(
            num_scalar_prefetch=1,
            grid=(2 * half,),
            in_specs=[whole(w) for w in rights]
            + [row(a) for a in lefts]
            + [row(x), whole(bias[None])],
            out_specs=[
                pl.BlockSpec((block, depth), lambda i, side: (jnp.minimum(i, half - 1), 0)),
                pl.BlockSpec((block, depth), lambda i, side: (jnp.maximum(i - half, 0), 0)),
            ],
        ),
        out_shape=[jax.ShapeDtypeStruct((rows // 2, depth), jnp.bfloat16)] * 2,
        compiler_params=params(),
        cost_estimate=takes(0.1),
        name="reduce_rows",
    )(side, *rights, *lefts, x, bias[None])


def back_kernel(count, at_ref, *refs):
    rights, lefts = refs[:count], refs[count : 2 * count]
    base_ref, above_ref, gain_ref, out_ref, sums_ref = refs[2 * count :]

    @pl.when(pl.program_id(0) == 0)
    def _():
        sums_ref[...] = jnp.zeros_like(sums_ref)

    g = dot_nt(lefts[0][...], rights[0][...])
    for left, right in zip(lefts[1:], rights[1:]):
        g = g + dot_nt(left[...], right[...])
    normed, scale = standardize(wide(base_ref[...]))
    u = g * gain_ref[...]
    above = wide(above_ref[...])
    inner = jnp.mean(u, -1, keepdims=True) + normed * jnp.mean(u * normed, -1, keepdims=True)
    out = low(above + scale * (u - inner))
    out_ref[...] = out
    sums_ref[0] += fold(g * normed)
    sums_ref[1] += fold(g)
    sums_ref[2] += fold(wide(out))
    sums_ref[3] += fold(above)


def back_norm(at, rows, lefts, rights, base, above, gain, block=320):
    depth = base.shape[1]
    row = lambda array: pl.BlockSpec((block, array.shape[1]), lambda i, at: (at[0] + i, 0))
    return pl.pallas_call(
        functools.partial(back_kernel, len(lefts)),
        grid_spec=pltpu.PrefetchScalarGridSpec(
            num_scalar_prefetch=1,
            grid=(rows // block,),
            in_specs=[whole(w) for w in rights]
            + [row(a) for a in lefts]
            + [row(base), row(above), whole(gain[None])],
            out_specs=[
                pl.BlockSpec((block, depth), lambda i, at: (i, 0)),
                pl.BlockSpec((4, 8, depth), lambda i, at: (0, 0, 0)),
            ],
        ),
        out_shape=[
            jax.ShapeDtypeStruct((rows, depth), jnp.bfloat16),
            jax.ShapeDtypeStruct((4, 8, depth), jnp.float32),
        ],
        compiler_params=params(),
        cost_estimate=takes(0.1 if rows == base.shape[0] else 10),
        name="back_norm",
    )(at, *rights, *lefts, base, above, gain[None])


def place_kernel(steps, flag_ref, mine_ref, theirs_ref, out_ref):
    @pl.when(pl.program_id(0) < steps)
    def _():
        out_ref[...] = mine_ref[...].astype(out_ref.dtype).reshape(out_ref.shape)

    @pl.when(pl.program_id(0) >= steps)
    def _():
        out_ref[...] = theirs_ref[...].astype(out_ref.dtype).reshape(out_ref.shape)


def place(flag, mine, theirs, steps, in_block, in_index, out_shape, out_block, out_index, dtype):
    def target(i, flag):
        return out_index(jnp.where(i < steps, flag[0], 1 - flag[0]), jnp.where(i < steps, i, i - steps))

    return pl.pallas_call(
        functools.partial(place_kernel, steps),
        grid_spec=pltpu.PrefetchScalarGridSpec(
            num_scalar_prefetch=1,
            grid=(2 * steps,),
            in_specs=[
                pl.BlockSpec(in_block, lambda i, flag: in_index(jnp.minimum(i, steps - 1))),
                pl.BlockSpec(in_block, lambda i, flag: in_index(jnp.maximum(i - steps, 0))),
            ],
            out_specs=pl.BlockSpec(out_block, target),
        ),
        out_shape=jax.ShapeDtypeStruct(out_shape, dtype),
        compiler_params=params(),
        cost_estimate=takes(4),
        name="place",
    )(flag, mine, theirs)


def place_rows(flag, mine, theirs, steps, dtype):
    rows, width = mine.shape
    block = (rows // steps, width)
    return place(
        flag, mine, theirs, steps, block, lambda j: (j, 0),
        (2 * rows, width), block, lambda half, j: (half * steps + j, 0), dtype,
    )


def place_columns(flag, mine, theirs, steps, dtype):
    rows, width = mine.shape
    block = (rows // steps, width)
    return place(
        flag, mine, theirs, steps, block, lambda j: (j, 0),
        (rows, 2 * width), block, lambda half, j: (j, half), dtype,
    )


def place_heads(flag, mine, theirs, dtype):
    rows, width = mine.shape[0], mine.shape[1] // 3
    return place(
        flag, mine, theirs, 3, (rows, width), lambda j: (0, j),
        (3, rows, 2 * width), (1, rows, width), lambda half, j: (j, 0, half), dtype,
    )


def column_sums(matrix):
    unit_column = jnp.ones((matrix.shape[0],), matrix.dtype)
    return jnp.dot(unit_column, matrix, preferred_element_type=jnp.float32)


KEEP, SEND = 0, 1
OWN, FAR = 0, 1
QUARTERS = ((FAR, SEND), (FAR, KEEP), (OWN, SEND), (OWN, KEEP))


def on_device(
    spread,
    tokens,
    cotangent,
    patch_count,
    first_gain,
    first_shift,
    heads_weight,
    heads_bias,
    merge_weight,
    merge_bias,
    second_gain,
    second_shift,
    expand_weight,
    expand_bias,
    reduce_weight,
    reduce_bias,
):
    levels = spread.bit_length() - 1
    rest = list(range(1, levels))
    chunks = spread // 2
    location = lax.axis_index("dp")
    side = lax.axis_index("mp")
    sides = side[None].astype(jnp.int32)
    previous = []

    def bit(level):
        return (location >> level) & 1

    core = bit(0)[None].astype(jnp.int32)

    def tie(array, *others):
        return lax.optimization_barrier((array,) + others)[0] if others else array

    def after(array):
        return tie(array, *previous)

    def did(*arrays):
        previous[:] = arrays
        return arrays[0] if len(arrays) == 1 else arrays

    def swap(array, level):
        return lax.ppermute(array, "dp", [(i, i ^ (1 << level)) for i in range(spread)])

    def cross(array):
        return lax.ppermute(array, "mp", [(0, 1), (1, 0)])

    def half_of(array, flag, axis=0):
        size = array.shape[axis] // 2
        return lax.dynamic_slice_in_dim(array, flag * size, size, axis)

    def chunk_of(array):
        size = array.shape[0] // chunks
        return lax.dynamic_slice_in_dim(array, (location >> 1) * size, size, 0)

    def split(array, level, open_levels=None):
        left = 1 << sum(other > level for other in (open_levels or rest))
        four = array.reshape(left, 2, -1, array.shape[1])
        part = lambda flag: lax.dynamic_index_in_dim(four, flag, 1, False).reshape(-1, array.shape[1])
        return part(bit(level)), part(1 - bit(level))

    def join(mine, theirs, level, open_levels=None):
        left = 1 << sum(other > level for other in (open_levels or rest))
        four = lambda array: array.reshape(left, 1, -1, array.shape[1])
        pair = jnp.where(
            bit(level) == 0,
            jnp.concatenate([four(mine), four(theirs)], 1),
            jnp.concatenate([four(theirs), four(mine)], 1),
        )
        return pair.reshape(-1, mine.shape[1])

    def quarters_of(own, axis):
        return [half_of(own, bit(0), axis), half_of(own, 1 - bit(0), axis)]

    tokens, cotangent = tokens[:, 0], cotangent[:, 0]
    tokens_far = cross(lax.dynamic_index_in_dim(tokens, 1 - side, 0, False))
    heads_three = heads_weight.transpose(1, 0, 2)
    heads_own = [
        jnp.concatenate([half_of(heads_three[n], flag, 1) for n in range(3)], 1)
        for flag in (bit(0), 1 - bit(0))
    ]
    merge_own = quarters_of(merge_weight, 0)
    expand_own = quarters_of(expand_weight, 1)
    reduce_own = quarters_of(reduce_weight, 0)
    pack = lambda hb, eb: jnp.concatenate([hb.reshape(-1), eb])
    bias_own = [
        pack(half_of(heads_bias, flag, 1), half_of(expand_bias, flag)) for flag in (bit(0), 1 - bit(0))
    ]
    three = heads_bias.size // 2
    near = rest[:2]
    heads_piece = heads_own[KEEP]
    for n, level in enumerate(near):
        heads_piece = split(heads_piece, level, near[n:])[0]
    up_piece = jnp.concatenate([chunk_of(expand_own[KEEP]), chunk_of(merge_own[KEEP])])
    down_piece = chunk_of(reduce_own[KEEP])

    count_one = lax.dynamic_index_in_dim(patch_count[:, 0], side, 0, False)
    length = 2 * tokens.shape[1]
    first_key, past_key, frame_id, patch_row, column, segment, starts = slot_layout(count_one, length)
    tables = rotary_tables(frame_id, patch_row, column)
    lanes = segment_lanes(first_key, past_key, segment, starts)
    first_key, past_key = first_key[None], past_key[None]

    did(heads_piece, up_piece, down_piece, *heads_own, *merge_own, *expand_own, *reduce_own, *tables, *lanes)
    heads_piece = cross(tie(heads_piece, tokens_far))
    up_piece = cross(tie(up_piece, tokens_far))
    bias_both = cross(tie(jnp.concatenate(bias_own), tokens_far))
    bias_far = [bias_both[: bias_both.size // 2], bias_both[bias_both.size // 2 :]]
    stream, first_out = did(*enter(sides, after(tokens), tokens_far, first_gain, first_shift))
    heads, seen = {}, {}
    heads_all = [heads_own, None]
    bias_all = (bias_own, bias_far)

    def look(p):
        biases = [bias[:three] for bias in bias_all[p]]
        heads[p] = did(project(after(first_out), heads_all[p], biases, tables))

    def attention(p):
        seen[p] = did(*attend(after(heads[p]), lanes, first_key, past_key))

    def gathered(array, *splits):
        array = lax.all_gather(array, "dp", axis=0, tiled=True)
        array = array.reshape(chunks, 2, -1, array.shape[1])
        quarters, at = [], 0
        for size in splits:
            part = array[:, :, at : at + size]
            quarters.append(
                [
                    lax.dynamic_index_in_dim(part, flag, 1, False).reshape(-1, array.shape[3])
                    for flag in (bit(0), 1 - bit(0))
                ]
            )
            at += size
        return quarters

    look(OWN)
    heads_piece = did(after(heads_piece))
    if len(near) > 1:
        heads_next = swap(heads_piece, near[1])
    up_sizes = (expand_own[0].shape[0] // chunks, merge_own[0].shape[0] // chunks)
    up_gathered = gathered(after(up_piece), *up_sizes)
    down_piece = cross(after(down_piece))
    if len(near) > 1:
        heads_piece = did(join(after(heads_piece), heads_next, near[1], near[1:]))
    heads_next = swap(heads_piece, near[0])
    attention(OWN)
    heads_piece = did(join(after(heads_piece), heads_next, near[0], near))
    heads_all[FAR] = [heads_piece, swap(heads_piece, 0)]
    cotangent_far = cross(after(lax.dynamic_index_in_dim(cotangent, 1 - side, 0, False)))
    (reduce_far,) = gathered(after(down_piece), down_piece.shape[0])
    look(FAR)
    attention(FAR)
    expand_far, merge_far = ([after(q) for q in quarters] for quarters in up_gathered)
    merge_all = (merge_own, merge_far)
    expand_all = (expand_own, expand_far)
    reduce_all = (reduce_own, reduce_far)
    width = seen[OWN][0].shape[1] // 2
    mixed = {(p, c): seen[p][0][:, c * width : (c + 1) * width] for p, c in QUARTERS}
    residual, second_out = did(
        *merge(
            [seen[OWN][0], seen[FAR][0]], [merge_all[p][c] for p in (OWN, FAR) for c in (KEEP, SEND)],
            after(stream), merge_bias, second_gain, second_shift,
        )
    )
    cotangent_far = after(cotangent_far)
    grad_two = jnp.where(
        side == 0,
        jnp.concatenate([cotangent[0], cotangent_far]),
        jnp.concatenate([cotangent_far, cotangent[1]]),
    )

    active, slope, grad_pre = {}, {}, {}

    def widen(p, c):
        active[p, c], slope[p, c] = did(
            *expand(after(second_out), expand_all[p][c], bias_all[p][c][three:])
        )

    def back_active(p, c):
        grad_pre[p, c] = did(low(dot_nt(after(grad_two), reduce_all[p][c]) * wide(slope[p, c])))

    def product(left, right, *arrived):
        total = dot_tn(after(left), right)
        for array in arrived:
            total = total + wide(array)
        return did(low(total))

    def scattered(array, level, open_levels=None):
        keep, send = split(after(array), level, open_levels or rest[rest.index(level) :])
        did(send)
        return keep, swap(send, level)

    def summed(keep, arrived):
        return did(low(wide(after(keep)) + wide(arrived)))

    def rows_out(keep, arrived, dtype):
        return place_rows(sides, keep, arrived, 1, dtype).reshape(2, 1, length // 2, -1)

    widen(FAR, SEND)
    widen(FAR, KEEP)
    sent = swap(product(active[FAR, SEND], grad_two), 0)
    widen(OWN, SEND)
    reduce_far_sum = product(active[FAR, KEEP], grad_two, sent)
    reduce_cross = cross(reduce_far_sum)
    widen(OWN, KEEP)
    sent = swap(product(active[OWN, SEND], grad_two), 0)
    back_active(FAR, SEND)
    reduce_sum = product(active[OWN, KEEP], grad_two, sent)
    back_active(FAR, KEEP)
    sent = swap(product(second_out, grad_pre[FAR, SEND]), 0)
    layer_send, layer_keep = did(
        *reduce_rows(
            sides, [active[q] for q in QUARTERS], [reduce_all[p][c] for p, c in QUARTERS],
            after(residual), reduce_bias,
        )
    )
    back_active(OWN, SEND)
    expand_far_sum = product(second_out, grad_pre[FAR, KEEP], sent)
    back_active(OWN, KEEP)
    sent = swap(product(second_out, grad_pre[OWN, SEND]), 0)
    reduce_sum = summed(reduce_sum, reduce_cross)
    expand_cross = cross(tie(expand_far_sum, reduce_cross))
    reduce_keep, reduce_next = scattered(reduce_sum, rest[0])
    expand_sum = product(second_out, grad_pre[OWN, KEEP], sent)
    zero = jnp.zeros((1,), jnp.int32)
    grad_one, second_sums = did(
        *back_norm(
            zero, length, [grad_pre[q] for q in QUARTERS], [expand_all[p][c] for p, c in QUARTERS],
            after(residual), grad_two, second_gain,
        )
    )
    reduce_sum = summed(reduce_keep, reduce_next)
    reduce_keep, reduce_next = scattered(reduce_sum, rest[1])

    grad_mixed, grad_heads, head_sums = {}, {}, {}

    def back_mixed(p, c):
        grad_mixed[p, c] = did(low(dot_nt(after(grad_one), merge_all[p][c])))

    def back_attention(q):
        p, c = q
        grad_heads[q], sums = did(
            *attend_back(c, heads[p], after(grad_mixed[q]), *seen[p], tables)
        )
        head_sums[q] = jnp.sum(sums, 0)

    sent_far = swap(product(mixed[FAR, SEND], grad_one), 0)
    sent_own = swap(product(mixed[OWN, SEND], grad_one), 0)
    for p, c in QUARTERS:
        back_mixed(p, c)
    merge_far_sum = product(mixed[FAR, KEEP], grad_one, sent_far)
    merge_sum = product(mixed[OWN, KEEP], grad_one, sent_own)
    expand_sum = summed(expand_sum, expand_cross)
    merge_cross = cross(tie(merge_far_sum, expand_cross))
    layer_far = cross(tie(layer_send, expand_cross))
    expand_keep, expand_next = scattered(expand_sum, rest[0])
    reduce_sum = summed(reduce_keep, reduce_next)
    for level in rest[2:]:
        reduce_keep, reduce_next = scattered(reduce_sum, level)
        reduce_sum = low(wide(reduce_keep) + wide(reduce_next))
    back_attention((FAR, SEND))
    reduce_total = lax.all_gather(after(reduce_sum), "dp", axis=0, tiled=True)
    expand_sum = summed(expand_keep, expand_next)
    expand_keep, expand_next = scattered(expand_sum, rest[1])
    sent = swap(product(first_out, grad_heads[FAR, SEND]), 0)
    merge_sum = summed(merge_sum, merge_cross)
    merge_keep, merge_next = scattered(merge_sum, rest[0])
    back_attention((FAR, KEEP))
    heads_far_sum = product(first_out, grad_heads[FAR, KEEP], sent)
    heads_cross = cross(heads_far_sum)
    expand_sum = summed(expand_keep, expand_next)
    merge_sum = summed(merge_keep, merge_next)
    merge_keep, merge_next = scattered(merge_sum, rest[1])
    for level in rest[2:]:
        expand_keep, expand_next = scattered(expand_sum, level)
        expand_sum = low(wide(expand_keep) + wide(expand_next))
    back_attention((OWN, SEND))
    merge_sum = summed(merge_keep, merge_next)
    layer_out = rows_out(after(layer_keep), layer_far, jnp.bfloat16)
    merge_sum, layer_out = lax.optimization_barrier((merge_sum, layer_out))
    for level in rest[2:]:
        merge_keep, merge_next = scattered(merge_sum, level)
        merge_sum = low(wide(merge_keep) + wide(merge_next))
    sent = swap(product(first_out, grad_heads[OWN, SEND]), 0)
    back_attention((OWN, KEEP))
    expand_total = lax.all_gather(
        after(jnp.concatenate([expand_sum, merge_sum])), "dp", axis=0, tiled=True
    )
    heads_sum = product(first_out, grad_heads[OWN, KEEP], sent, heads_cross)
    orders = [rest, rest[1:2] + rest[:1] + rest[2:]]
    middle = heads_sum.shape[1] // 2
    heads_sums = [heads_sum[:, :middle], heads_sum[:, middle:]]

    def both_scattered(n):
        return [scattered(total, order[n], order[n:]) for total, order in zip(heads_sums, orders)]

    def both_summed(pairs):
        return [summed(*pair) for pair in pairs]

    def in_rows(array):
        return wide(array.transpose(1, 0, 2, 3).reshape(-1, array.shape[3]))

    reduce_total = reduce_total.reshape(chunks, 2, -1, reduce_total.shape[1])
    expand_total = expand_total.reshape(chunks, 2, -1, expand_total.shape[1])
    rows = expand_sum.shape[0]

    pairs = both_scattered(0)
    lefts = [grad_heads[q] for q in QUARTERS]
    rights = [heads_all[p][c] for p, c in QUARTERS]
    per_half = length // 2 // 320
    tokens_send, sums_a = did(
        *back_norm(
            (1 - sides) * per_half, length // 2, lefts, rights, stream, grad_one, after(first_gain)
        )
    )
    tokens_cross = cross(tokens_send)
    heads_sums = both_summed(pairs)
    pairs = both_scattered(1)
    tokens_keep, sums_b = did(
        *back_norm(sides * per_half, length // 2, lefts, rights, stream, grad_one, after(first_gain))
    )
    first_sums = sums_a + sums_b

    small = {q: jnp.concatenate([head_sums[q], column_sums(grad_pre[q])]) for q in QUARTERS}
    both = jnp.concatenate(
        [
            jnp.sum(part, 0)
            for part in (
                first_sums[0], first_sums[1], second_sums[0], second_sums[1], second_sums[2], second_sums[3],
            )
        ]
    )
    far_send, own_send, both = did(*(after(v) for v in (small[FAR, SEND], small[OWN, SEND], both)))
    arrived = swap(jnp.concatenate([far_send, own_send, both]), 0)
    size = own_send.size
    heads_sums = both_summed(pairs)
    mine = jnp.concatenate([small[FAR, KEEP] + arrived[:size], small[OWN, KEEP], both])
    mine = did(
        jnp.concatenate([mine[:size], mine[size:] + after(arrived)[size:]])
    )
    for n in range(2, len(rest)):
        pairs = both_scattered(n)
        small_next = swap(mine, rest[n])
        if n == 2:
            reduce_out = in_rows(after(reduce_total))
            mine, reduce_out = lax.optimization_barrier((mine, reduce_out))
            did(mine)
        heads_sums = both_summed(pairs)
        mine = did(mine + after(small_next))
    for n in range(len(rest))[::-1]:
        arrived = [swap(total, order[n]) for total, order in zip(heads_sums, orders)]
        small_next = swap(mine, rest[n]) if n < 2 else None
        if n == len(rest) - 1:
            expand_out = wide(
                jnp.concatenate(
                    [
                        after(expand_total)[:, n, :rows].reshape(-1, expand_total.shape[3])
                        for n in range(2)
                    ],
                    1,
                )
            )
            mine, expand_out = lax.optimization_barrier((mine, expand_out))
            did(mine)
        if n == 0:
            tokens_out = rows_out(after(tokens_keep), tokens_cross, jnp.float32)
            mine, tokens_out = lax.optimization_barrier((mine, tokens_out))
            did(mine)
        heads_sums = [
            did(join(after(total), other, order[n], order[n:]))
            for total, other, order in zip(heads_sums, arrived, orders)
        ]
        if n < 2:
            mine = did(mine + after(small_next))
    heads_sum = jnp.concatenate(heads_sums, 1)
    heads_next = swap(heads_sum, 0)
    arrived = cross(jnp.concatenate([mine[:size], mine[2 * size :]]))
    both = mine[2 * size :] + arrived[size:]
    mine = mine[size : 2 * size] + arrived[:size]
    theirs = swap(mine, 0)
    first = jnp.where(bit(0) == 0, mine, theirs)
    second = jnp.where(bit(0) == 0, theirs, mine)
    heads_bias_total = jnp.concatenate([first[:three].reshape(3, -1), second[:three].reshape(3, -1)], 1)
    expand_bias_total = jnp.concatenate([first[three:], second[three:]])
    (first_gain_total, first_shift_total, second_gain_total, second_shift_total, merge_bias_total,
     reduce_bias_total) = both.reshape(6, -1)
    heads_out = place_heads(core, heads_sum, heads_next, jnp.float32)
    return (
        layer_out,
        tokens_out,
        first_gain_total,
        first_shift_total,
        heads_out.transpose(1, 0, 2),
        heads_bias_total,
        in_rows(expand_total[:, :, rows:]),
        merge_bias_total,
        second_gain_total,
        second_shift_total,
        expand_out,
        expand_bias_total,
        reduce_out,
        reduce_bias_total,
    )


def solution(mesh):
    rows = P(None, "dp", "mp", None)
    columns = P(None, "mp")
    heads = P(None, None, "mp")
    return jax.shard_map(
        functools.partial(on_device, mesh.shape["dp"]),
        mesh=mesh,
        in_specs=(
            rows, rows, P(None, "dp"), P(), P(), heads, columns, P("mp", None), P(), P(), P(), columns,
            P("mp"), P("mp", None), P(),
        ),
        out_specs=(
            rows, rows, P(), P(), heads, columns, P("mp", None), P(), P(), P(), columns, P("mp"),
            P("mp", None), P(),
        ),
        check_vma=False,
    )
```

```python
import functools
import math

import jax
import jax.numpy as jnp
from jax import lax
from jax.experimental import pallas as pl
from jax.experimental.pallas import tpu as pltpu
from jax.sharding import PartitionSpec as P

HEAD_DIM = 64
FRAMES = 2
SIDE_SMALL = 16
SIDE_LARGE = 24
EPSILON = 1e-06
ROOT_HALF = 0.7071067811865476
GAUSS_NORM = 0.3989422804014327
LOG2E = math.log2(math.e)
PAIR = 128
NEG = -1e30
STRIPS = ((0, 512, 592), (512, 1024, 1168), (1024, 1280, 1280))
EARLY = 512


def params(mib=50):
    return pltpu.CompilerParams(vmem_limit_bytes=mib * 2**20)


def takes(microseconds):
    return pl.CostEstimate(
        flops=int(microseconds * 4e9), bytes_accessed=int(microseconds * 4e6), transcendentals=0
    )


def low(array):
    return array.astype(jnp.bfloat16)


def wide(array):
    return array.astype(jnp.float32)


def dot(left, right):
    return jnp.dot(left, right, preferred_element_type=jnp.float32)


def dot_nt(left, right):
    return lax.dot_general(
        left, right, (((1,), (1,)), ((), ())), preferred_element_type=jnp.float32
    )


def dot_tn(left, right):
    return lax.dot_general(
        left, right, (((0,), (0,)), ((), ())), preferred_element_type=jnp.float32
    )


def slot_layout(count_one, length):
    large_count = SIDE_LARGE * SIDE_LARGE
    grid_side = jnp.where(count_one == large_count, SIDE_LARGE, SIDE_SMALL).astype(jnp.int32)
    frame_len = grid_side * grid_side + 2
    clip_len = FRAMES * frame_len
    clip_total = jnp.where(count_one == large_count, 1, 2).astype(jnp.int32)
    slot_id = jnp.arange(length, dtype=jnp.int32)
    clip_id = jnp.minimum(slot_id // clip_len, clip_total)
    offset_in = slot_id - clip_id * clip_len
    frame_id = offset_in // frame_len
    place_in = offset_in - frame_id * frame_len - 2
    patch_id = jnp.maximum(place_in, 0)
    is_live = clip_id < clip_total
    is_patch = is_live & (place_in >= 0)
    frame_id = jnp.where(is_live, frame_id, 0)
    patch_row = jnp.where(is_patch, patch_id // grid_side, 0)
    column = jnp.where(is_patch, patch_id - patch_id // grid_side * grid_side, 0)
    first_key = clip_id * clip_len
    past_key = jnp.where(is_live, first_key + (frame_id + 1) * frame_len, length)
    segment = FRAMES * clip_id + frame_id
    starts = [n * frame_len for n in range(FRAMES * 2 + 1)]
    return (first_key, past_key, frame_id, patch_row, column, segment, starts)


def rotary_tables(frame_id, patch_row, column):
    segment = 2 * (HEAD_DIM // 3 // 2)
    half_width = segment // 2
    dim_index = jnp.arange(PAIR, dtype=jnp.int32) % HEAD_DIM
    segment_id = dim_index // segment
    exponent = (dim_index % segment % half_width).astype(jnp.float32)
    frequency = jnp.exp(exponent * (-math.log(10000.0) / half_width))
    pick = lambda number: wide(jnp.where(segment_id == number, 1.0, 0.0))[None, :]
    position = (
        pick(0) * wide(frame_id[:, None])
        + pick(1) * wide(patch_row[:, None])
        + pick(2) * wide(column[:, None])
    )
    angles = position * frequency[None, :]
    lower = (dim_index % segment < half_width)[None, :]
    sine = jnp.where((segment_id < 3)[None, :], jnp.sin(angles), 0.0)
    return (jnp.cos(angles), jnp.where(lower, -sine, 0.0), jnp.where(lower, 0.0, sine))


def spin(x, cos, up, down):
    turn = HEAD_DIM // 3 // 2
    return x * cos + pltpu.roll(x, PAIR - turn, 1) * up + pltpu.roll(x, turn, 1) * down


def standardize(values_in):
    row_mean = jnp.mean(values_in, -1, keepdims=True)
    centred = values_in - row_mean
    norm_scale = lax.rsqrt(jnp.mean(centred * centred, -1, keepdims=True) + EPSILON)
    return (centred * norm_scale, norm_scale)


def fold(x):
    return jnp.sum(x.reshape(x.shape[0] // 8, 8, x.shape[1]), 0)


def whole(array):
    return pl.BlockSpec(array.shape, lambda *_: (0,) * array.ndim, pipeline_mode=pl.Buffered(1))


def enter_kernel(side_ref, mine_ref, arrived_ref, gain_ref, shift_ref, stream_ref, out_ref):
    def step(rows):
        stream_ref[...] = rows
        normed, _ = standardize(wide(rows))
        out_ref[...] = low(normed * gain_ref[...] + shift_ref[...])

    @pl.when(pl.program_id(0) == 0)
    def _():
        step(mine_ref[0])

    @pl.when(pl.program_id(0) == 1)
    def _():
        step(arrived_ref[...])


def enter(side, tokens, arrived, gain, shift):
    _, half, depth = tokens.shape
    vector = pl.BlockSpec((1, depth), lambda i, side: (0, 0))
    out = pl.BlockSpec((half, depth), lambda i, side: (jnp.where(i == 0, side[0], 1 - side[0]), 0))
    return pl.pallas_call(
        enter_kernel,
        grid_spec=pltpu.PrefetchScalarGridSpec(
            num_scalar_prefetch=1,
            grid=(2,),
            in_specs=[
                pl.BlockSpec((1, half, depth), lambda i, side: (side[0], 0, 0)),
                pl.BlockSpec((half, depth), lambda i, side: (0, 0)),
                vector,
                vector,
            ],
            out_specs=[out, out],
        ),
        out_shape=[jax.ShapeDtypeStruct((2 * half, depth), jnp.bfloat16)] * 2,
        compiler_params=params(),
        cost_estimate=takes(5),
        name="enter",
    )(side, tokens, arrived, gain[None], shift[None])


def collect_kernel(side_ref, mine_ref, arrived_ref, out_ref):
    @pl.when(pl.program_id(0) == 0)
    def _():
        out_ref[...] = mine_ref[0]

    @pl.when(pl.program_id(0) == 1)
    def _():
        out_ref[...] = arrived_ref[...]


def collect(side, array, arrived):
    _, half, depth = array.shape
    return pl.pallas_call(
        collect_kernel,
        grid_spec=pltpu.PrefetchScalarGridSpec(
            num_scalar_prefetch=1,
            grid=(2,),
            in_specs=[
                pl.BlockSpec((1, half, depth), lambda i, side: (side[0], 0, 0)),
                pl.BlockSpec((half, depth), lambda i, side: (0, 0)),
            ],
            out_specs=pl.BlockSpec(
                (half, depth), lambda i, side: (jnp.where(i == 0, side[0], 1 - side[0]), 0)
            ),
        ),
        out_shape=jax.ShapeDtypeStruct((2 * half, depth), array.dtype),
        compiler_params=params(),
        cost_estimate=takes(2),
        name="collect",
    )(side, array, arrived)


def project_kernel(chunk, count, x_ref, *refs):
    weights, biases, outs = refs[:count], refs[count : 2 * count], refs[2 * count + 3]
    tables = refs[2 * count : 2 * count + 3]
    for at in range(0, x_ref.shape[0], chunk):
        rows = slice(at, at + chunk)
        cos, up, down = (table[rows, :] for table in tables)
        for number, (w_ref, b_ref) in enumerate(zip(weights, biases)):
            base, width = number * w_ref.shape[1], w_ref.shape[1] // 3
            y = dot(x_ref[rows, :], w_ref[...]) + b_ref[...]
            for lane in range(0, 2 * width, PAIR):
                turned = spin(y[:, lane : lane + PAIR], cos, up, down)
                outs[rows, base + lane : base + lane + PAIR] = low(turned)
            outs[rows, base + 2 * width : base + 3 * width] = low(y[:, 2 * width :])


def project(x, weights, biases, tables, block=640, chunk=320):
    rows, depth = x.shape
    width = weights[0].shape[1] * len(weights)
    biases = [bias[None] for bias in biases]
    row = lambda array: pl.BlockSpec((block, array.shape[1]), lambda i: (i, 0))
    return pl.pallas_call(
        functools.partial(project_kernel, chunk, len(weights)),
        grid=(rows // block,),
        in_specs=[row(x)] + [whole(a) for a in (*weights, *biases)] + [row(t) for t in tables],
        out_specs=pl.BlockSpec((block, width), lambda i: (i, 0)),
        out_shape=jax.ShapeDtypeStruct((rows, width), jnp.bfloat16),
        compiler_params=params(),
        cost_estimate=takes(9),
        name="project",
    )(x, *weights, *biases, *tables)


SEGMENTS = 5
BOUND_LANE = SEGMENTS


def segment_lanes(first_key, past_key, segment, starts):
    lane = jnp.arange(PAIR, dtype=jnp.int32)[None, :] % HEAD_DIM
    start = sum(jnp.where(lane == n, starts[n], 0) for n in range(SEGMENTS))
    inside = (start >= first_key[:, None]) & (start < past_key[:, None])
    for_query = jnp.where((lane < SEGMENTS) & ~inside, NEG, 0.0)
    for_key = jnp.where((lane == segment[:, None]) | (lane == BOUND_LANE), 1.0, 0.0)
    return low(for_query), low(for_key)


def own_lanes(head):
    lane = lax.broadcasted_iota(jnp.int32, (1, PAIR), 1)
    return (lane >= HEAD_DIM) == (head == 1), lane % HEAD_DIM


def attend_strips(shifted, v_ref, out_ref, root_ref, early_ref, late_ref):
    values = v_ref[...].T
    least = None
    for strip in STRIPS:
        first, past, stop = strip
        outs, roots = [], []
        for head in range(2):
            powers = jnp.exp2(shifted(head, strip))
            total = jnp.sum(powers, 0, keepdims=True)
            least = jnp.min(total) if least is None else jnp.minimum(least, jnp.min(total))
            root = 1.0 / total
            powers = low(powers)
            if past <= EARLY:
                early_ref[head, :, first:past] = powers
            else:
                late_ref[head, 0:stop, first - EARLY : past - EARLY] = powers
            rows = slice(head * HEAD_DIM, (head + 1) * HEAD_DIM)
            outs.append(dot(values[rows, 0:stop], powers) * root)
            roots.append(jnp.broadcast_to(root, (HEAD_DIM, past - first)))
        out_ref[first:past, :] = low(jnp.concatenate(outs, 0).T)
        root_ref[first:past, :] = jnp.concatenate(roots, 0).T
    return least


def attend_kernel(
    q_ref, k_ref, v_ref, query_ref, key_ref, lo_ref, hi_ref, out_ref, root_ref, early_ref, late_ref
):
    factor = HEAD_DIM**-0.5 * LOG2E
    squares = wide(k_ref[...]) * wide(k_ref[...])
    keys, longest = [], []
    for head in range(2):
        own, _ = own_lanes(head)
        keys.append(jnp.where(own, k_ref[...], key_ref[...]))
        length = jnp.sum(jnp.where(own, squares, 0.0), 1, keepdims=True)
        longest.append(jnp.max(length, 0, keepdims=True))

    def below_bound(head, strip):
        first, past, stop = strip
        own, lane = own_lanes(head)
        q = q_ref[first:past, :]
        length = jnp.sum(jnp.where(own, wide(q) * wide(q), 0.0), 1, keepdims=True)
        bound = jnp.sqrt(length * longest[head]) * 1.01
        beside = jnp.where(lane == BOUND_LANE, low(-bound), query_ref[first:past, :])
        return dot_nt(keys[head][0:stop], jnp.where(own, q, beside)) * factor

    outs = (v_ref, out_ref, root_ref, early_ref, late_ref)
    least = attend_strips(below_bound, *outs)

    @pl.when(jnp.logical_not(least > 1e-20))
    def _():
        def below_maximum(head, strip):
            first, past, stop = strip
            own, _ = own_lanes(head)
            q = q_ref[first:past, :]
            scores = dot_nt(k_ref[0:stop, :], jnp.where(own, q, jnp.zeros_like(q)))
            key = lax.broadcasted_iota(jnp.int32, scores.shape, 0)
            allowed = (key >= lo_ref[:, first:past]) & (key < hi_ref[:, first:past])
            scores = jnp.where(allowed, scores, NEG)
            return (scores - jnp.max(scores, 0, keepdims=True)) * factor

        attend_strips(below_maximum, *outs)


def kept_specs(rows, base):
    return [
        pl.BlockSpec((2, STRIPS[0][2], EARLY), lambda i: (base + i, 0, 0)),
        pl.BlockSpec((2, rows, rows - EARLY), lambda i: (base + i, 0, 0)),
    ]


QUARTER_PAIRS = 2


def head_specs(rows, base):
    pair = lambda i: (base + i) // QUARTER_PAIRS * 3 * QUARTER_PAIRS + (base + i) % QUARTER_PAIRS
    part = lambda number: pl.BlockSpec((rows, PAIR), lambda i: (0, pair(i) + number * QUARTER_PAIRS))
    return [part(0), part(1), part(2)], pl.BlockSpec((rows, PAIR), lambda i: (0, base + i))


def attend(heads, lanes, first_key, past_key):
    rows, width = heads.shape[0], heads.shape[1] // 3
    pairs = width // PAIR
    parts, block = head_specs(rows, 0)
    beside = (*lanes, first_key, past_key)
    return pl.pallas_call(
        attend_kernel,
        grid=(pairs,),
        in_specs=parts + [whole(array) for array in beside],
        out_specs=[block, block] + kept_specs(rows, 0),
        out_shape=[
            jax.ShapeDtypeStruct((rows, width), jnp.bfloat16),
            jax.ShapeDtypeStruct((rows, width), jnp.float32),
            jax.ShapeDtypeStruct((2 * pairs, STRIPS[0][2], EARLY), jnp.bfloat16),
            jax.ShapeDtypeStruct((2 * pairs, rows, rows - EARLY), jnp.bfloat16),
        ],
        compiler_params=params(),
        cost_estimate=takes(20),
        name="attend",
    )(heads, heads, heads, *beside)


def attend_back_kernel(
    q_ref, k_ref, v_ref, g_ref, o_ref, root_ref, early_ref, late_ref, cos_ref, up_ref, down_ref,
    out_ref, sums_ref, keys_acc, values_acc, queries_acc,
):
    pair = pl.program_id(0)
    pairs = out_ref.shape[1] // (3 * PAIR)
    scale = HEAD_DIM**-0.5
    keys = k_ref[...].T
    values = []
    for head in range(2):
        own, lane = own_lanes(head)
        values.append(jnp.where(own, v_ref[...], low(jnp.where(lane < 3, 1.0, 0.0))))
    for first, past, stop in STRIPS[::-1]:
        q = q_ref[first:past, :]
        g = wide(g_ref[first:past, :]) * root_ref[first:past, :]
        inner = g * wide(o_ref[first:past, :])
        g = low(g)
        zero = jnp.zeros_like(g)
        for head in range(2):
            own, lane = own_lanes(head)
            rows = slice(head * HEAD_DIM, (head + 1) * HEAD_DIM)
            shift = -jnp.sum(jnp.where(own, inner, 0.0), 1, keepdims=True)
            beside = zero
            for number in range(3):
                part = low(shift)
                shift = shift - wide(part)
                beside = jnp.where(lane == number, part, beside)
            if past <= EARLY:
                powers = early_ref[head, :, first:past]
            else:
                powers = late_ref[head, 0:stop, first - EARLY : past - EARLY]
            g_scores = low(wide(powers) * dot_nt(values[head][0:stop], jnp.where(own, g, beside)))
            queries_acc[rows, first:past] = dot(keys[rows, 0:stop], g_scores)
            g_keys = dot(g_scores, jnp.where(own, q, zero))
            g_values = dot(powers, jnp.where(own, g, zero))
            if head == 0:
                total_keys, total_values = g_keys, g_values
            else:
                total_keys, total_values = total_keys + g_keys, total_values + g_values
        if past == STRIPS[-1][1]:
            keys_acc[...] = total_keys
            values_acc[...] = total_values
        else:
            keys_acc[0:stop, :] += total_keys
            values_acc[0:stop, :] += total_values
    cos, up, down = cos_ref[...], -up_ref[...], -down_ref[...]
    grads = (
        low(spin(queries_acc[...].T * scale, cos, up, down)),
        low(spin(keys_acc[...] * scale, cos, up, down)),
        low(values_acc[...]),
    )
    for number, grad in enumerate(grads):
        lanes = pl.ds(pl.multiple_of((number * pairs + pair) * PAIR, PAIR), PAIR)
        out_ref[:, lanes] = grad
        sums_ref[:, lanes] = fold(wide(grad))


def attend_back(quarter, heads, g, out, root, early, late, tables):
    rows, width = g.shape
    pairs = width // PAIR
    parts, block = head_specs(rows, quarter * pairs)
    return pl.pallas_call(
        attend_back_kernel,
        grid=(pairs,),
        in_specs=parts
        + [pl.BlockSpec((rows, PAIR), lambda i: (0, i)), block, block]
        + kept_specs(rows, quarter * pairs)
        + [whole(table) for table in tables],
        out_specs=[
            pl.BlockSpec((rows, 3 * width), lambda i: (0, 0)),
            pl.BlockSpec((8, 3 * width), lambda i: (0, 0)),
        ],
        out_shape=[
            jax.ShapeDtypeStruct((rows, 3 * width), jnp.bfloat16),
            jax.ShapeDtypeStruct((8, 3 * width), jnp.float32),
        ],
        scratch_shapes=[
            pltpu.VMEM((rows, PAIR), jnp.float32),
            pltpu.VMEM((rows, PAIR), jnp.float32),
            pltpu.VMEM((PAIR, rows), jnp.float32),
        ],
        compiler_params=params(56),
        cost_estimate=takes(16),
        name="attend_back",
    )(heads, heads, heads, g, out, root, early, late, *tables)


def merge_kernel(count, *refs):
    rights, lefts = refs[: 2 * count], refs[2 * count : 3 * count]
    x_ref, bias_ref, gain_ref, shift_ref, residual_ref, out_ref = refs[3 * count :]
    total = wide(x_ref[...]) + bias_ref[...]
    for number, right in enumerate(rights):
        left, width = lefts[number // 2], right.shape[0]
        total = total + dot(left[:, number % 2 * width : (number % 2 + 1) * width], right[...])
    residual_ref[...] = total
    normed, _ = standardize(total)
    out_ref[...] = low(normed * gain_ref[...] + shift_ref[...])


def merge(lefts, rights, x, bias, gain, shift, block=320):
    rows, depth = x.shape
    row = lambda array: pl.BlockSpec((block, array.shape[1]), lambda i: (i, 0))
    vectors = (bias[None], gain[None], shift[None])
    return pl.pallas_call(
        functools.partial(merge_kernel, len(lefts)),
        grid=(rows // block,),
        in_specs=[whole(w) for w in rights]
        + [row(a) for a in lefts]
        + [row(x)]
        + [whole(v) for v in vectors],
        out_specs=[row(x), row(x)],
        out_shape=[
            jax.ShapeDtypeStruct((rows, depth), jnp.float32),
            jax.ShapeDtypeStruct((rows, depth), jnp.bfloat16),
        ],
        compiler_params=params(),
        cost_estimate=takes(8),
        name="merge",
    )(*rights, *lefts, x, *vectors)


def expand_kernel(chunk, x_ref, w_ref, b_ref, active_ref, slope_ref):
    for at in range(0, x_ref.shape[0], chunk):
        rows = slice(at, at + chunk)
        v = dot(x_ref[rows, :], w_ref[...]) + b_ref[...]
        below = 0.5 + 0.5 * lax.erf(v * ROOT_HALF)
        active_ref[rows, :] = low(v * below)
        slope_ref[rows, :] = low(below + v * jnp.exp(-0.5 * v * v) * GAUSS_NORM)


def expand(x, weight, bias, block=512, chunk=256):
    rows, depth = x.shape
    width = weight.shape[1]
    out = pl.BlockSpec((rows, block), lambda i: (0, i))
    return pl.pallas_call(
        functools.partial(expand_kernel, chunk),
        grid=(width // block,),
        in_specs=[
            whole(x),
            pl.BlockSpec((depth, block), lambda i: (0, i)),
            pl.BlockSpec((1, block), lambda i: (0, i)),
        ],
        out_specs=[out, out],
        out_shape=[jax.ShapeDtypeStruct((rows, width), jnp.bfloat16)] * 2,
        compiler_params=params(),
        cost_estimate=takes(8.5),
        name="expand",
    )(x, weight, bias[None])


def reduce_kernel(count, half, side_ref, *refs):
    rights, lefts = refs[:count], refs[count : 2 * count]
    x_ref, bias_ref, send_ref, keep_ref = refs[2 * count :]
    total = x_ref[...] + bias_ref[...]
    for left, right in zip(lefts, rights):
        total = total + dot(left[...], right[...])

    @pl.when(pl.program_id(0) < half)
    def _():
        send_ref[...] = low(total)

    @pl.when(pl.program_id(0) >= half)
    def _():
        keep_ref[...] = low(total)


def reduce_rows(side, lefts, rights, x, bias, block=320):
    rows, depth = x.shape
    half = rows // 2 // block
    at = lambda i, side: jnp.where(i < half, (1 - side[0]) * half + i, side[0] * half + i - half)
    row = lambda array: pl.BlockSpec((block, array.shape[1]), lambda i, side: (at(i, side), 0))
    return pl.pallas_call(
        functools.partial(reduce_kernel, len(lefts), half),
        grid_spec=pltpu.PrefetchScalarGridSpec(
            num_scalar_prefetch=1,
            grid=(2 * half,),
            in_specs=[whole(w) for w in rights]
            + [row(a) for a in lefts]
            + [row(x), whole(bias[None])],
            out_specs=[
                pl.BlockSpec((block, depth), lambda i, side: (jnp.minimum(i, half - 1), 0)),
                pl.BlockSpec((block, depth), lambda i, side: (jnp.maximum(i - half, 0), 0)),
            ],
        ),
        out_shape=[jax.ShapeDtypeStruct((rows // 2, depth), jnp.bfloat16)] * 2,
        compiler_params=params(),
        cost_estimate=takes(0.1),
        name="reduce_rows",
    )(side, *rights, *lefts, x, bias[None])


def back_kernel(count, at_ref, *refs):
    rights, lefts = refs[:count], refs[count : 2 * count]
    base_ref, above_ref, gain_ref, out_ref, sums_ref = refs[2 * count :]

    @pl.when(pl.program_id(0) == 0)
    def _():
        sums_ref[...] = jnp.zeros_like(sums_ref)

    g = dot_nt(lefts[0][...], rights[0][...])
    for left, right in zip(lefts[1:], rights[1:]):
        g = g + dot_nt(left[...], right[...])
    normed, scale = standardize(wide(base_ref[...]))
    u = g * gain_ref[...]
    above = wide(above_ref[...])
    inner = jnp.mean(u, -1, keepdims=True) + normed * jnp.mean(u * normed, -1, keepdims=True)
    out = low(above + scale * (u - inner))
    out_ref[...] = out
    sums_ref[0] += fold(g * normed)
    sums_ref[1] += fold(g)
    sums_ref[2] += fold(wide(out))
    sums_ref[3] += fold(above)


def back_norm(at, lefts, rights, base, above, gain, block=320):
    rows, depth = base.shape
    row = lambda array: pl.BlockSpec((block, array.shape[1]), lambda i, at: (at[i], 0))
    return pl.pallas_call(
        functools.partial(back_kernel, len(lefts)),
        grid_spec=pltpu.PrefetchScalarGridSpec(
            num_scalar_prefetch=1,
            grid=(at.size,),
            in_specs=[whole(w) for w in rights]
            + [row(a) for a in lefts]
            + [row(base), row(above), whole(gain[None])],
            out_specs=[
                pl.BlockSpec((block, depth), lambda i, at: (i, 0)),
                pl.BlockSpec((4, 8, depth), lambda i, at: (0, 0, 0)),
            ],
        ),
        out_shape=[
            jax.ShapeDtypeStruct((rows, depth), jnp.bfloat16),
            jax.ShapeDtypeStruct((4, 8, depth), jnp.float32),
        ],
        compiler_params=params(),
        cost_estimate=takes(0.1 if base.dtype == jnp.float32 else 20),
        name="back_norm",
    )(at, *rights, *lefts, base, above, gain[None])


def place_kernel(steps, flag_ref, mine_ref, theirs_ref, out_ref):
    @pl.when(pl.program_id(0) < steps)
    def _():
        out_ref[...] = mine_ref[...].astype(out_ref.dtype).reshape(out_ref.shape)

    @pl.when(pl.program_id(0) >= steps)
    def _():
        out_ref[...] = theirs_ref[...].astype(out_ref.dtype).reshape(out_ref.shape)


def place(flag, mine, theirs, steps, in_block, in_index, out_shape, out_block, out_index, dtype):
    def target(i, flag):
        return out_index(jnp.where(i < steps, flag[0], 1 - flag[0]), jnp.where(i < steps, i, i - steps))

    return pl.pallas_call(
        functools.partial(place_kernel, steps),
        grid_spec=pltpu.PrefetchScalarGridSpec(
            num_scalar_prefetch=1,
            grid=(2 * steps,),
            in_specs=[
                pl.BlockSpec(in_block, lambda i, flag: in_index(jnp.minimum(i, steps - 1))),
                pl.BlockSpec(in_block, lambda i, flag: in_index(jnp.maximum(i - steps, 0))),
            ],
            out_specs=pl.BlockSpec(out_block, target),
        ),
        out_shape=jax.ShapeDtypeStruct(out_shape, dtype),
        compiler_params=params(),
        cost_estimate=takes(4),
        name="place",
    )(flag, mine, theirs)


def place_rows(flag, mine, theirs, steps, dtype):
    rows, width = mine.shape
    block = (rows // steps, width)
    return place(
        flag, mine, theirs, steps, block, lambda j: (j, 0),
        (2 * rows, width), block, lambda half, j: (half * steps + j, 0), dtype,
    )


def place_columns(flag, mine, theirs, steps, dtype):
    rows, width = mine.shape
    block = (rows // steps, width)
    return place(
        flag, mine, theirs, steps, block, lambda j: (j, 0),
        (rows, 2 * width), block, lambda half, j: (j, half), dtype,
    )


def place_heads(flag, mine, theirs, dtype):
    rows, width = mine.shape[0], mine.shape[1] // 3
    return place(
        flag, mine, theirs, 3, (rows, width), lambda j: (0, j),
        (3, rows, 2 * width), (1, rows, width), lambda half, j: (j, 0, half), dtype,
    )


def column_sums(matrix):
    unit_column = jnp.ones((matrix.shape[0],), matrix.dtype)
    return jnp.dot(unit_column, matrix, preferred_element_type=jnp.float32)


KEEP, SEND = 0, 1
OWN, FAR = 0, 1
QUARTERS = ((FAR, SEND), (FAR, KEEP), (OWN, SEND), (OWN, KEEP))


def on_device(
    spread,
    tokens,
    cotangent,
    patch_count,
    first_gain,
    first_shift,
    heads_weight,
    heads_bias,
    merge_weight,
    merge_bias,
    second_gain,
    second_shift,
    expand_weight,
    expand_bias,
    reduce_weight,
    reduce_bias,
):
    levels = spread.bit_length() - 1
    rest = list(range(1, levels))
    chunks = spread // 2
    location = lax.axis_index("dp")
    side = lax.axis_index("mp")
    sides = side[None].astype(jnp.int32)
    previous = []

    def bit(level):
        return (location >> level) & 1

    core = bit(0)[None].astype(jnp.int32)

    def tie(array, *others):
        return lax.optimization_barrier((array,) + others)[0] if others else array

    def after(array):
        return tie(array, *previous)

    def did(*arrays):
        previous[:] = arrays
        return arrays[0] if len(arrays) == 1 else arrays

    def swap(array, level):
        return lax.ppermute(array, "dp", [(i, i ^ (1 << level)) for i in range(spread)])

    def cross(array):
        return lax.ppermute(array, "mp", [(0, 1), (1, 0)])

    def half_of(array, flag, axis=0):
        size = array.shape[axis] // 2
        return lax.dynamic_slice_in_dim(array, flag * size, size, axis)

    def chunk_of(array):
        size = array.shape[0] // chunks
        return lax.dynamic_slice_in_dim(array, (location >> 1) * size, size, 0)

    def split(array, level, open_levels=None):
        left = 1 << sum(other > level for other in (open_levels or rest))
        four = array.reshape(left, 2, -1, array.shape[1])
        part = lambda flag: lax.dynamic_index_in_dim(four, flag, 1, False).reshape(-1, array.shape[1])
        return part(bit(level)), part(1 - bit(level))

    def join(mine, theirs, level, open_levels=None):
        left = 1 << sum(other > level for other in (open_levels or rest))
        four = lambda array: array.reshape(left, 1, -1, array.shape[1])
        pair = jnp.where(
            bit(level) == 0,
            jnp.concatenate([four(mine), four(theirs)], 1),
            jnp.concatenate([four(theirs), four(mine)], 1),
        )
        return pair.reshape(-1, mine.shape[1])

    def quarters_of(own, axis):
        return [half_of(own, bit(0), axis), half_of(own, 1 - bit(0), axis)]

    tokens, cotangent = tokens[:, 0], cotangent[:, 0]
    heads_three = heads_weight.transpose(1, 0, 2)
    near = rest[:2]
    piece_rows = heads_three.shape[1] >> len(near)
    piece_width = heads_three.shape[2] // 2
    piece_at = ((location >> 1) & ((1 << len(near)) - 1)) * piece_rows
    heads_piece = jnp.concatenate(
        [
            lax.dynamic_slice(
                heads_three, (n, piece_at, bit(0) * piece_width), (1, piece_rows, piece_width)
            )[0]
            for n in range(3)
        ],
        1,
    )
    heads_cross = cross(heads_piece)
    tokens_far = cross(lax.dynamic_index_in_dim(tie(tokens, heads_piece), 1 - side, 0, False))
    heads_own = [
        jnp.concatenate([half_of(heads_three[n], flag, 1) for n in range(3)], 1)
        for flag in (bit(0), 1 - bit(0))
    ]
    merge_own = quarters_of(merge_weight, 0)
    expand_own = quarters_of(expand_weight, 1)
    reduce_own = quarters_of(reduce_weight, 0)
    pack = lambda hb, eb: jnp.concatenate([hb.reshape(-1), eb])
    bias_own = [
        pack(half_of(heads_bias, flag, 1), half_of(expand_bias, flag)) for flag in (bit(0), 1 - bit(0))
    ]
    three = heads_bias.size // 2
    up_piece = jnp.concatenate([chunk_of(expand_own[KEEP]), chunk_of(merge_own[KEEP])])
    down_piece = chunk_of(reduce_own[KEEP])

    count_one = lax.dynamic_index_in_dim(patch_count[:, 0], side, 0, False)
    length = 2 * tokens.shape[1]
    first_key, past_key, frame_id, patch_row, column, segment, starts = slot_layout(count_one, length)
    tables = rotary_tables(frame_id, patch_row, column)
    lanes = segment_lanes(first_key, past_key, segment, starts)
    first_key, past_key = first_key[None], past_key[None]

    bias_pieces = jnp.concatenate(bias_own)
    did(*heads_own, *merge_own)
    heads_piece = did(after(heads_cross))
    if len(near) > 1:
        heads_next = swap(heads_piece, near[1])
        expand_own = quarters_of(after(expand_weight), 1)
        up_piece = jnp.concatenate([chunk_of(expand_own[KEEP]), chunk_of(merge_own[KEEP])])
        did(*expand_own, up_piece)
        heads_piece = did(join(after(heads_piece), heads_next, near[1], near[1:]))
    heads_next = swap(heads_piece, near[0])
    up_piece = cross(tie(up_piece, heads_piece))
    bias_both = cross(tie(bias_pieces, heads_piece))
    did(heads_piece, down_piece, *heads_own, *merge_own, *expand_own, *reduce_own, *tables, *lanes)
    bias_far = [bias_both[: bias_both.size // 2], bias_both[bias_both.size // 2 :]]
    stream, first_out = did(*enter(sides, after(tokens), tokens_far, first_gain, first_shift))
    heads, seen = {}, {}
    heads_all = [heads_own, None]
    bias_all = (bias_own, bias_far)

    def look(p):
        biases = [bias[:three] for bias in bias_all[p]]
        heads[p] = did(project(after(first_out), heads_all[p], biases, tables))

    def attention(p):
        seen[p] = did(*attend(after(heads[p]), lanes, first_key, past_key))

    def gathered(array, *splits):
        array = lax.all_gather(array, "dp", axis=0, tiled=True)
        array = array.reshape(chunks, 2, -1, array.shape[1])
        quarters, at = [], 0
        for size in splits:
            part = array[:, :, at : at + size]
            quarters.append(
                [
                    lax.dynamic_index_in_dim(part, flag, 1, False).reshape(-1, array.shape[3])
                    for flag in (bit(0), 1 - bit(0))
                ]
            )
            at += size
        return quarters

    look(OWN)
    up_sizes = (expand_own[0].shape[0] // chunks, merge_own[0].shape[0] // chunks)
    up_gathered = gathered(after(up_piece), *up_sizes)
    down_piece = cross(after(down_piece))
    heads_piece = did(join(after(heads_piece), heads_next, near[0], near))
    heads_all[FAR] = [heads_piece, swap(heads_piece, 0)]
    attention(OWN)
    cotangent_far = cross(after(lax.dynamic_index_in_dim(cotangent, 1 - side, 0, False)))
    look(FAR)
    (reduce_far,) = gathered(after(down_piece), down_piece.shape[0])
    attention(FAR)
    expand_far, merge_far = ([after(q) for q in quarters] for quarters in up_gathered)
    merge_all = (merge_own, merge_far)
    expand_all = (expand_own, expand_far)
    reduce_all = (reduce_own, reduce_far)
    width = seen[OWN][0].shape[1] // 2
    residual, second_out = did(
        *merge(
            [seen[OWN][0], seen[FAR][0]], [merge_all[p][c] for p in (OWN, FAR) for c in (KEEP, SEND)],
            after(stream), merge_bias, second_gain, second_shift,
        )
    )
    grad_two = did(collect(sides, after(cotangent), cotangent_far))

    active, slope, grad_pre = {}, {}, {}

    def widen(p, c):
        active[p, c], slope[p, c] = did(
            *expand(after(second_out), expand_all[p][c], bias_all[p][c][three:])
        )

    def back_active(p, c):
        grad_pre[p, c] = did(low(dot_nt(after(grad_two), reduce_all[p][c]) * wide(slope[p, c])))

    def product(left, right, *arrived):
        total = dot_tn(after(left), right)
        for array in arrived:
            total = total + wide(array)
        return did(low(total))

    def scattered(array, level, open_levels=None):
        keep, send = split(after(array), level, open_levels or rest[rest.index(level) :])
        did(send)
        return keep, swap(send, level)

    def summed(keep, arrived):
        return did(low(wide(after(keep)) + wide(arrived)))

    def rows_out(keep, arrived, dtype):
        return place_rows(sides, keep, arrived, 1, dtype).reshape(2, 1, length // 2, -1)

    widen(FAR, SEND)
    widen(FAR, KEEP)
    sent = swap(product(active[FAR, SEND], grad_two), 0)
    widen(OWN, SEND)
    reduce_far_sum = product(active[FAR, KEEP], grad_two, sent)
    reduce_cross = cross(reduce_far_sum)
    widen(OWN, KEEP)
    sent = swap(product(active[OWN, SEND], grad_two), 0)
    back_active(FAR, SEND)
    reduce_sum = product(active[OWN, KEEP], grad_two, sent)
    back_active(FAR, KEEP)
    sent = swap(product(second_out, grad_pre[FAR, SEND]), 0)
    back_active(OWN, SEND)
    expand_far_sum = product(second_out, grad_pre[FAR, KEEP], sent)
    back_active(OWN, KEEP)
    sent = swap(product(second_out, grad_pre[OWN, SEND]), 0)
    expand_sum = product(second_out, grad_pre[OWN, KEEP], sent)
    expand_cross = cross(expand_far_sum)
    blocks = jnp.arange(length // 320, dtype=jnp.int32)
    grad_one, second_sums = did(
        *back_norm(
            blocks, [grad_pre[q] for q in QUARTERS], [expand_all[p][c] for p, c in QUARTERS],
            after(residual), grad_two, second_gain,
        )
    )
    grad_mixed, grad_heads, head_sums = {}, {}, {}

    def back_mixed(p, c):
        grad_mixed[p, c] = did(low(dot_nt(after(grad_one), merge_all[p][c])))

    def back_attention(q):
        p, c = q
        grad_heads[q], sums = did(
            *attend_back(c, heads[p], after(grad_mixed[q]), *seen[p], tables)
        )
        head_sums[q] = jnp.sum(sums, 0)

    merge_far_sum = product(seen[FAR][0], grad_one)
    sent_far = swap(merge_far_sum[width:], 0)
    merge_sum = product(seen[OWN][0], grad_one)
    sent_own = swap(merge_sum[width:], 0)
    for p, c in QUARTERS:
        back_mixed(p, c)
    merge_far_sum = summed(merge_far_sum[:width], sent_far)
    merge_sum = summed(merge_sum[:width], sent_own)
    merge_cross = cross(tie(merge_far_sum, reduce_cross))
    reduce_sum = summed(reduce_sum, reduce_cross)
    reduce_keep, reduce_next = scattered(reduce_sum, rest[0])
    back_attention((FAR, SEND))
    reduce_sum = summed(reduce_keep, reduce_next)
    reduce_keep, reduce_next = scattered(reduce_sum, rest[1])
    sent = swap(product(first_out, grad_heads[FAR, SEND]), 0)
    expand_sum = summed(expand_sum, expand_cross)
    expand_keep, expand_next = scattered(expand_sum, rest[0])
    merge_sum = summed(merge_sum, merge_cross)
    merge_keep, merge_next = scattered(merge_sum, rest[0])
    reduce_sum = summed(reduce_keep, reduce_next)
    for level in rest[2:]:
        reduce_keep, reduce_next = scattered(reduce_sum, level)
        reduce_sum = low(wide(reduce_keep) + wide(reduce_next))
    back_attention((FAR, KEEP))
    reduce_total = lax.all_gather(after(reduce_sum), "dp", axis=0, tiled=True)
    heads_far_sum = product(first_out, grad_heads[FAR, KEEP], sent)
    heads_cross = cross(heads_far_sum)
    expand_sum = summed(expand_keep, expand_next)
    merge_sum = summed(merge_keep, merge_next)
    expand_keep, expand_next = scattered(expand_sum, rest[1])
    merge_keep, merge_next = scattered(merge_sum, rest[1])
    back_attention((OWN, SEND))
    expand_sum = summed(expand_keep, expand_next)
    merge_sum = summed(merge_keep, merge_next)
    for level in rest[2:]:
        expand_keep, expand_next = scattered(expand_sum, level)
        merge_keep, merge_next = scattered(merge_sum, level)
        expand_sum = low(wide(expand_keep) + wide(expand_next))
        merge_sum = low(wide(merge_keep) + wide(merge_next))
    sent = swap(product(first_out, grad_heads[OWN, SEND]), 0)
    back_attention((OWN, KEEP))
    expand_total = lax.all_gather(
        after(jnp.concatenate([expand_sum, merge_sum])), "dp", axis=0, tiled=True
    )
    heads_sum = product(first_out, grad_heads[OWN, KEEP], sent, heads_cross)
    orders = [rest, rest[1:2] + rest[:1] + rest[2:]]
    middle = heads_sum.shape[1] // 2
    heads_sums = [heads_sum[:, :middle], heads_sum[:, middle:]]

    def both_scattered(n):
        return [scattered(total, order[n], order[n:]) for total, order in zip(heads_sums, orders)]

    def both_summed(pairs):
        return [summed(*pair) for pair in pairs]

    def in_rows(array):
        return wide(array.transpose(1, 0, 2, 3).reshape(-1, array.shape[3]))

    reduce_total = reduce_total.reshape(chunks, 2, -1, reduce_total.shape[1])
    expand_total = expand_total.reshape(chunks, 2, -1, expand_total.shape[1])
    rows = expand_sum.shape[0]

    pairs = both_scattered(0)
    lefts = [grad_heads[q] for q in QUARTERS]
    rights = [heads_all[p][c] for p, c in QUARTERS]
    half = length // 2
    blocks = (blocks + (1 - sides) * (half // 320)) % (length // 320)
    tokens_rows, first_sums = did(
        *back_norm(blocks, lefts, rights, stream, grad_one, after(first_gain))
    )
    tokens_cross, tokens_keep = cross(tokens_rows[:half]), tokens_rows[half:]
    heads_sums = both_summed(pairs)
    pairs = both_scattered(1)

    small = {q: jnp.concatenate([head_sums[q], column_sums(grad_pre[q])]) for q in QUARTERS}
    both = jnp.concatenate(
        [
            jnp.sum(part, 0)
            for part in (
                first_sums[0], first_sums[1], second_sums[0], second_sums[1], second_sums[2], second_sums[3],
            )
        ]
    )
    far_send, own_send, both = did(*(after(v) for v in (small[FAR, SEND], small[OWN, SEND], both)))
    arrived = swap(jnp.concatenate([far_send, own_send, both]), 0)
    size = own_send.size
    reduce_out = in_rows(after(reduce_total))
    arrived, reduce_out = lax.optimization_barrier((arrived, reduce_out))
    did(arrived)
    heads_sums = both_summed(pairs)
    mine = jnp.concatenate([small[FAR, KEEP] + arrived[:size], small[OWN, KEEP], both])
    mine = did(
        jnp.concatenate([mine[:size], mine[size:] + after(arrived)[size:]])
    )
    for n in range(2, len(rest) - 1):
        pairs = both_scattered(n)
        small_next = swap(mine, rest[n])
        heads_sums = both_summed(pairs)
        mine = did(mine + after(small_next))
    arrived = [swap(total, rest[-1]) for total in heads_sums]
    small_next = swap(mine, rest[-1])
    layer_send, layer_keep = did(
        *reduce_rows(
            sides, [active[q] for q in QUARTERS], [reduce_all[p][c] for p, c in QUARTERS],
            after(residual), reduce_bias,
        )
    )
    heads_sums = both_summed(zip(heads_sums, arrived))
    mine = did(mine + after(small_next))
    layer_far = cross(tie(layer_send, tokens_cross))
    for n in range(len(rest) - 1)[::-1]:
        arrived = [swap(total, order[n]) for total, order in zip(heads_sums, orders)]
        small_next = swap(mine, rest[n]) if n < 2 else None
        if n == len(rest) - 2:
            tokens_out = rows_out(after(tokens_keep), tokens_cross, jnp.float32)
            mine, tokens_out = lax.optimization_barrier((mine, tokens_out))
            did(mine)
        if n == 0:
            expand_out = wide(
                jnp.concatenate(
                    [
                        after(expand_total)[:, half, :rows].reshape(-1, expand_total.shape[3])
                        for half in range(2)
                    ],
                    1,
                )
            )
            mine, expand_out = lax.optimization_barrier((mine, expand_out))
            did(mine)
        heads_sums = [
            did(join(after(total), other, order[n], order[n:]))
            for total, other, order in zip(heads_sums, arrived, orders)
        ]
        if n < 2:
            mine = did(mine + after(small_next))
    layer_out = rows_out(layer_keep, layer_far, jnp.bfloat16)
    heads_sum = jnp.concatenate(heads_sums, 1)
    heads_next = swap(heads_sum, 0)
    arrived = cross(jnp.concatenate([mine[:size], mine[2 * size :]]))
    both = mine[2 * size :] + arrived[size:]
    mine = mine[size : 2 * size] + arrived[:size]
    theirs = swap(mine, 0)
    first = jnp.where(bit(0) == 0, mine, theirs)
    second = jnp.where(bit(0) == 0, theirs, mine)
    heads_bias_total = jnp.concatenate([first[:three].reshape(3, -1), second[:three].reshape(3, -1)], 1)
    expand_bias_total = jnp.concatenate([first[three:], second[three:]])
    (first_gain_total, first_shift_total, second_gain_total, second_shift_total, merge_bias_total,
     reduce_bias_total) = both.reshape(6, -1)
    heads_out = place_heads(core, heads_sum, heads_next, jnp.float32)
    return (
        layer_out,
        tokens_out,
        first_gain_total,
        first_shift_total,
        heads_out.transpose(1, 0, 2),
        heads_bias_total,
        in_rows(expand_total[:, :, rows:]),
        merge_bias_total,
        second_gain_total,
        second_shift_total,
        expand_out,
        expand_bias_total,
        reduce_out,
        reduce_bias_total,
    )


def solution(mesh):
    rows = P(None, "dp", "mp", None)
    columns = P(None, "mp")
    heads = P(None, None, "mp")
    return jax.shard_map(
        functools.partial(on_device, mesh.shape["dp"]),
        mesh=mesh,
        in_specs=(
            rows, rows, P(None, "dp"), P(), P(), heads, columns, P("mp", None), P(), P(), P(), columns,
            P("mp"), P("mp", None), P(),
        ),
        out_specs=(
            rows, rows, P(), P(), heads, columns, P("mp", None), P(), P(), P(), columns, P("mp"),
            P("mp", None), P(),
        ),
        check_vma=False,
    )
```

```python
import functools
import math

import jax
import jax.numpy as jnp
from jax import lax
from jax.experimental import pallas as pl
from jax.experimental.pallas import tpu as pltpu
from jax.sharding import PartitionSpec as P

HEAD_DIM = 64
FRAMES = 2
SIDE_SMALL = 16
SIDE_LARGE = 24
EPSILON = 1e-06
ROOT_HALF = 0.7071067811865476
GAUSS_NORM = 0.3989422804014327
LOG2E = math.log2(math.e)
PAIR = 128
NEG = -1e30
STRIPS = ((0, 512, 592), (512, 1024, 1168), (1024, 1280, 1280))
EARLY = 512


def params(mib=50):
    return pltpu.CompilerParams(vmem_limit_bytes=mib * 2**20)


def takes(microseconds):
    return pl.CostEstimate(
        flops=int(microseconds * 4e9), bytes_accessed=int(microseconds * 4e6), transcendentals=0
    )


def low(array):
    return array.astype(jnp.bfloat16)


def wide(array):
    return array.astype(jnp.float32)


def dot(left, right):
    return jnp.dot(left, right, preferred_element_type=jnp.float32)


def dot_nt(left, right):
    return lax.dot_general(
        left, right, (((1,), (1,)), ((), ())), preferred_element_type=jnp.float32
    )


def dot_tn(left, right):
    return lax.dot_general(
        left, right, (((0,), (0,)), ((), ())), preferred_element_type=jnp.float32
    )


def slot_layout(count_one, length):
    large_count = SIDE_LARGE * SIDE_LARGE
    grid_side = jnp.where(count_one == large_count, SIDE_LARGE, SIDE_SMALL).astype(jnp.int32)
    frame_len = grid_side * grid_side + 2
    clip_len = FRAMES * frame_len
    clip_total = jnp.where(count_one == large_count, 1, 2).astype(jnp.int32)
    slot_id = jnp.arange(length, dtype=jnp.int32)
    clip_id = jnp.minimum(slot_id // clip_len, clip_total)
    offset_in = slot_id - clip_id * clip_len
    frame_id = offset_in // frame_len
    place_in = offset_in - frame_id * frame_len - 2
    patch_id = jnp.maximum(place_in, 0)
    is_live = clip_id < clip_total
    is_patch = is_live & (place_in >= 0)
    frame_id = jnp.where(is_live, frame_id, 0)
    patch_row = jnp.where(is_patch, patch_id // grid_side, 0)
    column = jnp.where(is_patch, patch_id - patch_id // grid_side * grid_side, 0)
    first_key = clip_id * clip_len
    past_key = jnp.where(is_live, first_key + (frame_id + 1) * frame_len, length)
    segment = FRAMES * clip_id + frame_id
    starts = [n * frame_len for n in range(FRAMES * 2 + 1)]
    return (first_key, past_key, frame_id, patch_row, column, segment, starts)


def rotary_tables(frame_id, patch_row, column):
    segment = 2 * (HEAD_DIM // 3 // 2)
    half_width = segment // 2
    dim_index = jnp.arange(PAIR, dtype=jnp.int32) % HEAD_DIM
    segment_id = dim_index // segment
    exponent = (dim_index % segment % half_width).astype(jnp.float32)
    frequency = jnp.exp(exponent * (-math.log(10000.0) / half_width))
    pick = lambda number: wide(jnp.where(segment_id == number, 1.0, 0.0))[None, :]
    position = (
        pick(0) * wide(frame_id[:, None])
        + pick(1) * wide(patch_row[:, None])
        + pick(2) * wide(column[:, None])
    )
    angles = position * frequency[None, :]
    lower = (dim_index % segment < half_width)[None, :]
    sine = jnp.where((segment_id < 3)[None, :], jnp.sin(angles), 0.0)
    return (jnp.cos(angles), jnp.where(lower, -sine, 0.0), jnp.where(lower, 0.0, sine))


def spin(x, cos, up, down):
    turn = HEAD_DIM // 3 // 2
    return x * cos + pltpu.roll(x, PAIR - turn, 1) * up + pltpu.roll(x, turn, 1) * down


def standardize(values_in):
    row_mean = jnp.mean(values_in, -1, keepdims=True)
    centred = values_in - row_mean
    norm_scale = lax.rsqrt(jnp.mean(centred * centred, -1, keepdims=True) + EPSILON)
    return (centred * norm_scale, norm_scale)


def fold(x):
    return jnp.sum(x.reshape(x.shape[0] // 8, 8, x.shape[1]), 0)


def whole(array):
    return pl.BlockSpec(array.shape, lambda *_: (0,) * array.ndim, pipeline_mode=pl.Buffered(1))


def enter_kernel(side_ref, mine_ref, arrived_ref, gain_ref, shift_ref, stream_ref, out_ref):
    def step(rows):
        stream_ref[...] = rows
        normed, _ = standardize(wide(rows))
        out_ref[...] = low(normed * gain_ref[...] + shift_ref[...])

    @pl.when(pl.program_id(0) == 0)
    def _():
        step(mine_ref[0])

    @pl.when(pl.program_id(0) == 1)
    def _():
        step(arrived_ref[...])


def enter(side, tokens, arrived, gain, shift):
    _, half, depth = tokens.shape
    vector = pl.BlockSpec((1, depth), lambda i, side: (0, 0))
    out = pl.BlockSpec((half, depth), lambda i, side: (jnp.where(i == 0, side[0], 1 - side[0]), 0))
    return pl.pallas_call(
        enter_kernel,
        grid_spec=pltpu.PrefetchScalarGridSpec(
            num_scalar_prefetch=1,
            grid=(2,),
            in_specs=[
                pl.BlockSpec((1, half, depth), lambda i, side: (side[0], 0, 0)),
                pl.BlockSpec((half, depth), lambda i, side: (0, 0)),
                vector,
                vector,
            ],
            out_specs=[out, out],
        ),
        out_shape=[jax.ShapeDtypeStruct((2 * half, depth), jnp.bfloat16)] * 2,
        compiler_params=params(),
        cost_estimate=takes(5),
        name="enter",
    )(side, tokens, arrived, gain[None], shift[None])


def collect_kernel(side_ref, mine_ref, arrived_ref, out_ref):
    @pl.when(pl.program_id(0) == 0)
    def _():
        out_ref[...] = mine_ref[0]

    @pl.when(pl.program_id(0) == 1)
    def _():
        out_ref[...] = arrived_ref[...]


def collect(side, array, arrived):
    _, half, depth = array.shape
    return pl.pallas_call(
        collect_kernel,
        grid_spec=pltpu.PrefetchScalarGridSpec(
            num_scalar_prefetch=1,
            grid=(2,),
            in_specs=[
                pl.BlockSpec((1, half, depth), lambda i, side: (side[0], 0, 0)),
                pl.BlockSpec((half, depth), lambda i, side: (0, 0)),
            ],
            out_specs=pl.BlockSpec(
                (half, depth), lambda i, side: (jnp.where(i == 0, side[0], 1 - side[0]), 0)
            ),
        ),
        out_shape=jax.ShapeDtypeStruct((2 * half, depth), array.dtype),
        compiler_params=params(),
        cost_estimate=takes(2),
        name="collect",
    )(side, array, arrived)


def project_kernel(chunk, count, x_ref, *refs):
    weights, biases, outs = refs[:count], refs[count : 2 * count], refs[2 * count + 3]
    tables = refs[2 * count : 2 * count + 3]
    for at in range(0, x_ref.shape[0], chunk):
        rows = slice(at, at + chunk)
        cos, up, down = (table[rows, :] for table in tables)
        for number, (w_ref, b_ref) in enumerate(zip(weights, biases)):
            base, width = number * w_ref.shape[1], w_ref.shape[1] // 3
            y = dot(x_ref[rows, :], w_ref[...]) + b_ref[...]
            for lane in range(0, 2 * width, PAIR):
                turned = spin(y[:, lane : lane + PAIR], cos, up, down)
                outs[rows, base + lane : base + lane + PAIR] = low(turned)
            outs[rows, base + 2 * width : base + 3 * width] = low(y[:, 2 * width :])


def project(x, weights, biases, tables, block=640, chunk=320):
    rows, depth = x.shape
    width = weights[0].shape[1] * len(weights)
    biases = [bias[None] for bias in biases]
    row = lambda array: pl.BlockSpec((block, array.shape[1]), lambda i: (i, 0))
    return pl.pallas_call(
        functools.partial(project_kernel, chunk, len(weights)),
        grid=(rows // block,),
        in_specs=[row(x)] + [whole(a) for a in (*weights, *biases)] + [row(t) for t in tables],
        out_specs=pl.BlockSpec((block, width), lambda i: (i, 0)),
        out_shape=jax.ShapeDtypeStruct((rows, width), jnp.bfloat16),
        compiler_params=params(),
        cost_estimate=takes(9),
        name="project",
    )(x, *weights, *biases, *tables)


SEGMENTS = 5
BOUND_LANE = SEGMENTS


def segment_lanes(first_key, past_key, segment, starts):
    lane = jnp.arange(PAIR, dtype=jnp.int32)[None, :] % HEAD_DIM
    start = sum(jnp.where(lane == n, starts[n], 0) for n in range(SEGMENTS))
    inside = (start >= first_key[:, None]) & (start < past_key[:, None])
    for_query = jnp.where((lane < SEGMENTS) & ~inside, NEG, 0.0)
    for_key = jnp.where((lane == segment[:, None]) | (lane == BOUND_LANE), 1.0, 0.0)
    return low(for_query), low(for_key)


def own_lanes(head):
    lane = lax.broadcasted_iota(jnp.int32, (1, PAIR), 1)
    return (lane >= HEAD_DIM) == (head == 1), lane % HEAD_DIM


def attend_strips(shifted, v_ref, out_ref, root_ref, early_ref, late_ref):
    values = v_ref[...].T
    least = None
    for strip in STRIPS:
        first, past, stop = strip
        outs, roots = [], []
        for head in range(2):
            powers = jnp.exp2(shifted(head, strip))
            total = jnp.sum(powers, 0, keepdims=True)
            least = jnp.min(total) if least is None else jnp.minimum(least, jnp.min(total))
            root = 1.0 / total
            powers = low(powers)
            if past <= EARLY:
                early_ref[head, :, first:past] = powers
            else:
                late_ref[head, 0:stop, first - EARLY : past - EARLY] = powers
            rows = slice(head * HEAD_DIM, (head + 1) * HEAD_DIM)
            outs.append(dot(values[rows, 0:stop], powers) * root)
            roots.append(jnp.broadcast_to(root, (HEAD_DIM, past - first)))
        out_ref[first:past, :] = low(jnp.concatenate(outs, 0).T)
        root_ref[first:past, :] = jnp.concatenate(roots, 0).T
    return least


def attend_kernel(
    q_ref, k_ref, v_ref, query_ref, key_ref, lo_ref, hi_ref, out_ref, root_ref, early_ref, late_ref
):
    factor = HEAD_DIM**-0.5 * LOG2E
    squares = wide(k_ref[...]) * wide(k_ref[...])
    keys, longest = [], []
    for head in range(2):
        own, _ = own_lanes(head)
        keys.append(jnp.where(own, k_ref[...], key_ref[...]))
        length = jnp.sum(jnp.where(own, squares, 0.0), 1, keepdims=True)
        longest.append(jnp.max(length, 0, keepdims=True))

    def below_bound(head, strip):
        first, past, stop = strip
        own, lane = own_lanes(head)
        q = q_ref[first:past, :]
        length = jnp.sum(jnp.where(own, wide(q) * wide(q), 0.0), 1, keepdims=True)
        bound = jnp.sqrt(length * longest[head]) * 1.01
        beside = jnp.where(lane == BOUND_LANE, low(-bound), query_ref[first:past, :])
        return dot_nt(keys[head][0:stop], jnp.where(own, q, beside)) * factor

    outs = (v_ref, out_ref, root_ref, early_ref, late_ref)
    least = attend_strips(below_bound, *outs)

    @pl.when(jnp.logical_not(least > 1e-20))
    def _():
        def below_maximum(head, strip):
            first, past, stop = strip
            own, _ = own_lanes(head)
            q = q_ref[first:past, :]
            scores = dot_nt(k_ref[0:stop, :], jnp.where(own, q, jnp.zeros_like(q)))
            key = lax.broadcasted_iota(jnp.int32, scores.shape, 0)
            allowed = (key >= lo_ref[:, first:past]) & (key < hi_ref[:, first:past])
            scores = jnp.where(allowed, scores, NEG)
            return (scores - jnp.max(scores, 0, keepdims=True)) * factor

        attend_strips(below_maximum, *outs)


def kept_specs(rows, base):
    return [
        pl.BlockSpec((2, STRIPS[0][2], EARLY), lambda i: (base + i, 0, 0)),
        pl.BlockSpec((2, rows, rows - EARLY), lambda i: (base + i, 0, 0)),
    ]


QUARTER_PAIRS = 2


def head_specs(rows, base):
    pair = lambda i: (base + i) // QUARTER_PAIRS * 3 * QUARTER_PAIRS + (base + i) % QUARTER_PAIRS
    part = lambda number: pl.BlockSpec((rows, PAIR), lambda i: (0, pair(i) + number * QUARTER_PAIRS))
    return [part(0), part(1), part(2)], pl.BlockSpec((rows, PAIR), lambda i: (0, base + i))


def attend(heads, lanes, first_key, past_key):
    rows, width = heads.shape[0], heads.shape[1] // 3
    pairs = width // PAIR
    parts, block = head_specs(rows, 0)
    beside = (*lanes, first_key, past_key)
    return pl.pallas_call(
        attend_kernel,
        grid=(pairs,),
        in_specs=parts + [whole(array) for array in beside],
        out_specs=[block, block] + kept_specs(rows, 0),
        out_shape=[
            jax.ShapeDtypeStruct((rows, width), jnp.bfloat16),
            jax.ShapeDtypeStruct((rows, width), jnp.float32),
            jax.ShapeDtypeStruct((2 * pairs, STRIPS[0][2], EARLY), jnp.bfloat16),
            jax.ShapeDtypeStruct((2 * pairs, rows, rows - EARLY), jnp.bfloat16),
        ],
        compiler_params=params(),
        cost_estimate=takes(20),
        name="attend",
    )(heads, heads, heads, *beside)


def attend_back_kernel(
    q_ref, k_ref, v_ref, g_ref, o_ref, root_ref, early_ref, late_ref, cos_ref, up_ref, down_ref,
    out_ref, sums_ref, keys_acc, values_acc, queries_acc,
):
    pair = pl.program_id(0)
    pairs = out_ref.shape[1] // (3 * PAIR)
    scale = HEAD_DIM**-0.5
    keys = k_ref[...].T
    values = []
    for head in range(2):
        own, lane = own_lanes(head)
        values.append(jnp.where(own, v_ref[...], low(jnp.where(lane < 3, 1.0, 0.0))))
    for first, past, stop in STRIPS[::-1]:
        q = q_ref[first:past, :]
        g = wide(g_ref[first:past, :]) * root_ref[first:past, :]
        inner = g * wide(o_ref[first:past, :])
        g = low(g)
        zero = jnp.zeros_like(g)
        for head in range(2):
            own, lane = own_lanes(head)
            rows = slice(head * HEAD_DIM, (head + 1) * HEAD_DIM)
            shift = -jnp.sum(jnp.where(own, inner, 0.0), 1, keepdims=True)
            beside = zero
            for number in range(3):
                part = low(shift)
                shift = shift - wide(part)
                beside = jnp.where(lane == number, part, beside)
            if past <= EARLY:
                powers = early_ref[head, :, first:past]
            else:
                powers = late_ref[head, 0:stop, first - EARLY : past - EARLY]
            g_scores = low(wide(powers) * dot_nt(values[head][0:stop], jnp.where(own, g, beside)))
            queries_acc[rows, first:past] = dot(keys[rows, 0:stop], g_scores)
            g_keys = dot(g_scores, jnp.where(own, q, zero))
            g_values = dot(powers, jnp.where(own, g, zero))
            if head == 0:
                total_keys, total_values = g_keys, g_values
            else:
                total_keys, total_values = total_keys + g_keys, total_values + g_values
        if past == STRIPS[-1][1]:
            keys_acc[...] = total_keys
            values_acc[...] = total_values
        else:
            keys_acc[0:stop, :] += total_keys
            values_acc[0:stop, :] += total_values
    cos, up, down = cos_ref[...], -up_ref[...], -down_ref[...]
    grads = (
        low(spin(queries_acc[...].T * scale, cos, up, down)),
        low(spin(keys_acc[...] * scale, cos, up, down)),
        low(values_acc[...]),
    )
    for number, grad in enumerate(grads):
        lanes = pl.ds(pl.multiple_of((number * pairs + pair) * PAIR, PAIR), PAIR)
        out_ref[:, lanes] = grad
        sums_ref[:, lanes] = fold(wide(grad))


def attend_back(quarter, heads, g, out, root, early, late, tables):
    rows, width = g.shape
    pairs = width // PAIR
    parts, block = head_specs(rows, quarter * pairs)
    return pl.pallas_call(
        attend_back_kernel,
        grid=(pairs,),
        in_specs=parts
        + [pl.BlockSpec((rows, PAIR), lambda i: (0, i)), block, block]
        + kept_specs(rows, quarter * pairs)
        + [whole(table) for table in tables],
        out_specs=[
            pl.BlockSpec((rows, 3 * width), lambda i: (0, 0)),
            pl.BlockSpec((8, 3 * width), lambda i: (0, 0)),
        ],
        out_shape=[
            jax.ShapeDtypeStruct((rows, 3 * width), jnp.bfloat16),
            jax.ShapeDtypeStruct((8, 3 * width), jnp.float32),
        ],
        scratch_shapes=[
            pltpu.VMEM((rows, PAIR), jnp.float32),
            pltpu.VMEM((rows, PAIR), jnp.float32),
            pltpu.VMEM((PAIR, rows), jnp.float32),
        ],
        compiler_params=params(56),
        cost_estimate=takes(16),
        name="attend_back",
    )(heads, heads, heads, g, out, root, early, late, *tables)


def merge_kernel(count, *refs):
    rights, lefts = refs[: 2 * count], refs[2 * count : 3 * count]
    x_ref, bias_ref, gain_ref, shift_ref, residual_ref, out_ref = refs[3 * count :]
    total = wide(x_ref[...]) + bias_ref[...]
    for number, right in enumerate(rights):
        left, width = lefts[number // 2], right.shape[0]
        total = total + dot(left[:, number % 2 * width : (number % 2 + 1) * width], right[...])
    residual_ref[...] = total
    normed, _ = standardize(total)
    out_ref[...] = low(normed * gain_ref[...] + shift_ref[...])


def merge(lefts, rights, x, bias, gain, shift, block=320):
    rows, depth = x.shape
    row = lambda array: pl.BlockSpec((block, array.shape[1]), lambda i: (i, 0))
    vectors = (bias[None], gain[None], shift[None])
    return pl.pallas_call(
        functools.partial(merge_kernel, len(lefts)),
        grid=(rows // block,),
        in_specs=[whole(w) for w in rights]
        + [row(a) for a in lefts]
        + [row(x)]
        + [whole(v) for v in vectors],
        out_specs=[row(x), row(x)],
        out_shape=[
            jax.ShapeDtypeStruct((rows, depth), jnp.float32),
            jax.ShapeDtypeStruct((rows, depth), jnp.bfloat16),
        ],
        compiler_params=params(),
        cost_estimate=takes(8),
        name="merge",
    )(*rights, *lefts, x, *vectors)


def expand_kernel(chunk, count, x_ref, *refs):
    weights, biases = refs[:count], refs[count : 2 * count]
    actives, slopes = refs[2 * count : 3 * count], refs[3 * count :]
    for w_ref, b_ref, active_ref, slope_ref in zip(weights, biases, actives, slopes):
        for at in range(0, x_ref.shape[0], chunk):
            rows = slice(at, at + chunk)
            v = dot(x_ref[rows, :], w_ref[...]) + b_ref[...]
            below = 0.5 + 0.5 * lax.erf(v * ROOT_HALF)
            active_ref[rows, :] = low(v * below)
            slope_ref[rows, :] = low(below + v * jnp.exp(-0.5 * v * v) * GAUSS_NORM)


def expand(x, weights, biases, block=512, chunk=256):
    rows, depth = x.shape
    count, width = len(weights), weights[0].shape[1]
    column = lambda size: pl.BlockSpec((size, block), lambda i: (0, i))
    return pl.pallas_call(
        functools.partial(expand_kernel, chunk, count),
        grid=(width // block,),
        in_specs=[whole(x)] + [column(depth)] * count + [column(1)] * count,
        out_specs=[column(rows)] * (2 * count),
        out_shape=[jax.ShapeDtypeStruct((rows, width), jnp.bfloat16)] * (2 * count),
        compiler_params=params(),
        cost_estimate=takes(14),
        name="expand",
    )(x, *weights, *[bias[None] for bias in biases])


def reduce_kernel(count, half, side_ref, *refs):
    rights, lefts = refs[:count], refs[count : 2 * count]
    x_ref, bias_ref, send_ref, keep_ref = refs[2 * count :]
    total = x_ref[...] + bias_ref[...]
    for left, right in zip(lefts, rights):
        total = total + dot(left[...], right[...])

    @pl.when(pl.program_id(0) < half)
    def _():
        send_ref[...] = low(total)

    @pl.when(pl.program_id(0) >= half)
    def _():
        keep_ref[...] = low(total)


def reduce_rows(side, lefts, rights, x, bias, block=320):
    rows, depth = x.shape
    half = rows // 2 // block
    at = lambda i, side: jnp.where(i < half, (1 - side[0]) * half + i, side[0] * half + i - half)
    row = lambda array: pl.BlockSpec((block, array.shape[1]), lambda i, side: (at(i, side), 0))
    return pl.pallas_call(
        functools.partial(reduce_kernel, len(lefts), half),
        grid_spec=pltpu.PrefetchScalarGridSpec(
            num_scalar_prefetch=1,
            grid=(2 * half,),
            in_specs=[whole(w) for w in rights]
            + [row(a) for a in lefts]
            + [row(x), whole(bias[None])],
            out_specs=[
                pl.BlockSpec((block, depth), lambda i, side: (jnp.minimum(i, half - 1), 0)),
                pl.BlockSpec((block, depth), lambda i, side: (jnp.maximum(i - half, 0), 0)),
            ],
        ),
        out_shape=[jax.ShapeDtypeStruct((rows // 2, depth), jnp.bfloat16)] * 2,
        compiler_params=params(),
        cost_estimate=takes(0.1),
        name="reduce_rows",
    )(side, *rights, *lefts, x, bias[None])


def back_kernel(count, at_ref, *refs):
    rights, lefts = refs[:count], refs[count : 2 * count]
    base_ref, above_ref, gain_ref, out_ref, sums_ref = refs[2 * count :]

    @pl.when(pl.program_id(0) == 0)
    def _():
        sums_ref[...] = jnp.zeros_like(sums_ref)

    g = dot_nt(lefts[0][...], rights[0][...])
    for left, right in zip(lefts[1:], rights[1:]):
        g = g + dot_nt(left[...], right[...])
    normed, scale = standardize(wide(base_ref[...]))
    u = g * gain_ref[...]
    above = wide(above_ref[...])
    inner = jnp.mean(u, -1, keepdims=True) + normed * jnp.mean(u * normed, -1, keepdims=True)
    out = low(above + scale * (u - inner))
    out_ref[...] = out
    sums_ref[0] += fold(g * normed)
    sums_ref[1] += fold(g)
    sums_ref[2] += fold(wide(out))
    sums_ref[3] += fold(above)


def back_norm(at, lefts, rights, base, above, gain, block=320):
    rows, depth = base.shape
    row = lambda array: pl.BlockSpec((block, array.shape[1]), lambda i, at: (at[i], 0))
    return pl.pallas_call(
        functools.partial(back_kernel, len(lefts)),
        grid_spec=pltpu.PrefetchScalarGridSpec(
            num_scalar_prefetch=1,
            grid=(at.size,),
            in_specs=[whole(w) for w in rights]
            + [row(a) for a in lefts]
            + [row(base), row(above), whole(gain[None])],
            out_specs=[
                pl.BlockSpec((block, depth), lambda i, at: (i, 0)),
                pl.BlockSpec((4, 8, depth), lambda i, at: (0, 0, 0)),
            ],
        ),
        out_shape=[
            jax.ShapeDtypeStruct((rows, depth), jnp.bfloat16),
            jax.ShapeDtypeStruct((4, 8, depth), jnp.float32),
        ],
        compiler_params=params(),
        cost_estimate=takes(0.1 if base.dtype == jnp.float32 else 20),
        name="back_norm",
    )(at, *rights, *lefts, base, above, gain[None])


def place_kernel(steps, flag_ref, mine_ref, theirs_ref, out_ref):
    @pl.when(pl.program_id(0) < steps)
    def _():
        out_ref[...] = mine_ref[...].astype(out_ref.dtype).reshape(out_ref.shape)

    @pl.when(pl.program_id(0) >= steps)
    def _():
        out_ref[...] = theirs_ref[...].astype(out_ref.dtype).reshape(out_ref.shape)


def place(flag, mine, theirs, steps, in_block, in_index, out_shape, out_block, out_index, dtype):
    def target(i, flag):
        return out_index(jnp.where(i < steps, flag[0], 1 - flag[0]), jnp.where(i < steps, i, i - steps))

    return pl.pallas_call(
        functools.partial(place_kernel, steps),
        grid_spec=pltpu.PrefetchScalarGridSpec(
            num_scalar_prefetch=1,
            grid=(2 * steps,),
            in_specs=[
                pl.BlockSpec(in_block, lambda i, flag: in_index(jnp.minimum(i, steps - 1))),
                pl.BlockSpec(in_block, lambda i, flag: in_index(jnp.maximum(i - steps, 0))),
            ],
            out_specs=pl.BlockSpec(out_block, target),
        ),
        out_shape=jax.ShapeDtypeStruct(out_shape, dtype),
        compiler_params=params(),
        cost_estimate=takes(4),
        name="place",
    )(flag, mine, theirs)


def place_rows(flag, mine, theirs, steps, dtype):
    rows, width = mine.shape
    block = (rows // steps, width)
    return place(
        flag, mine, theirs, steps, block, lambda j: (j, 0),
        (2 * rows, width), block, lambda half, j: (half * steps + j, 0), dtype,
    )


def place_columns(flag, mine, theirs, steps, dtype):
    rows, width = mine.shape
    block = (rows // steps, width)
    return place(
        flag, mine, theirs, steps, block, lambda j: (j, 0),
        (rows, 2 * width), block, lambda half, j: (j, half), dtype,
    )


def place_heads(flag, mine, theirs, dtype):
    rows, width = mine.shape[0], mine.shape[1] // 3
    return place(
        flag, mine, theirs, 3, (rows, width), lambda j: (0, j),
        (3, rows, 2 * width), (1, rows, width), lambda half, j: (j, 0, half), dtype,
    )


def column_sums(matrix):
    unit_column = jnp.ones((matrix.shape[0],), matrix.dtype)
    return jnp.dot(unit_column, matrix, preferred_element_type=jnp.float32)


KEEP, SEND = 0, 1
OWN, FAR = 0, 1
QUARTERS = ((FAR, SEND), (FAR, KEEP), (OWN, SEND), (OWN, KEEP))


def on_device(
    spread,
    tokens,
    cotangent,
    patch_count,
    first_gain,
    first_shift,
    heads_weight,
    heads_bias,
    merge_weight,
    merge_bias,
    second_gain,
    second_shift,
    expand_weight,
    expand_bias,
    reduce_weight,
    reduce_bias,
):
    levels = spread.bit_length() - 1
    rest = list(range(1, levels))
    chunks = spread // 2
    location = lax.axis_index("dp")
    side = lax.axis_index("mp")
    sides = side[None].astype(jnp.int32)
    previous = []

    def bit(level):
        return (location >> level) & 1

    core = bit(0)[None].astype(jnp.int32)

    def tie(array, *others):
        return lax.optimization_barrier((array,) + others)[0] if others else array

    def after(array):
        return tie(array, *previous)

    def did(*arrays):
        previous[:] = arrays
        return arrays[0] if len(arrays) == 1 else arrays

    def swap(array, level):
        return lax.ppermute(array, "dp", [(i, i ^ (1 << level)) for i in range(spread)])

    def cross(array):
        return lax.ppermute(array, "mp", [(0, 1), (1, 0)])

    def half_of(array, flag, axis=0):
        size = array.shape[axis] // 2
        return lax.dynamic_slice_in_dim(array, flag * size, size, axis)

    def chunk_of(array):
        size = array.shape[0] // chunks
        return lax.dynamic_slice_in_dim(array, (location >> 1) * size, size, 0)

    def split(array, level, open_levels=None):
        left = 1 << sum(other > level for other in (open_levels or rest))
        four = array.reshape(left, 2, -1, array.shape[1])
        part = lambda flag: lax.dynamic_index_in_dim(four, flag, 1, False).reshape(-1, array.shape[1])
        return part(bit(level)), part(1 - bit(level))

    def join(mine, theirs, level, open_levels=None):
        left = 1 << sum(other > level for other in (open_levels or rest))
        four = lambda array: array.reshape(left, 1, -1, array.shape[1])
        pair = jnp.where(
            bit(level) == 0,
            jnp.concatenate([four(mine), four(theirs)], 1),
            jnp.concatenate([four(theirs), four(mine)], 1),
        )
        return pair.reshape(-1, mine.shape[1])

    def quarters_of(own, axis):
        return [half_of(own, bit(0), axis), half_of(own, 1 - bit(0), axis)]

    tokens, cotangent = tokens[:, 0], cotangent[:, 0]
    heads_three = heads_weight.transpose(1, 0, 2)
    near = rest[:2]
    piece_rows = heads_three.shape[1] >> len(near)
    piece_width = heads_three.shape[2] // 2
    piece_at = ((location >> 1) & ((1 << len(near)) - 1)) * piece_rows
    heads_piece = jnp.concatenate(
        [
            lax.dynamic_slice(
                heads_three, (n, piece_at, bit(0) * piece_width), (1, piece_rows, piece_width)
            )[0]
            for n in range(3)
        ],
        1,
    )
    heads_cross = cross(heads_piece)
    tokens_far = cross(lax.dynamic_index_in_dim(tie(tokens, heads_piece), 1 - side, 0, False))
    heads_own = [
        jnp.concatenate([half_of(heads_three[n], flag, 1) for n in range(3)], 1)
        for flag in (bit(0), 1 - bit(0))
    ]
    merge_own = quarters_of(merge_weight, 0)
    expand_own = quarters_of(expand_weight, 1)
    reduce_own = quarters_of(reduce_weight, 0)
    pack = lambda hb, eb: jnp.concatenate([hb.reshape(-1), eb])
    bias_own = [
        pack(half_of(heads_bias, flag, 1), half_of(expand_bias, flag)) for flag in (bit(0), 1 - bit(0))
    ]
    three = heads_bias.size // 2
    up_piece = jnp.concatenate([chunk_of(expand_own[KEEP]), chunk_of(merge_own[KEEP])])
    down_piece = chunk_of(reduce_own[KEEP])

    count_one = lax.dynamic_index_in_dim(patch_count[:, 0], side, 0, False)
    length = 2 * tokens.shape[1]
    first_key, past_key, frame_id, patch_row, column, segment, starts = slot_layout(count_one, length)
    tables = rotary_tables(frame_id, patch_row, column)
    lanes = segment_lanes(first_key, past_key, segment, starts)
    first_key, past_key = first_key[None], past_key[None]

    bias_pieces = jnp.concatenate(bias_own)
    did(*heads_own, *merge_own)
    heads_piece = did(after(heads_cross))
    if len(near) > 1:
        heads_next = swap(heads_piece, near[1])
        expand_own = quarters_of(after(expand_weight), 1)
        up_piece = jnp.concatenate([chunk_of(expand_own[KEEP]), chunk_of(merge_own[KEEP])])
        did(*expand_own, up_piece)
        heads_piece = did(join(after(heads_piece), heads_next, near[1], near[1:]))
    heads_next = swap(heads_piece, near[0])
    up_piece = cross(tie(up_piece, heads_piece))
    bias_both = cross(tie(bias_pieces, heads_piece))
    did(heads_piece, down_piece, *heads_own, *merge_own, *expand_own, *reduce_own, *tables, *lanes)
    bias_far = [bias_both[: bias_both.size // 2], bias_both[bias_both.size // 2 :]]
    stream, first_out = did(*enter(sides, after(tokens), tokens_far, first_gain, first_shift))
    heads, seen = {}, {}
    heads_all = [heads_own, None]
    bias_all = (bias_own, bias_far)

    def look(p):
        biases = [bias[:three] for bias in bias_all[p]]
        heads[p] = did(project(after(first_out), heads_all[p], biases, tables))

    def attention(p):
        seen[p] = did(*attend(after(heads[p]), lanes, first_key, past_key))

    def gathered(array, *splits):
        array = lax.all_gather(array, "dp", axis=0, tiled=True)
        array = array.reshape(chunks, 2, -1, array.shape[1])
        quarters, at = [], 0
        for size in splits:
            part = array[:, :, at : at + size]
            quarters.append(
                [
                    lax.dynamic_index_in_dim(part, flag, 1, False).reshape(-1, array.shape[3])
                    for flag in (bit(0), 1 - bit(0))
                ]
            )
            at += size
        return quarters

    look(OWN)
    up_sizes = (expand_own[0].shape[0] // chunks, merge_own[0].shape[0] // chunks)
    up_gathered = gathered(after(up_piece), *up_sizes)
    down_piece = cross(after(down_piece))
    heads_piece = did(join(after(heads_piece), heads_next, near[0], near))
    heads_all[FAR] = [heads_piece, swap(heads_piece, 0)]
    attention(OWN)
    cotangent_far = cross(after(lax.dynamic_index_in_dim(cotangent, 1 - side, 0, False)))
    look(FAR)
    (reduce_far,) = gathered(after(down_piece), down_piece.shape[0])
    attention(FAR)
    expand_far, merge_far = ([after(q) for q in quarters] for quarters in up_gathered)
    merge_all = (merge_own, merge_far)
    expand_all = (expand_own, expand_far)
    reduce_all = (reduce_own, reduce_far)
    width = seen[OWN][0].shape[1] // 2
    residual, second_out = did(
        *merge(
            [seen[OWN][0], seen[FAR][0]], [merge_all[p][c] for p in (OWN, FAR) for c in (KEEP, SEND)],
            after(stream), merge_bias, second_gain, second_shift,
        )
    )
    grad_two = did(collect(sides, after(cotangent), cotangent_far))

    active, slope, grad_pre = {}, {}, {}

    def widen(p):
        active[p, KEEP], active[p, SEND], slope[p, KEEP], slope[p, SEND] = did(
            *expand(after(second_out), expand_all[p], [bias[three:] for bias in bias_all[p]])
        )

    def back_active(p, c):
        grad_pre[p, c] = did(low(dot_nt(after(grad_two), reduce_all[p][c]) * wide(slope[p, c])))

    def product(left, right, *arrived):
        total = dot_tn(after(left), right)
        for array in arrived:
            total = total + wide(array)
        return did(low(total))

    def scattered(array, level, open_levels=None):
        keep, send = split(after(array), level, open_levels or rest[rest.index(level) :])
        did(send)
        return keep, swap(send, level)

    def summed(keep, arrived):
        return did(low(wide(after(keep)) + wide(arrived)))

    def rows_out(keep, arrived, dtype):
        return place_rows(sides, keep, arrived, 1, dtype).reshape(2, 1, length // 2, -1)

    widen(FAR)
    sent = swap(product(active[FAR, SEND], grad_two), 0)
    widen(OWN)
    reduce_far_sum = product(active[FAR, KEEP], grad_two, sent)
    reduce_cross = cross(reduce_far_sum)
    sent = swap(product(active[OWN, SEND], grad_two), 0)
    back_active(FAR, SEND)
    reduce_sum = product(active[OWN, KEEP], grad_two, sent)
    back_active(FAR, KEEP)
    sent = swap(product(second_out, grad_pre[FAR, SEND]), 0)
    back_active(OWN, SEND)
    expand_far_sum = product(second_out, grad_pre[FAR, KEEP], sent)
    back_active(OWN, KEEP)
    sent = swap(product(second_out, grad_pre[OWN, SEND]), 0)
    expand_sum = product(second_out, grad_pre[OWN, KEEP], sent)
    expand_cross = cross(expand_far_sum)
    blocks = jnp.arange(length // 320, dtype=jnp.int32)
    grad_one, second_sums = did(
        *back_norm(
            blocks, [grad_pre[q] for q in QUARTERS], [expand_all[p][c] for p, c in QUARTERS],
            after(residual), grad_two, second_gain,
        )
    )
    grad_mixed, grad_heads, head_sums = {}, {}, {}

    def back_mixed(p, c):
        grad_mixed[p, c] = did(low(dot_nt(after(grad_one), merge_all[p][c])))

    def back_attention(q):
        p, c = q
        grad_heads[q], sums = did(
            *attend_back(c, heads[p], after(grad_mixed[q]), *seen[p], tables)
        )
        head_sums[q] = jnp.sum(sums, 0)

    merge_far_sum = product(seen[FAR][0], grad_one)
    sent_far = swap(merge_far_sum[width:], 0)
    merge_sum = product(seen[OWN][0], grad_one)
    sent_own = swap(merge_sum[width:], 0)
    for p, c in QUARTERS:
        back_mixed(p, c)
    merge_far_sum = summed(merge_far_sum[:width], sent_far)
    merge_sum = summed(merge_sum[:width], sent_own)
    merge_cross = cross(tie(merge_far_sum, reduce_cross))
    reduce_sum = summed(reduce_sum, reduce_cross)
    reduce_keep, reduce_next = scattered(reduce_sum, rest[0])
    back_attention((FAR, SEND))
    reduce_sum = summed(reduce_keep, reduce_next)
    reduce_keep, reduce_next = scattered(reduce_sum, rest[1])
    sent = swap(product(first_out, grad_heads[FAR, SEND]), 0)
    expand_sum = summed(expand_sum, expand_cross)
    expand_keep, expand_next = scattered(expand_sum, rest[0])
    merge_sum = summed(merge_sum, merge_cross)
    merge_keep, merge_next = scattered(merge_sum, rest[0])
    reduce_sum = summed(reduce_keep, reduce_next)
    for level in rest[2:]:
        reduce_keep, reduce_next = scattered(reduce_sum, level)
        reduce_sum = low(wide(reduce_keep) + wide(reduce_next))
    back_attention((FAR, KEEP))
    reduce_total = lax.all_gather(after(reduce_sum), "dp", axis=0, tiled=True)
    heads_far_sum = product(first_out, grad_heads[FAR, KEEP], sent)
    heads_cross = cross(heads_far_sum)
    expand_sum = summed(expand_keep, expand_next)
    merge_sum = summed(merge_keep, merge_next)
    expand_keep, expand_next = scattered(expand_sum, rest[1])
    merge_keep, merge_next = scattered(merge_sum, rest[1])
    back_attention((OWN, SEND))
    expand_sum = summed(expand_keep, expand_next)
    merge_sum = summed(merge_keep, merge_next)
    for level in rest[2:]:
        expand_keep, expand_next = scattered(expand_sum, level)
        merge_keep, merge_next = scattered(merge_sum, level)
        expand_sum = low(wide(expand_keep) + wide(expand_next))
        merge_sum = low(wide(merge_keep) + wide(merge_next))
    sent = swap(product(first_out, grad_heads[OWN, SEND]), 0)
    back_attention((OWN, KEEP))
    expand_total = lax.all_gather(
        after(jnp.concatenate([expand_sum, merge_sum])), "dp", axis=0, tiled=True
    )
    heads_sum = product(first_out, grad_heads[OWN, KEEP], sent, heads_cross)
    orders = [rest, rest[1:2] + rest[:1] + rest[2:]]
    middle = heads_sum.shape[1] // 2
    heads_sums = [heads_sum[:, :middle], heads_sum[:, middle:]]

    def both_scattered(n):
        return [scattered(total, order[n], order[n:]) for total, order in zip(heads_sums, orders)]

    def both_summed(pairs):
        return [summed(*pair) for pair in pairs]

    def in_rows(array):
        return wide(array.transpose(1, 0, 2, 3).reshape(-1, array.shape[3]))

    reduce_total = reduce_total.reshape(chunks, 2, -1, reduce_total.shape[1])
    expand_total = expand_total.reshape(chunks, 2, -1, expand_total.shape[1])
    rows = expand_sum.shape[0]

    pairs = both_scattered(0)
    lefts = [grad_heads[q] for q in QUARTERS]
    rights = [heads_all[p][c] for p, c in QUARTERS]
    half = length // 2
    blocks = (blocks + (1 - sides) * (half // 320)) % (length // 320)
    tokens_rows, first_sums = did(
        *back_norm(blocks, lefts, rights, stream, grad_one, after(first_gain))
    )
    tokens_cross, tokens_keep = cross(tokens_rows[:half]), tokens_rows[half:]
    heads_sums = both_summed(pairs)
    pairs = both_scattered(1)

    small = {q: jnp.concatenate([head_sums[q], column_sums(grad_pre[q])]) for q in QUARTERS}
    both = jnp.concatenate(
        [
            jnp.sum(part, 0)
            for part in (
                first_sums[0], first_sums[1], second_sums[0], second_sums[1], second_sums[2], second_sums[3],
            )
        ]
    )
    far_send, own_send, both = did(*(after(v) for v in (small[FAR, SEND], small[OWN, SEND], both)))
    arrived = swap(jnp.concatenate([far_send, own_send, both]), 0)
    size = own_send.size
    reduce_out = in_rows(after(reduce_total))
    arrived, reduce_out = lax.optimization_barrier((arrived, reduce_out))
    did(arrived)
    heads_sums = both_summed(pairs)
    mine = jnp.concatenate([small[FAR, KEEP] + arrived[:size], small[OWN, KEEP], both])
    mine = did(
        jnp.concatenate([mine[:size], mine[size:] + after(arrived)[size:]])
    )
    for n in range(2, len(rest) - 1):
        pairs = both_scattered(n)
        small_next = swap(mine, rest[n])
        heads_sums = both_summed(pairs)
        mine = did(mine + after(small_next))
    arrived = [swap(total, rest[-1]) for total in heads_sums]
    small_next = swap(mine, rest[-1])
    layer_send, layer_keep = did(
        *reduce_rows(
            sides, [active[q] for q in QUARTERS], [reduce_all[p][c] for p, c in QUARTERS],
            after(residual), reduce_bias,
        )
    )
    heads_sums = both_summed(zip(heads_sums, arrived))
    mine = did(mine + after(small_next))
    layer_far = cross(tie(layer_send, tokens_cross))
    for n in range(len(rest) - 1)[::-1]:
        arrived = [swap(total, order[n]) for total, order in zip(heads_sums, orders)]
        small_next = swap(mine, rest[n]) if n < 2 else None
        if n == len(rest) - 2:
            tokens_out = rows_out(after(tokens_keep), tokens_cross, jnp.float32)
            mine, tokens_out = lax.optimization_barrier((mine, tokens_out))
            did(mine)
        if n == 0:
            expand_out = wide(
                jnp.concatenate(
                    [
                        after(expand_total)[:, half, :rows].reshape(-1, expand_total.shape[3])
                        for half in range(2)
                    ],
                    1,
                )
            )
            mine, expand_out = lax.optimization_barrier((mine, expand_out))
            did(mine)
        heads_sums = [
            did(join(after(total), other, order[n], order[n:]))
            for total, other, order in zip(heads_sums, arrived, orders)
        ]
        if n < 2:
            mine = did(mine + after(small_next))
    layer_out = rows_out(layer_keep, layer_far, jnp.bfloat16)
    heads_sum = jnp.concatenate(heads_sums, 1)
    heads_next = swap(heads_sum, 0)
    arrived = cross(jnp.concatenate([mine[:size], mine[2 * size :]]))
    both = mine[2 * size :] + arrived[size:]
    mine = mine[size : 2 * size] + arrived[:size]
    theirs = swap(mine, 0)
    first = jnp.where(bit(0) == 0, mine, theirs)
    second = jnp.where(bit(0) == 0, theirs, mine)
    heads_bias_total = jnp.concatenate([first[:three].reshape(3, -1), second[:three].reshape(3, -1)], 1)
    expand_bias_total = jnp.concatenate([first[three:], second[three:]])
    (first_gain_total, first_shift_total, second_gain_total, second_shift_total, merge_bias_total,
     reduce_bias_total) = both.reshape(6, -1)
    heads_out = place_heads(core, heads_sum, heads_next, jnp.float32)
    return (
        layer_out,
        tokens_out,
        first_gain_total,
        first_shift_total,
        heads_out.transpose(1, 0, 2),
        heads_bias_total,
        in_rows(expand_total[:, :, rows:]),
        merge_bias_total,
        second_gain_total,
        second_shift_total,
        expand_out,
        expand_bias_total,
        reduce_out,
        reduce_bias_total,
    )


def solution(mesh):
    rows = P(None, "dp", "mp", None)
    columns = P(None, "mp")
    heads = P(None, None, "mp")
    return jax.shard_map(
        functools.partial(on_device, mesh.shape["dp"]),
        mesh=mesh,
        in_specs=(
            rows, rows, P(None, "dp"), P(), P(), heads, columns, P("mp", None), P(), P(), P(), columns,
            P("mp"), P("mp", None), P(),
        ),
        out_specs=(
            rows, rows, P(), P(), heads, columns, P("mp", None), P(), P(), P(), columns, P("mp"),
            P("mp", None), P(),
        ),
        check_vma=False,
    )
```

```python
import functools
import math

import jax
import jax.numpy as jnp
from jax import lax
from jax.experimental import pallas as pl
from jax.experimental.pallas import tpu as pltpu
from jax.sharding import PartitionSpec as P

HEAD_DIM = 64
FRAMES = 2
SIDE_SMALL = 16
SIDE_LARGE = 24
EPSILON = 1e-06
ROOT_HALF = 0.7071067811865476
GAUSS_NORM = 0.3989422804014327
LOG2E = math.log2(math.e)
PAIR = 128
NEG = -1e30
STRIPS = ((0, 512, 592), (512, 1024, 1168), (1024, 1280, 1280))
EARLY = 512


def params(mib=50):
    return pltpu.CompilerParams(vmem_limit_bytes=mib * 2**20)


def takes(microseconds):
    return pl.CostEstimate(
        flops=int(microseconds * 4e9), bytes_accessed=int(microseconds * 4e6), transcendentals=0
    )


def low(array):
    return array.astype(jnp.bfloat16)


def wide(array):
    return array.astype(jnp.float32)


def dot(left, right):
    return jnp.dot(left, right, preferred_element_type=jnp.float32)


def dot_nt(left, right):
    return lax.dot_general(
        left, right, (((1,), (1,)), ((), ())), preferred_element_type=jnp.float32
    )


def dot_tn(left, right):
    return lax.dot_general(
        left, right, (((0,), (0,)), ((), ())), preferred_element_type=jnp.float32
    )


def slot_layout(count_one, length):
    large_count = SIDE_LARGE * SIDE_LARGE
    grid_side = jnp.where(count_one == large_count, SIDE_LARGE, SIDE_SMALL).astype(jnp.int32)
    frame_len = grid_side * grid_side + 2
    clip_len = FRAMES * frame_len
    clip_total = jnp.where(count_one == large_count, 1, 2).astype(jnp.int32)
    slot_id = jnp.arange(length, dtype=jnp.int32)
    clip_id = jnp.minimum(slot_id // clip_len, clip_total)
    offset_in = slot_id - clip_id * clip_len
    frame_id = offset_in // frame_len
    place_in = offset_in - frame_id * frame_len - 2
    patch_id = jnp.maximum(place_in, 0)
    is_live = clip_id < clip_total
    is_patch = is_live & (place_in >= 0)
    frame_id = jnp.where(is_live, frame_id, 0)
    patch_row = jnp.where(is_patch, patch_id // grid_side, 0)
    column = jnp.where(is_patch, patch_id - patch_id // grid_side * grid_side, 0)
    first_key = clip_id * clip_len
    past_key = jnp.where(is_live, first_key + (frame_id + 1) * frame_len, length)
    segment = FRAMES * clip_id + frame_id
    starts = [n * frame_len for n in range(FRAMES * 2 + 1)]
    return (first_key, past_key, frame_id, patch_row, column, segment, starts)


def rotary_tables(frame_id, patch_row, column):
    segment = 2 * (HEAD_DIM // 3 // 2)
    half_width = segment // 2
    dim_index = jnp.arange(PAIR, dtype=jnp.int32) % HEAD_DIM
    segment_id = dim_index // segment
    exponent = (dim_index % segment % half_width).astype(jnp.float32)
    frequency = jnp.exp(exponent * (-math.log(10000.0) / half_width))
    pick = lambda number: wide(jnp.where(segment_id == number, 1.0, 0.0))[None, :]
    position = (
        pick(0) * wide(frame_id[:, None])
        + pick(1) * wide(patch_row[:, None])
        + pick(2) * wide(column[:, None])
    )
    angles = position * frequency[None, :]
    lower = (dim_index % segment < half_width)[None, :]
    sine = jnp.where((segment_id < 3)[None, :], jnp.sin(angles), 0.0)
    return (jnp.cos(angles), jnp.where(lower, -sine, 0.0), jnp.where(lower, 0.0, sine))


def spin(x, cos, up, down):
    turn = HEAD_DIM // 3 // 2
    return x * cos + pltpu.roll(x, PAIR - turn, 1) * up + pltpu.roll(x, turn, 1) * down


def standardize(values_in):
    row_mean = jnp.mean(values_in, -1, keepdims=True)
    centred = values_in - row_mean
    norm_scale = lax.rsqrt(jnp.mean(centred * centred, -1, keepdims=True) + EPSILON)
    return (centred * norm_scale, norm_scale)


def fold(x):
    return jnp.sum(x.reshape(x.shape[0] // 8, 8, x.shape[1]), 0)


def whole(array):
    return pl.BlockSpec(array.shape, lambda *_: (0,) * array.ndim, pipeline_mode=pl.Buffered(1))


def enter_kernel(side_ref, mine_ref, arrived_ref, gain_ref, shift_ref, stream_ref, out_ref):
    def step(rows):
        stream_ref[...] = rows
        normed, _ = standardize(wide(rows))
        out_ref[...] = low(normed * gain_ref[...] + shift_ref[...])

    @pl.when(pl.program_id(0) == 0)
    def _():
        step(mine_ref[0])

    @pl.when(pl.program_id(0) == 1)
    def _():
        step(arrived_ref[...])


def enter(side, tokens, arrived, gain, shift):
    _, half, depth = tokens.shape
    vector = pl.BlockSpec((1, depth), lambda i, side: (0, 0))
    out = pl.BlockSpec((half, depth), lambda i, side: (jnp.where(i == 0, side[0], 1 - side[0]), 0))
    return pl.pallas_call(
        enter_kernel,
        grid_spec=pltpu.PrefetchScalarGridSpec(
            num_scalar_prefetch=1,
            grid=(2,),
            in_specs=[
                pl.BlockSpec((1, half, depth), lambda i, side: (side[0], 0, 0)),
                pl.BlockSpec((half, depth), lambda i, side: (0, 0)),
                vector,
                vector,
            ],
            out_specs=[out, out],
        ),
        out_shape=[jax.ShapeDtypeStruct((2 * half, depth), jnp.bfloat16)] * 2,
        compiler_params=params(),
        cost_estimate=takes(5),
        name="enter",
    )(side, tokens, arrived, gain[None], shift[None])


def collect_kernel(side_ref, mine_ref, arrived_ref, out_ref):
    @pl.when(pl.program_id(0) == 0)
    def _():
        out_ref[...] = mine_ref[0]

    @pl.when(pl.program_id(0) == 1)
    def _():
        out_ref[...] = arrived_ref[...]


def collect(side, array, arrived):
    _, half, depth = array.shape
    return pl.pallas_call(
        collect_kernel,
        grid_spec=pltpu.PrefetchScalarGridSpec(
            num_scalar_prefetch=1,
            grid=(2,),
            in_specs=[
                pl.BlockSpec((1, half, depth), lambda i, side: (side[0], 0, 0)),
                pl.BlockSpec((half, depth), lambda i, side: (0, 0)),
            ],
            out_specs=pl.BlockSpec(
                (half, depth), lambda i, side: (jnp.where(i == 0, side[0], 1 - side[0]), 0)
            ),
        ),
        out_shape=jax.ShapeDtypeStruct((2 * half, depth), array.dtype),
        compiler_params=params(),
        cost_estimate=takes(2),
        name="collect",
    )(side, array, arrived)


def project_kernel(chunk, count, x_ref, *refs):
    weights, biases, outs = refs[:count], refs[count : 2 * count], refs[2 * count + 3]
    tables = refs[2 * count : 2 * count + 3]
    for at in range(0, x_ref.shape[0], chunk):
        rows = slice(at, at + chunk)
        cos, up, down = (table[rows, :] for table in tables)
        for number, (w_ref, b_ref) in enumerate(zip(weights, biases)):
            base, width = number * w_ref.shape[1], w_ref.shape[1] // 3
            y = dot(x_ref[rows, :], w_ref[...]) + b_ref[...]
            for lane in range(0, 2 * width, PAIR):
                turned = spin(y[:, lane : lane + PAIR], cos, up, down)
                outs[rows, base + lane : base + lane + PAIR] = low(turned)
            outs[rows, base + 2 * width : base + 3 * width] = low(y[:, 2 * width :])


def project(x, weights, biases, tables, block=640, chunk=320):
    rows, depth = x.shape
    width = weights[0].shape[1] * len(weights)
    biases = [bias[None] for bias in biases]
    row = lambda array: pl.BlockSpec((block, array.shape[1]), lambda i: (i, 0))
    return pl.pallas_call(
        functools.partial(project_kernel, chunk, len(weights)),
        grid=(rows // block,),
        in_specs=[row(x)] + [whole(a) for a in (*weights, *biases)] + [row(t) for t in tables],
        out_specs=pl.BlockSpec((block, width), lambda i: (i, 0)),
        out_shape=jax.ShapeDtypeStruct((rows, width), jnp.bfloat16),
        compiler_params=params(),
        cost_estimate=takes(9),
        name="project",
    )(x, *weights, *biases, *tables)


SEGMENTS = 5
BOUND_LANE = SEGMENTS


def segment_lanes(first_key, past_key, segment, starts):
    lane = jnp.arange(PAIR, dtype=jnp.int32)[None, :] % HEAD_DIM
    start = sum(jnp.where(lane == n, starts[n], 0) for n in range(SEGMENTS))
    inside = (start >= first_key[:, None]) & (start < past_key[:, None])
    for_query = jnp.where((lane < SEGMENTS) & ~inside, NEG, 0.0)
    for_key = jnp.where((lane == segment[:, None]) | (lane == BOUND_LANE), 1.0, 0.0)
    return low(for_query), low(for_key)


def own_lanes(head):
    lane = lax.broadcasted_iota(jnp.int32, (1, PAIR), 1)
    return (lane >= HEAD_DIM) == (head == 1), lane % HEAD_DIM


def attend_strips(shifted, v_ref, out_ref, root_ref, early_ref, late_ref):
    values = v_ref[...].T
    least = None
    for strip in STRIPS:
        first, past, stop = strip
        outs, roots = [], []
        for head in range(2):
            powers = jnp.exp2(shifted(head, strip))
            total = jnp.sum(powers, 0, keepdims=True)
            least = jnp.min(total) if least is None else jnp.minimum(least, jnp.min(total))
            root = 1.0 / total
            powers = low(powers)
            if past <= EARLY:
                early_ref[head, :, first:past] = powers
            else:
                late_ref[head, 0:stop, first - EARLY : past - EARLY] = powers
            rows = slice(head * HEAD_DIM, (head + 1) * HEAD_DIM)
            outs.append(dot(values[rows, 0:stop], powers) * root)
            roots.append(jnp.broadcast_to(root, (HEAD_DIM, past - first)))
        out_ref[first:past, :] = low(jnp.concatenate(outs, 0).T)
        root_ref[first:past, :] = jnp.concatenate(roots, 0).T
    return least


def attend_kernel(
    q_ref, k_ref, v_ref, query_ref, key_ref, lo_ref, hi_ref, out_ref, root_ref, early_ref, late_ref
):
    factor = HEAD_DIM**-0.5 * LOG2E
    squares = wide(k_ref[...]) * wide(k_ref[...])
    keys, longest = [], []
    for head in range(2):
        own, _ = own_lanes(head)
        keys.append(jnp.where(own, k_ref[...], key_ref[...]))
        length = jnp.sum(jnp.where(own, squares, 0.0), 1, keepdims=True)
        longest.append(jnp.max(length, 0, keepdims=True))

    def below_bound(head, strip):
        first, past, stop = strip
        own, lane = own_lanes(head)
        q = q_ref[first:past, :]
        length = jnp.sum(jnp.where(own, wide(q) * wide(q), 0.0), 1, keepdims=True)
        bound = jnp.sqrt(length * longest[head]) * 1.01
        beside = jnp.where(lane == BOUND_LANE, low(-bound), query_ref[first:past, :])
        return dot_nt(keys[head][0:stop], jnp.where(own, q, beside)) * factor

    outs = (v_ref, out_ref, root_ref, early_ref, late_ref)
    least = attend_strips(below_bound, *outs)

    @pl.when(jnp.logical_not(least > 1e-20))
    def _():
        def below_maximum(head, strip):
            first, past, stop = strip
            own, _ = own_lanes(head)
            q = q_ref[first:past, :]
            scores = dot_nt(k_ref[0:stop, :], jnp.where(own, q, jnp.zeros_like(q)))
            key = lax.broadcasted_iota(jnp.int32, scores.shape, 0)
            allowed = (key >= lo_ref[:, first:past]) & (key < hi_ref[:, first:past])
            scores = jnp.where(allowed, scores, NEG)
            return (scores - jnp.max(scores, 0, keepdims=True)) * factor

        attend_strips(below_maximum, *outs)


def kept_specs(rows, base):
    return [
        pl.BlockSpec((2, STRIPS[0][2], EARLY), lambda i: (base + i, 0, 0)),
        pl.BlockSpec((2, rows, rows - EARLY), lambda i: (base + i, 0, 0)),
    ]


QUARTER_PAIRS = 2


def head_specs(rows, base):
    pair = lambda i: (base + i) // QUARTER_PAIRS * 3 * QUARTER_PAIRS + (base + i) % QUARTER_PAIRS
    part = lambda number: pl.BlockSpec((rows, PAIR), lambda i: (0, pair(i) + number * QUARTER_PAIRS))
    return [part(0), part(1), part(2)], pl.BlockSpec((rows, PAIR), lambda i: (0, base + i))


def attend(heads, lanes, first_key, past_key):
    rows, width = heads.shape[0], heads.shape[1] // 3
    pairs = width // PAIR
    parts, block = head_specs(rows, 0)
    beside = (*lanes, first_key, past_key)
    return pl.pallas_call(
        attend_kernel,
        grid=(pairs,),
        in_specs=parts + [whole(array) for array in beside],
        out_specs=[block, block] + kept_specs(rows, 0),
        out_shape=[
            jax.ShapeDtypeStruct((rows, width), jnp.bfloat16),
            jax.ShapeDtypeStruct((rows, width), jnp.float32),
            jax.ShapeDtypeStruct((2 * pairs, STRIPS[0][2], EARLY), jnp.bfloat16),
            jax.ShapeDtypeStruct((2 * pairs, rows, rows - EARLY), jnp.bfloat16),
        ],
        compiler_params=params(),
        cost_estimate=takes(20),
        name="attend",
    )(heads, heads, heads, *beside)


def attend_back_kernel(
    q_ref, k_ref, v_ref, g_ref, o_ref, root_ref, early_ref, late_ref, cos_ref, up_ref, down_ref,
    out_ref, sums_ref, keys_acc, values_acc, queries_acc,
):
    pair = pl.program_id(0)
    pairs = out_ref.shape[1] // (3 * PAIR)
    scale = HEAD_DIM**-0.5
    keys = k_ref[...].T
    values = []
    for head in range(2):
        own, lane = own_lanes(head)
        values.append(jnp.where(own, v_ref[...], low(jnp.where(lane < 3, 1.0, 0.0))))
    for first, past, stop in STRIPS[::-1]:
        q = q_ref[first:past, :]
        g = wide(g_ref[first:past, :]) * root_ref[first:past, :]
        inner = g * wide(o_ref[first:past, :])
        g = low(g)
        zero = jnp.zeros_like(g)
        for head in range(2):
            own, lane = own_lanes(head)
            rows = slice(head * HEAD_DIM, (head + 1) * HEAD_DIM)
            shift = -jnp.sum(jnp.where(own, inner, 0.0), 1, keepdims=True)
            beside = zero
            for number in range(3):
                part = low(shift)
                shift = shift - wide(part)
                beside = jnp.where(lane == number, part, beside)
            if past <= EARLY:
                powers = early_ref[head, :, first:past]
            else:
                powers = late_ref[head, 0:stop, first - EARLY : past - EARLY]
            g_scores = low(wide(powers) * dot_nt(values[head][0:stop], jnp.where(own, g, beside)))
            queries_acc[rows, first:past] = dot(keys[rows, 0:stop], g_scores)
            g_keys = dot(g_scores, jnp.where(own, q, zero))
            g_values = dot(powers, jnp.where(own, g, zero))
            if head == 0:
                total_keys, total_values = g_keys, g_values
            else:
                total_keys, total_values = total_keys + g_keys, total_values + g_values
        if past == STRIPS[-1][1]:
            keys_acc[...] = total_keys
            values_acc[...] = total_values
        else:
            keys_acc[0:stop, :] += total_keys
            values_acc[0:stop, :] += total_values
    cos, up, down = cos_ref[...], -up_ref[...], -down_ref[...]
    grads = (
        low(spin(queries_acc[...].T * scale, cos, up, down)),
        low(spin(keys_acc[...] * scale, cos, up, down)),
        low(values_acc[...]),
    )
    for number, grad in enumerate(grads):
        lanes = pl.ds(pl.multiple_of((number * pairs + pair) * PAIR, PAIR), PAIR)
        out_ref[:, lanes] = grad
        sums_ref[:, lanes] = fold(wide(grad))


def attend_back(quarter, heads, g, out, root, early, late, tables):
    rows, width = g.shape
    pairs = width // PAIR
    parts, block = head_specs(rows, quarter * pairs)
    return pl.pallas_call(
        attend_back_kernel,
        grid=(pairs,),
        in_specs=parts
        + [pl.BlockSpec((rows, PAIR), lambda i: (0, i)), block, block]
        + kept_specs(rows, quarter * pairs)
        + [whole(table) for table in tables],
        out_specs=[
            pl.BlockSpec((rows, 3 * width), lambda i: (0, 0)),
            pl.BlockSpec((8, 3 * width), lambda i: (0, 0)),
        ],
        out_shape=[
            jax.ShapeDtypeStruct((rows, 3 * width), jnp.bfloat16),
            jax.ShapeDtypeStruct((8, 3 * width), jnp.float32),
        ],
        scratch_shapes=[
            pltpu.VMEM((rows, PAIR), jnp.float32),
            pltpu.VMEM((rows, PAIR), jnp.float32),
            pltpu.VMEM((PAIR, rows), jnp.float32),
        ],
        compiler_params=params(56),
        cost_estimate=takes(16),
        name="attend_back",
    )(heads, heads, heads, g, out, root, early, late, *tables)


def merge_kernel(count, *refs):
    rights, lefts = refs[: 2 * count], refs[2 * count : 3 * count]
    x_ref, bias_ref, gain_ref, shift_ref, residual_ref, out_ref = refs[3 * count :]
    total = wide(x_ref[...]) + bias_ref[...]
    for number, right in enumerate(rights):
        left, width = lefts[number // 2], right.shape[0]
        total = total + dot(left[:, number % 2 * width : (number % 2 + 1) * width], right[...])
    residual_ref[...] = total
    normed, _ = standardize(total)
    out_ref[...] = low(normed * gain_ref[...] + shift_ref[...])


def merge(lefts, rights, x, bias, gain, shift, block=320):
    rows, depth = x.shape
    row = lambda array: pl.BlockSpec((block, array.shape[1]), lambda i: (i, 0))
    vectors = (bias[None], gain[None], shift[None])
    return pl.pallas_call(
        functools.partial(merge_kernel, len(lefts)),
        grid=(rows // block,),
        in_specs=[whole(w) for w in rights]
        + [row(a) for a in lefts]
        + [row(x)]
        + [whole(v) for v in vectors],
        out_specs=[row(x), row(x)],
        out_shape=[
            jax.ShapeDtypeStruct((rows, depth), jnp.float32),
            jax.ShapeDtypeStruct((rows, depth), jnp.bfloat16),
        ],
        compiler_params=params(),
        cost_estimate=takes(8),
        name="merge",
    )(*rights, *lefts, x, *vectors)


def expand_kernel(chunk, count, x_ref, *refs):
    weights, biases = refs[:count], refs[count : 2 * count]
    actives, slopes = refs[2 * count : 3 * count], refs[3 * count :]
    for w_ref, b_ref, active_ref, slope_ref in zip(weights, biases, actives, slopes):
        for at in range(0, x_ref.shape[0], chunk):
            rows = slice(at, at + chunk)
            v = dot(x_ref[rows, :], w_ref[...]) + b_ref[...]
            below = 0.5 + 0.5 * lax.erf(v * ROOT_HALF)
            active_ref[rows, :] = low(v * below)
            slope_ref[rows, :] = low(below + v * jnp.exp(-0.5 * v * v) * GAUSS_NORM)


def expand(x, weights, biases, block=512, chunk=256):
    rows, depth = x.shape
    count, width = len(weights), weights[0].shape[1]
    column = lambda size: pl.BlockSpec((size, block), lambda i: (0, i))
    return pl.pallas_call(
        functools.partial(expand_kernel, chunk, count),
        grid=(width // block,),
        in_specs=[whole(x)] + [column(depth)] * count + [column(1)] * count,
        out_specs=[column(rows)] * (2 * count),
        out_shape=[jax.ShapeDtypeStruct((rows, width), jnp.bfloat16)] * (2 * count),
        compiler_params=params(),
        cost_estimate=takes(14),
        name="expand",
    )(x, *weights, *[bias[None] for bias in biases])


def reduce_kernel(count, half, side_ref, *refs):
    rights, lefts = refs[:count], refs[count : 2 * count]
    x_ref, bias_ref, send_ref, keep_ref = refs[2 * count :]
    total = x_ref[...] + bias_ref[...]
    for left, right in zip(lefts, rights):
        total = total + dot(left[...], right[...])

    @pl.when(pl.program_id(0) < half)
    def _():
        send_ref[...] = low(total)

    @pl.when(pl.program_id(0) >= half)
    def _():
        keep_ref[...] = low(total)


def reduce_rows(side, lefts, rights, x, bias, block=320):
    rows, depth = x.shape
    half = rows // 2 // block
    at = lambda i, side: jnp.where(i < half, (1 - side[0]) * half + i, side[0] * half + i - half)
    row = lambda array: pl.BlockSpec((block, array.shape[1]), lambda i, side: (at(i, side), 0))
    return pl.pallas_call(
        functools.partial(reduce_kernel, len(lefts), half),
        grid_spec=pltpu.PrefetchScalarGridSpec(
            num_scalar_prefetch=1,
            grid=(2 * half,),
            in_specs=[whole(w) for w in rights]
            + [row(a) for a in lefts]
            + [row(x), whole(bias[None])],
            out_specs=[
                pl.BlockSpec((block, depth), lambda i, side: (jnp.minimum(i, half - 1), 0)),
                pl.BlockSpec((block, depth), lambda i, side: (jnp.maximum(i - half, 0), 0)),
            ],
        ),
        out_shape=[jax.ShapeDtypeStruct((rows // 2, depth), jnp.bfloat16)] * 2,
        compiler_params=params(),
        cost_estimate=takes(0.1),
        name="reduce_rows",
    )(side, *rights, *lefts, x, bias[None])


def back_kernel(count, at_ref, *refs):
    rights, lefts = refs[:count], refs[count : 2 * count]
    base_ref, above_ref, gain_ref, out_ref, sums_ref = refs[2 * count :]

    @pl.when(pl.program_id(0) == 0)
    def _():
        sums_ref[...] = jnp.zeros_like(sums_ref)

    g = dot_nt(lefts[0][...], rights[0][...])
    for left, right in zip(lefts[1:], rights[1:]):
        g = g + dot_nt(left[...], right[...])
    normed, scale = standardize(wide(base_ref[...]))
    u = g * gain_ref[...]
    above = wide(above_ref[...])
    inner = jnp.mean(u, -1, keepdims=True) + normed * jnp.mean(u * normed, -1, keepdims=True)
    out = low(above + scale * (u - inner))
    out_ref[...] = out
    sums_ref[0] += fold(g * normed)
    sums_ref[1] += fold(g)
    sums_ref[2] += fold(wide(out))
    sums_ref[3] += fold(above)


def back_norm(at, lefts, rights, base, above, gain, block=320):
    rows, depth = base.shape
    row = lambda array: pl.BlockSpec((block, array.shape[1]), lambda i, at: (at[i], 0))
    return pl.pallas_call(
        functools.partial(back_kernel, len(lefts)),
        grid_spec=pltpu.PrefetchScalarGridSpec(
            num_scalar_prefetch=1,
            grid=(at.size,),
            in_specs=[whole(w) for w in rights]
            + [row(a) for a in lefts]
            + [row(base), row(above), whole(gain[None])],
            out_specs=[
                pl.BlockSpec((block, depth), lambda i, at: (i, 0)),
                pl.BlockSpec((4, 8, depth), lambda i, at: (0, 0, 0)),
            ],
        ),
        out_shape=[
            jax.ShapeDtypeStruct((rows, depth), jnp.bfloat16),
            jax.ShapeDtypeStruct((4, 8, depth), jnp.float32),
        ],
        compiler_params=params(),
        cost_estimate=takes(0.1 if base.dtype == jnp.float32 else 20),
        name="back_norm",
    )(at, *rights, *lefts, base, above, gain[None])


def place_kernel(steps, flag_ref, mine_ref, theirs_ref, out_ref):
    @pl.when(pl.program_id(0) < steps)
    def _():
        out_ref[...] = mine_ref[...].astype(out_ref.dtype).reshape(out_ref.shape)

    @pl.when(pl.program_id(0) >= steps)
    def _():
        out_ref[...] = theirs_ref[...].astype(out_ref.dtype).reshape(out_ref.shape)


def place(flag, mine, theirs, steps, in_block, in_index, out_shape, out_block, out_index, dtype):
    def target(i, flag):
        return out_index(jnp.where(i < steps, flag[0], 1 - flag[0]), jnp.where(i < steps, i, i - steps))

    return pl.pallas_call(
        functools.partial(place_kernel, steps),
        grid_spec=pltpu.PrefetchScalarGridSpec(
            num_scalar_prefetch=1,
            grid=(2 * steps,),
            in_specs=[
                pl.BlockSpec(in_block, lambda i, flag: in_index(jnp.minimum(i, steps - 1))),
                pl.BlockSpec(in_block, lambda i, flag: in_index(jnp.maximum(i - steps, 0))),
            ],
            out_specs=pl.BlockSpec(out_block, target),
        ),
        out_shape=jax.ShapeDtypeStruct(out_shape, dtype),
        compiler_params=params(),
        cost_estimate=takes(4),
        name="place",
    )(flag, mine, theirs)


def place_rows(flag, mine, theirs, steps, dtype):
    rows, width = mine.shape
    block = (rows // steps, width)
    return place(
        flag, mine, theirs, steps, block, lambda j: (j, 0),
        (2 * rows, width), block, lambda half, j: (half * steps + j, 0), dtype,
    )


def place_columns(flag, mine, theirs, steps, dtype):
    rows, width = mine.shape
    block = (rows // steps, width)
    return place(
        flag, mine, theirs, steps, block, lambda j: (j, 0),
        (rows, 2 * width), block, lambda half, j: (j, half), dtype,
    )


def place_heads(flag, mine, theirs, dtype):
    rows, width = mine.shape[0], mine.shape[1] // 3
    return place(
        flag, mine, theirs, 3, (rows, width), lambda j: (0, j),
        (3, rows, 2 * width), (1, rows, width), lambda half, j: (j, 0, half), dtype,
    )


def column_sums(matrix):
    unit_column = jnp.ones((matrix.shape[0],), matrix.dtype)
    return jnp.dot(unit_column, matrix, preferred_element_type=jnp.float32)


KEEP, SEND = 0, 1
OWN, FAR = 0, 1
QUARTERS = ((FAR, SEND), (FAR, KEEP), (OWN, SEND), (OWN, KEEP))


def on_device(
    spread,
    tokens,
    cotangent,
    patch_count,
    first_gain,
    first_shift,
    heads_weight,
    heads_bias,
    merge_weight,
    merge_bias,
    second_gain,
    second_shift,
    expand_weight,
    expand_bias,
    reduce_weight,
    reduce_bias,
):
    levels = spread.bit_length() - 1
    rest = list(range(1, levels))
    chunks = spread // 2
    location = lax.axis_index("dp")
    side = lax.axis_index("mp")
    sides = side[None].astype(jnp.int32)
    previous = []

    def bit(level):
        return (location >> level) & 1

    core = bit(0)[None].astype(jnp.int32)

    def tie(array, *others):
        return lax.optimization_barrier((array,) + others)[0] if others else array

    def after(array):
        return tie(array, *previous)

    def did(*arrays):
        previous[:] = arrays
        return arrays[0] if len(arrays) == 1 else arrays

    def swap(array, level):
        return lax.ppermute(array, "dp", [(i, i ^ (1 << level)) for i in range(spread)])

    def cross(array):
        return lax.ppermute(array, "mp", [(0, 1), (1, 0)])

    def half_of(array, flag, axis=0):
        size = array.shape[axis] // 2
        return lax.dynamic_slice_in_dim(array, flag * size, size, axis)

    def chunk_of(array):
        size = array.shape[0] // chunks
        return lax.dynamic_slice_in_dim(array, (location >> 1) * size, size, 0)

    def split(array, level, open_levels=None):
        left = 1 << sum(other > level for other in (open_levels or rest))
        four = array.reshape(left, 2, -1, array.shape[1])
        part = lambda flag: lax.dynamic_index_in_dim(four, flag, 1, False).reshape(-1, array.shape[1])
        return part(bit(level)), part(1 - bit(level))

    def join(mine, theirs, level, open_levels=None):
        left = 1 << sum(other > level for other in (open_levels or rest))
        four = lambda array: array.reshape(left, 1, -1, array.shape[1])
        pair = jnp.where(
            bit(level) == 0,
            jnp.concatenate([four(mine), four(theirs)], 1),
            jnp.concatenate([four(theirs), four(mine)], 1),
        )
        return pair.reshape(-1, mine.shape[1])

    def quarters_of(own, axis):
        return [half_of(own, bit(0), axis), half_of(own, 1 - bit(0), axis)]

    tokens, cotangent = tokens[:, 0], cotangent[:, 0]
    heads_three = heads_weight.transpose(1, 0, 2)
    near = rest[:2]
    piece_rows = heads_three.shape[1] >> len(near)
    piece_width = heads_three.shape[2] // 2
    piece_at = ((location >> 1) & ((1 << len(near)) - 1)) * piece_rows
    heads_piece = jnp.concatenate(
        [
            lax.dynamic_slice(
                heads_three, (n, piece_at, bit(0) * piece_width), (1, piece_rows, piece_width)
            )[0]
            for n in range(3)
        ],
        1,
    )
    heads_cross = cross(heads_piece)
    tokens_far = cross(lax.dynamic_index_in_dim(tie(tokens, heads_piece), 1 - side, 0, False))
    heads_own = [
        jnp.concatenate([half_of(heads_three[n], flag, 1) for n in range(3)], 1)
        for flag in (bit(0), 1 - bit(0))
    ]
    merge_own = quarters_of(merge_weight, 0)
    expand_own = quarters_of(expand_weight, 1)
    reduce_own = quarters_of(reduce_weight, 0)
    pack = lambda hb, eb: jnp.concatenate([hb.reshape(-1), eb])
    bias_own = [
        pack(half_of(heads_bias, flag, 1), half_of(expand_bias, flag)) for flag in (bit(0), 1 - bit(0))
    ]
    three = heads_bias.size // 2
    up_piece = jnp.concatenate([chunk_of(expand_own[KEEP]), chunk_of(merge_own[KEEP])])
    down_piece = chunk_of(reduce_own[KEEP])

    count_one = lax.dynamic_index_in_dim(patch_count[:, 0], side, 0, False)
    length = 2 * tokens.shape[1]
    first_key, past_key, frame_id, patch_row, column, segment, starts = slot_layout(count_one, length)
    tables = rotary_tables(frame_id, patch_row, column)
    lanes = segment_lanes(first_key, past_key, segment, starts)
    first_key, past_key = first_key[None], past_key[None]

    bias_pieces = jnp.concatenate(bias_own)
    did(*heads_own, *merge_own)
    heads_piece = did(after(heads_cross))
    if len(near) > 1:
        heads_next = swap(heads_piece, near[1])
        expand_own = quarters_of(after(expand_weight), 1)
        up_piece = jnp.concatenate([chunk_of(expand_own[KEEP]), chunk_of(merge_own[KEEP])])
        did(*expand_own, up_piece)
        heads_piece = did(join(after(heads_piece), heads_next, near[1], near[1:]))
    heads_next = swap(heads_piece, near[0])
    up_piece = cross(tie(up_piece, heads_piece))
    bias_both = cross(tie(bias_pieces, heads_piece))
    did(heads_piece, down_piece, *heads_own, *merge_own, *expand_own, *reduce_own, *tables, *lanes)
    bias_far = [bias_both[: bias_both.size // 2], bias_both[bias_both.size // 2 :]]
    stream, first_out = did(*enter(sides, after(tokens), tokens_far, first_gain, first_shift))
    heads, seen = {}, {}
    heads_all = [heads_own, None]
    bias_all = (bias_own, bias_far)

    def look(p):
        biases = [bias[:three] for bias in bias_all[p]]
        heads[p] = did(project(after(first_out), heads_all[p], biases, tables))

    def attention(p):
        seen[p] = did(*attend(after(heads[p]), lanes, first_key, past_key))

    def gathered(array, *splits):
        array = lax.all_gather(array, "dp", axis=0, tiled=True)
        array = array.reshape(chunks, 2, -1, array.shape[1])
        quarters, at = [], 0
        for size in splits:
            part = array[:, :, at : at + size]
            quarters.append(
                [
                    lax.dynamic_index_in_dim(part, flag, 1, False).reshape(-1, array.shape[3])
                    for flag in (bit(0), 1 - bit(0))
                ]
            )
            at += size
        return quarters

    look(OWN)
    up_sizes = (expand_own[0].shape[0] // chunks, merge_own[0].shape[0] // chunks)
    up_gathered = gathered(after(up_piece), *up_sizes)
    down_piece = cross(after(down_piece))
    heads_piece = did(join(after(heads_piece), heads_next, near[0], near))
    heads_all[FAR] = [heads_piece, swap(heads_piece, 0)]
    attention(OWN)
    cotangent_far = cross(after(lax.dynamic_index_in_dim(cotangent, 1 - side, 0, False)))
    look(FAR)
    (reduce_far,) = gathered(after(down_piece), down_piece.shape[0])
    attention(FAR)
    expand_far, merge_far = ([after(q) for q in quarters] for quarters in up_gathered)
    merge_all = (merge_own, merge_far)
    expand_all = (expand_own, expand_far)
    reduce_all = (reduce_own, reduce_far)
    width = seen[OWN][0].shape[1] // 2
    residual, second_out = did(
        *merge(
            [seen[OWN][0], seen[FAR][0]], [merge_all[p][c] for p in (OWN, FAR) for c in (KEEP, SEND)],
            after(stream), merge_bias, second_gain, second_shift,
        )
    )
    grad_two = did(collect(sides, after(cotangent), cotangent_far))

    active, slope, grad_pre = {}, {}, {}

    def widen(p):
        active[p, KEEP], active[p, SEND], slope[p, KEEP], slope[p, SEND] = did(
            *expand(after(second_out), expand_all[p], [bias[three:] for bias in bias_all[p]])
        )

    def back_active(p, c):
        grad_pre[p, c] = did(low(dot_nt(after(grad_two), reduce_all[p][c]) * wide(slope[p, c])))

    def product(left, right, *arrived):
        total = dot_tn(after(left), right)
        for array in arrived:
            total = total + wide(array)
        return did(low(total))

    def scattered(array, level, open_levels=None):
        keep, send = split(after(array), level, open_levels or rest[rest.index(level) :])
        did(send)
        return keep, swap(send, level)

    def summed(keep, arrived):
        return did(low(wide(after(keep)) + wide(arrived)))

    def rows_out(keep, arrived, dtype):
        return place_rows(sides, keep, arrived, 1, dtype).reshape(2, 1, length // 2, -1)

    widen(FAR)
    sent = swap(product(active[FAR, SEND], grad_two), 0)
    widen(OWN)
    reduce_far_sum = product(active[FAR, KEEP], grad_two, sent)
    reduce_cross = cross(reduce_far_sum)
    sent = swap(product(active[OWN, SEND], grad_two), 0)
    back_active(FAR, SEND)
    reduce_sum = product(active[OWN, KEEP], grad_two, sent)
    back_active(FAR, KEEP)
    sent = swap(product(second_out, grad_pre[FAR, SEND]), 0)
    back_active(OWN, SEND)
    expand_far_sum = product(second_out, grad_pre[FAR, KEEP], sent)
    back_active(OWN, KEEP)
    sent = swap(product(second_out, grad_pre[OWN, SEND]), 0)
    expand_sum = product(second_out, grad_pre[OWN, KEEP], sent)
    expand_cross = cross(expand_far_sum)
    blocks = jnp.arange(length // 320, dtype=jnp.int32)
    grad_one, second_sums = did(
        *back_norm(
            blocks, [grad_pre[q] for q in QUARTERS], [expand_all[p][c] for p, c in QUARTERS],
            after(residual), grad_two, second_gain,
        )
    )
    grad_mixed, grad_heads, head_sums = {}, {}, {}

    def back_mixed(p, c):
        grad_mixed[p, c] = did(low(dot_nt(after(grad_one), merge_all[p][c])))

    def back_attention(q):
        p, c = q
        grad_heads[q], sums = did(
            *attend_back(c, heads[p], after(grad_mixed[q]), *seen[p], tables)
        )
        head_sums[q] = jnp.sum(sums, 0)

    merge_far_sum = product(seen[FAR][0], grad_one)
    sent_far = swap(merge_far_sum[width:], 0)
    merge_sum = product(seen[OWN][0], grad_one)
    sent_own = swap(merge_sum[width:], 0)
    for p, c in QUARTERS:
        back_mixed(p, c)
    merge_far_sum = summed(merge_far_sum[:width], sent_far)
    merge_sum = summed(merge_sum[:width], sent_own)
    merge_cross = cross(tie(merge_far_sum, reduce_cross))
    reduce_sum = summed(reduce_sum, reduce_cross)
    reduce_keep, reduce_next = scattered(reduce_sum, rest[0])
    back_attention((FAR, SEND))
    reduce_sum = summed(reduce_keep, reduce_next)
    reduce_keep, reduce_next = scattered(reduce_sum, rest[1])
    sent = swap(product(first_out, grad_heads[FAR, SEND]), 0)
    expand_sum = summed(expand_sum, expand_cross)
    expand_keep, expand_next = scattered(expand_sum, rest[0])
    merge_sum = summed(merge_sum, merge_cross)
    merge_keep, merge_next = scattered(merge_sum, rest[0])
    reduce_sum = summed(reduce_keep, reduce_next)
    for level in rest[2:]:
        reduce_keep, reduce_next = scattered(reduce_sum, level)
        reduce_sum = low(wide(reduce_keep) + wide(reduce_next))
    back_attention((FAR, KEEP))
    reduce_total = lax.all_gather(after(reduce_sum), "dp", axis=0, tiled=True)
    heads_far_sum = product(first_out, grad_heads[FAR, KEEP], sent)
    heads_cross = cross(heads_far_sum)
    expand_sum = summed(expand_keep, expand_next)
    merge_sum = summed(merge_keep, merge_next)
    expand_keep, expand_next = scattered(expand_sum, rest[1])
    merge_keep, merge_next = scattered(merge_sum, rest[1])
    back_attention((OWN, SEND))
    expand_sum = summed(expand_keep, expand_next)
    merge_sum = summed(merge_keep, merge_next)
    for level in rest[2:]:
        expand_keep, expand_next = scattered(expand_sum, level)
        merge_keep, merge_next = scattered(merge_sum, level)
        expand_sum = low(wide(expand_keep) + wide(expand_next))
        merge_sum = low(wide(merge_keep) + wide(merge_next))
    sent = swap(product(first_out, grad_heads[OWN, SEND]), 0)
    back_attention((OWN, KEEP))
    expand_total = lax.all_gather(
        after(jnp.concatenate([expand_sum, merge_sum])), "dp", axis=0, tiled=True
    )
    heads_sum = product(first_out, grad_heads[OWN, KEEP], sent, heads_cross)
    orders = [rest[:1] + rest[2:] + rest[1:2], rest[1:2] + rest[:1] + rest[2:]]
    middle = heads_sum.shape[1] // 2
    heads_sums = [heads_sum[:, :middle], heads_sum[:, middle:]]

    def both_scattered(n):
        return [scattered(total, order[n], order[n:]) for total, order in zip(heads_sums, orders)]

    def both_summed(pairs):
        return [summed(*pair) for pair in pairs]

    def in_rows(array):
        return wide(array.transpose(1, 0, 2, 3).reshape(-1, array.shape[3]))

    reduce_total = reduce_total.reshape(chunks, 2, -1, reduce_total.shape[1])
    expand_total = expand_total.reshape(chunks, 2, -1, expand_total.shape[1])
    rows = expand_sum.shape[0]

    pairs = both_scattered(0)
    lefts = [grad_heads[q] for q in QUARTERS]
    rights = [heads_all[p][c] for p, c in QUARTERS]
    half = length // 2
    blocks = (blocks + (1 - sides) * (half // 320)) % (length // 320)
    tokens_rows, first_sums = did(
        *back_norm(blocks, lefts, rights, stream, grad_one, after(first_gain))
    )
    tokens_cross, tokens_keep = cross(tokens_rows[:half]), tokens_rows[half:]
    heads_sums = both_summed(pairs)
    pairs = both_scattered(1)

    small = {q: jnp.concatenate([head_sums[q], column_sums(grad_pre[q])]) for q in QUARTERS}
    both = jnp.concatenate(
        [
            jnp.sum(part, 0)
            for part in (
                first_sums[0], first_sums[1], second_sums[0], second_sums[1], second_sums[2], second_sums[3],
            )
        ]
    )
    far_send, own_send, both = did(*(after(v) for v in (small[FAR, SEND], small[OWN, SEND], both)))
    arrived = swap(jnp.concatenate([far_send, own_send, both]), 0)
    size = own_send.size
    layer_send, layer_keep = did(
        *reduce_rows(
            sides, [active[q] for q in QUARTERS], [reduce_all[p][c] for p, c in QUARTERS],
            after(residual), reduce_bias,
        )
    )
    heads_sums = both_summed(pairs)
    mine = jnp.concatenate([small[FAR, KEEP] + arrived[:size], small[OWN, KEEP], both])
    mine = did(
        jnp.concatenate([mine[:size], mine[size:] + after(arrived)[size:]])
    )
    for n in range(2, len(rest) - 1):
        pairs = both_scattered(n)
        small_next = swap(mine, rest[n])
        heads_sums = both_summed(pairs)
        mine = did(mine + after(small_next))
    arrived = [swap(total, order[-1]) for total, order in zip(heads_sums, orders)]
    small_next = swap(mine, rest[-1])
    reduce_out = in_rows(after(reduce_total))
    mine, reduce_out = lax.optimization_barrier((mine, reduce_out))
    did(mine)
    heads_sums = both_summed(zip(heads_sums, arrived))
    mine = did(mine + after(small_next))
    layer_far = cross(tie(layer_send, tokens_cross))
    for n in range(len(rest) - 1)[::-1]:
        arrived = [swap(total, order[n]) for total, order in zip(heads_sums, orders)]
        small_next = swap(mine, rest[n]) if n < 2 else None
        if n == len(rest) - 2:
            tokens_out = rows_out(after(tokens_keep), tokens_cross, jnp.float32)
            mine, tokens_out = lax.optimization_barrier((mine, tokens_out))
            did(mine)
        if n == 0:
            expand_out = wide(
                jnp.concatenate(
                    [
                        after(expand_total)[:, half, :rows].reshape(-1, expand_total.shape[3])
                        for half in range(2)
                    ],
                    1,
                )
            )
            mine, expand_out = lax.optimization_barrier((mine, expand_out))
            did(mine)
        heads_sums = [
            did(join(after(total), other, order[n], order[n:]))
            for total, other, order in zip(heads_sums, arrived, orders)
        ]
        if n < 2:
            mine = did(mine + after(small_next))
    layer_out = rows_out(layer_keep, layer_far, jnp.bfloat16)
    heads_sum = jnp.concatenate(heads_sums, 1)
    heads_next = swap(heads_sum, 0)
    arrived = cross(jnp.concatenate([mine[:size], mine[2 * size :]]))
    both = mine[2 * size :] + arrived[size:]
    mine = mine[size : 2 * size] + arrived[:size]
    theirs = swap(mine, 0)
    first = jnp.where(bit(0) == 0, mine, theirs)
    second = jnp.where(bit(0) == 0, theirs, mine)
    heads_bias_total = jnp.concatenate([first[:three].reshape(3, -1), second[:three].reshape(3, -1)], 1)
    expand_bias_total = jnp.concatenate([first[three:], second[three:]])
    (first_gain_total, first_shift_total, second_gain_total, second_shift_total, merge_bias_total,
     reduce_bias_total) = both.reshape(6, -1)
    heads_out = place_heads(core, heads_sum, heads_next, jnp.float32)
    return (
        layer_out,
        tokens_out,
        first_gain_total,
        first_shift_total,
        heads_out.transpose(1, 0, 2),
        heads_bias_total,
        in_rows(expand_total[:, :, rows:]),
        merge_bias_total,
        second_gain_total,
        second_shift_total,
        expand_out,
        expand_bias_total,
        reduce_out,
        reduce_bias_total,
    )


def solution(mesh):
    rows = P(None, "dp", "mp", None)
    columns = P(None, "mp")
    heads = P(None, None, "mp")
    return jax.shard_map(
        functools.partial(on_device, mesh.shape["dp"]),
        mesh=mesh,
        in_specs=(
            rows, rows, P(None, "dp"), P(), P(), heads, columns, P("mp", None), P(), P(), P(), columns,
            P("mp"), P("mp", None), P(),
        ),
        out_specs=(
            rows, rows, P(), P(), heads, columns, P("mp", None), P(), P(), P(), columns, P("mp"),
            P("mp", None), P(),
        ),
        check_vma=False,
    )
```

```python
import functools
import math

import jax
import jax.numpy as jnp
from jax import lax
from jax.experimental import pallas as pl
from jax.experimental.pallas import tpu as pltpu
from jax.sharding import PartitionSpec as P

HEAD_DIM = 64
FRAMES = 2
SIDE_SMALL = 16
SIDE_LARGE = 24
EPSILON = 1e-06
ROOT_HALF = 0.7071067811865476
GAUSS_NORM = 0.3989422804014327
LOG2E = math.log2(math.e)
PAIR = 128
NEG = -1e30
STRIPS = ((0, 512, 592), (512, 1024, 1168), (1024, 1280, 1280))
EARLY = 512


def params(mib=50):
    return pltpu.CompilerParams(vmem_limit_bytes=mib * 2**20)


def takes(microseconds):
    return pl.CostEstimate(
        flops=int(microseconds * 4e9), bytes_accessed=int(microseconds * 4e6), transcendentals=0
    )


def low(array):
    return array.astype(jnp.bfloat16)


def wide(array):
    return array.astype(jnp.float32)


def dot(left, right):
    return jnp.dot(left, right, preferred_element_type=jnp.float32)


def dot_nt(left, right):
    return lax.dot_general(
        left, right, (((1,), (1,)), ((), ())), preferred_element_type=jnp.float32
    )


def dot_tn(left, right):
    return lax.dot_general(
        left, right, (((0,), (0,)), ((), ())), preferred_element_type=jnp.float32
    )


def slot_layout(count_one, length):
    large_count = SIDE_LARGE * SIDE_LARGE
    grid_side = jnp.where(count_one == large_count, SIDE_LARGE, SIDE_SMALL).astype(jnp.int32)
    frame_len = grid_side * grid_side + 2
    clip_len = FRAMES * frame_len
    clip_total = jnp.where(count_one == large_count, 1, 2).astype(jnp.int32)
    slot_id = jnp.arange(length, dtype=jnp.int32)
    clip_id = jnp.minimum(slot_id // clip_len, clip_total)
    offset_in = slot_id - clip_id * clip_len
    frame_id = offset_in // frame_len
    place_in = offset_in - frame_id * frame_len - 2
    patch_id = jnp.maximum(place_in, 0)
    is_live = clip_id < clip_total
    is_patch = is_live & (place_in >= 0)
    frame_id = jnp.where(is_live, frame_id, 0)
    patch_row = jnp.where(is_patch, patch_id // grid_side, 0)
    column = jnp.where(is_patch, patch_id - patch_id // grid_side * grid_side, 0)
    first_key = clip_id * clip_len
    past_key = jnp.where(is_live, first_key + (frame_id + 1) * frame_len, length)
    segment = FRAMES * clip_id + frame_id
    starts = [n * frame_len for n in range(FRAMES * 2 + 1)]
    return (first_key, past_key, frame_id, patch_row, column, segment, starts)


def rotary_tables(frame_id, patch_row, column):
    segment = 2 * (HEAD_DIM // 3 // 2)
    half_width = segment // 2
    dim_index = jnp.arange(PAIR, dtype=jnp.int32) % HEAD_DIM
    segment_id = dim_index // segment
    exponent = (dim_index % segment % half_width).astype(jnp.float32)
    frequency = jnp.exp(exponent * (-math.log(10000.0) / half_width))
    pick = lambda number: wide(jnp.where(segment_id == number, 1.0, 0.0))[None, :]
    position = (
        pick(0) * wide(frame_id[:, None])
        + pick(1) * wide(patch_row[:, None])
        + pick(2) * wide(column[:, None])
    )
    angles = position * frequency[None, :]
    lower = (dim_index % segment < half_width)[None, :]
    sine = jnp.where((segment_id < 3)[None, :], jnp.sin(angles), 0.0)
    return (jnp.cos(angles), jnp.where(lower, -sine, 0.0), jnp.where(lower, 0.0, sine))


def spin(x, cos, up, down):
    turn = HEAD_DIM // 3 // 2
    return x * cos + pltpu.roll(x, PAIR - turn, 1) * up + pltpu.roll(x, turn, 1) * down


def standardize(values_in):
    row_mean = jnp.mean(values_in, -1, keepdims=True)
    centred = values_in - row_mean
    norm_scale = lax.rsqrt(jnp.mean(centred * centred, -1, keepdims=True) + EPSILON)
    return (centred * norm_scale, norm_scale)


def fold(x):
    return jnp.sum(x.reshape(x.shape[0] // 8, 8, x.shape[1]), 0)


def whole(array):
    return pl.BlockSpec(array.shape, lambda *_: (0,) * array.ndim, pipeline_mode=pl.Buffered(1))


def enter_kernel(side_ref, mine_ref, arrived_ref, gain_ref, shift_ref, stream_ref, out_ref):
    def step(rows):
        stream_ref[...] = rows
        normed, _ = standardize(wide(rows))
        out_ref[...] = low(normed * gain_ref[...] + shift_ref[...])

    @pl.when(pl.program_id(0) == 0)
    def _():
        step(mine_ref[0])

    @pl.when(pl.program_id(0) == 1)
    def _():
        step(arrived_ref[...])


def enter(side, tokens, arrived, gain, shift):
    _, half, depth = tokens.shape
    vector = pl.BlockSpec((1, depth), lambda i, side: (0, 0))
    out = pl.BlockSpec((half, depth), lambda i, side: (jnp.where(i == 0, side[0], 1 - side[0]), 0))
    return pl.pallas_call(
        enter_kernel,
        grid_spec=pltpu.PrefetchScalarGridSpec(
            num_scalar_prefetch=1,
            grid=(2,),
            in_specs=[
                pl.BlockSpec((1, half, depth), lambda i, side: (side[0], 0, 0)),
                pl.BlockSpec((half, depth), lambda i, side: (0, 0)),
                vector,
                vector,
            ],
            out_specs=[out, out],
        ),
        out_shape=[jax.ShapeDtypeStruct((2 * half, depth), jnp.bfloat16)] * 2,
        compiler_params=params(),
        cost_estimate=takes(5),
        name="enter",
    )(side, tokens, arrived, gain[None], shift[None])


def collect_kernel(side_ref, mine_ref, arrived_ref, out_ref):
    @pl.when(pl.program_id(0) == 0)
    def _():
        out_ref[...] = mine_ref[0]

    @pl.when(pl.program_id(0) == 1)
    def _():
        out_ref[...] = arrived_ref[...]


def collect(side, array, arrived):
    _, half, depth = array.shape
    return pl.pallas_call(
        collect_kernel,
        grid_spec=pltpu.PrefetchScalarGridSpec(
            num_scalar_prefetch=1,
            grid=(2,),
            in_specs=[
                pl.BlockSpec((1, half, depth), lambda i, side: (side[0], 0, 0)),
                pl.BlockSpec((half, depth), lambda i, side: (0, 0)),
            ],
            out_specs=pl.BlockSpec(
                (half, depth), lambda i, side: (jnp.where(i == 0, side[0], 1 - side[0]), 0)
            ),
        ),
        out_shape=jax.ShapeDtypeStruct((2 * half, depth), array.dtype),
        compiler_params=params(),
        cost_estimate=takes(2),
        name="collect",
    )(side, array, arrived)


def project_kernel(chunk, count, x_ref, *refs):
    weights, biases, outs = refs[:count], refs[count : 2 * count], refs[2 * count + 3]
    tables = refs[2 * count : 2 * count + 3]
    for at in range(0, x_ref.shape[0], chunk):
        rows = slice(at, at + chunk)
        cos, up, down = (table[rows, :] for table in tables)
        for number, (w_ref, b_ref) in enumerate(zip(weights, biases)):
            base, width = number * w_ref.shape[1], w_ref.shape[1] // 3
            y = dot(x_ref[rows, :], w_ref[...]) + b_ref[...]
            for lane in range(0, 2 * width, PAIR):
                turned = spin(y[:, lane : lane + PAIR], cos, up, down)
                outs[rows, base + lane : base + lane + PAIR] = low(turned)
            outs[rows, base + 2 * width : base + 3 * width] = low(y[:, 2 * width :])


def project(x, weights, biases, tables, block=640, chunk=320):
    rows, depth = x.shape
    width = weights[0].shape[1] * len(weights)
    biases = [bias[None] for bias in biases]
    row = lambda array: pl.BlockSpec((block, array.shape[1]), lambda i: (i, 0))
    return pl.pallas_call(
        functools.partial(project_kernel, chunk, len(weights)),
        grid=(rows // block,),
        in_specs=[row(x)] + [whole(a) for a in (*weights, *biases)] + [row(t) for t in tables],
        out_specs=pl.BlockSpec((block, width), lambda i: (i, 0)),
        out_shape=jax.ShapeDtypeStruct((rows, width), jnp.bfloat16),
        compiler_params=params(),
        cost_estimate=takes(9),
        name="project",
    )(x, *weights, *biases, *tables)


SEGMENTS = 5
BOUND_LANE = SEGMENTS


def segment_lanes(first_key, past_key, segment, starts):
    lane = jnp.arange(PAIR, dtype=jnp.int32)[None, :] % HEAD_DIM
    start = sum(jnp.where(lane == n, starts[n], 0) for n in range(SEGMENTS))
    inside = (start >= first_key[:, None]) & (start < past_key[:, None])
    for_query = jnp.where((lane < SEGMENTS) & ~inside, NEG, 0.0)
    for_key = jnp.where((lane == segment[:, None]) | (lane == BOUND_LANE), 1.0, 0.0)
    return low(for_query), low(for_key)


def own_lanes(head):
    lane = lax.broadcasted_iota(jnp.int32, (1, PAIR), 1)
    return (lane >= HEAD_DIM) == (head == 1), lane % HEAD_DIM


def attend_strips(shifted, v_ref, out_ref, root_ref, early_ref, late_ref):
    values = v_ref[...].T
    least = None
    for strip in STRIPS:
        first, past, stop = strip
        outs, roots = [], []
        for head in range(2):
            powers = jnp.exp2(shifted(head, strip))
            total = jnp.sum(powers, 0, keepdims=True)
            least = jnp.min(total) if least is None else jnp.minimum(least, jnp.min(total))
            root = 1.0 / total
            powers = low(powers)
            if past <= EARLY:
                early_ref[head, :, first:past] = powers
            else:
                late_ref[head, 0:stop, first - EARLY : past - EARLY] = powers
            rows = slice(head * HEAD_DIM, (head + 1) * HEAD_DIM)
            outs.append(dot(values[rows, 0:stop], powers) * root)
            roots.append(jnp.broadcast_to(root, (HEAD_DIM, past - first)))
        out_ref[first:past, :] = low(jnp.concatenate(outs, 0).T)
        root_ref[first:past, :] = jnp.concatenate(roots, 0).T
    return least


def attend_kernel(
    q_ref, k_ref, v_ref, query_ref, key_ref, lo_ref, hi_ref, out_ref, root_ref, early_ref, late_ref
):
    factor = HEAD_DIM**-0.5 * LOG2E
    squares = wide(k_ref[...]) * wide(k_ref[...])
    keys, longest = [], []
    for head in range(2):
        own, _ = own_lanes(head)
        keys.append(jnp.where(own, k_ref[...], key_ref[...]))
        length = jnp.sum(jnp.where(own, squares, 0.0), 1, keepdims=True)
        longest.append(jnp.max(length, 0, keepdims=True))

    def below_bound(head, strip):
        first, past, stop = strip
        own, lane = own_lanes(head)
        q = q_ref[first:past, :]
        length = jnp.sum(jnp.where(own, wide(q) * wide(q), 0.0), 1, keepdims=True)
        bound = jnp.sqrt(length * longest[head]) * 1.01
        beside = jnp.where(lane == BOUND_LANE, low(-bound), query_ref[first:past, :])
        return dot_nt(keys[head][0:stop], jnp.where(own, q, beside)) * factor

    outs = (v_ref, out_ref, root_ref, early_ref, late_ref)
    least = attend_strips(below_bound, *outs)

    @pl.when(jnp.logical_not(least > 1e-20))
    def _():
        def below_maximum(head, strip):
            first, past, stop = strip
            own, _ = own_lanes(head)
            q = q_ref[first:past, :]
            scores = dot_nt(k_ref[0:stop, :], jnp.where(own, q, jnp.zeros_like(q)))
            key = lax.broadcasted_iota(jnp.int32, scores.shape, 0)
            allowed = (key >= lo_ref[:, first:past]) & (key < hi_ref[:, first:past])
            scores = jnp.where(allowed, scores, NEG)
            return (scores - jnp.max(scores, 0, keepdims=True)) * factor

        attend_strips(below_maximum, *outs)


def kept_specs(rows, base):
    return [
        pl.BlockSpec((2, STRIPS[0][2], EARLY), lambda i: (base + i, 0, 0)),
        pl.BlockSpec((2, rows, rows - EARLY), lambda i: (base + i, 0, 0)),
    ]


QUARTER_PAIRS = 2


def head_specs(rows, base):
    pair = lambda i: (base + i) // QUARTER_PAIRS * 3 * QUARTER_PAIRS + (base + i) % QUARTER_PAIRS
    part = lambda number: pl.BlockSpec((rows, PAIR), lambda i: (0, pair(i) + number * QUARTER_PAIRS))
    return [part(0), part(1), part(2)], pl.BlockSpec((rows, PAIR), lambda i: (0, base + i))


def attend(heads, lanes, first_key, past_key):
    rows, width = heads.shape[0], heads.shape[1] // 3
    pairs = width // PAIR
    parts, block = head_specs(rows, 0)
    beside = (*lanes, first_key, past_key)
    return pl.pallas_call(
        attend_kernel,
        grid=(pairs,),
        in_specs=parts + [whole(array) for array in beside],
        out_specs=[block, block] + kept_specs(rows, 0),
        out_shape=[
            jax.ShapeDtypeStruct((rows, width), jnp.bfloat16),
            jax.ShapeDtypeStruct((rows, width), jnp.float32),
            jax.ShapeDtypeStruct((2 * pairs, STRIPS[0][2], EARLY), jnp.bfloat16),
            jax.ShapeDtypeStruct((2 * pairs, rows, rows - EARLY), jnp.bfloat16),
        ],
        compiler_params=params(),
        cost_estimate=takes(20),
        name="attend",
    )(heads, heads, heads, *beside)


def attend_back_kernel(
    q_ref, k_ref, v_ref, g_ref, o_ref, root_ref, early_ref, late_ref, cos_ref, up_ref, down_ref,
    out_ref, sums_ref, keys_acc, values_acc, queries_acc,
):
    pair = pl.program_id(0)
    pairs = out_ref.shape[1] // (3 * PAIR)
    scale = HEAD_DIM**-0.5
    keys = k_ref[...].T
    values = []
    for head in range(2):
        own, lane = own_lanes(head)
        values.append(jnp.where(own, v_ref[...], low(jnp.where(lane < 3, 1.0, 0.0))))
    for first, past, stop in STRIPS[::-1]:
        q = q_ref[first:past, :]
        g = wide(g_ref[first:past, :]) * root_ref[first:past, :]
        inner = g * wide(o_ref[first:past, :])
        g = low(g)
        zero = jnp.zeros_like(g)
        for head in range(2):
            own, lane = own_lanes(head)
            rows = slice(head * HEAD_DIM, (head + 1) * HEAD_DIM)
            shift = -jnp.sum(jnp.where(own, inner, 0.0), 1, keepdims=True)
            beside = zero
            for number in range(3):
                part = low(shift)
                shift = shift - wide(part)
                beside = jnp.where(lane == number, part, beside)
            if past <= EARLY:
                powers = early_ref[head, :, first:past]
            else:
                powers = late_ref[head, 0:stop, first - EARLY : past - EARLY]
            g_scores = low(wide(powers) * dot_nt(values[head][0:stop], jnp.where(own, g, beside)))
            queries_acc[rows, first:past] = dot(keys[rows, 0:stop], g_scores)
            g_keys = dot(g_scores, jnp.where(own, q, zero))
            g_values = dot(powers, jnp.where(own, g, zero))
            if head == 0:
                total_keys, total_values = g_keys, g_values
            else:
                total_keys, total_values = total_keys + g_keys, total_values + g_values
        if past == STRIPS[-1][1]:
            keys_acc[...] = total_keys
            values_acc[...] = total_values
        else:
            keys_acc[0:stop, :] += total_keys
            values_acc[0:stop, :] += total_values
    cos, up, down = cos_ref[...], -up_ref[...], -down_ref[...]
    grads = (
        low(spin(queries_acc[...].T * scale, cos, up, down)),
        low(spin(keys_acc[...] * scale, cos, up, down)),
        low(values_acc[...]),
    )
    for number, grad in enumerate(grads):
        lanes = pl.ds(pl.multiple_of((number * pairs + pair) * PAIR, PAIR), PAIR)
        out_ref[:, lanes] = grad
        sums_ref[:, lanes] = fold(wide(grad))


def attend_back(quarter, heads, g, out, root, early, late, tables):
    rows, width = g.shape
    pairs = width // PAIR
    parts, block = head_specs(rows, quarter * pairs)
    return pl.pallas_call(
        attend_back_kernel,
        grid=(pairs,),
        in_specs=parts
        + [pl.BlockSpec((rows, PAIR), lambda i: (0, i)), block, block]
        + kept_specs(rows, quarter * pairs)
        + [whole(table) for table in tables],
        out_specs=[
            pl.BlockSpec((rows, 3 * width), lambda i: (0, 0)),
            pl.BlockSpec((8, 3 * width), lambda i: (0, 0)),
        ],
        out_shape=[
            jax.ShapeDtypeStruct((rows, 3 * width), jnp.bfloat16),
            jax.ShapeDtypeStruct((8, 3 * width), jnp.float32),
        ],
        scratch_shapes=[
            pltpu.VMEM((rows, PAIR), jnp.float32),
            pltpu.VMEM((rows, PAIR), jnp.float32),
            pltpu.VMEM((PAIR, rows), jnp.float32),
        ],
        compiler_params=params(56),
        cost_estimate=takes(16),
        name="attend_back",
    )(heads, heads, heads, g, out, root, early, late, *tables)


def merge_kernel(count, *refs):
    rights, lefts = refs[: 2 * count], refs[2 * count : 3 * count]
    x_ref, bias_ref, gain_ref, shift_ref, residual_ref, out_ref = refs[3 * count :]
    total = wide(x_ref[...]) + bias_ref[...]
    for number, right in enumerate(rights):
        left, width = lefts[number // 2], right.shape[0]
        total = total + dot(left[:, number % 2 * width : (number % 2 + 1) * width], right[...])
    residual_ref[...] = total
    normed, _ = standardize(total)
    out_ref[...] = low(normed * gain_ref[...] + shift_ref[...])


def merge(lefts, rights, x, bias, gain, shift, block=320):
    rows, depth = x.shape
    row = lambda array: pl.BlockSpec((block, array.shape[1]), lambda i: (i, 0))
    vectors = (bias[None], gain[None], shift[None])
    return pl.pallas_call(
        functools.partial(merge_kernel, len(lefts)),
        grid=(rows // block,),
        in_specs=[whole(w) for w in rights]
        + [row(a) for a in lefts]
        + [row(x)]
        + [whole(v) for v in vectors],
        out_specs=[row(x), row(x)],
        out_shape=[
            jax.ShapeDtypeStruct((rows, depth), jnp.float32),
            jax.ShapeDtypeStruct((rows, depth), jnp.bfloat16),
        ],
        compiler_params=params(),
        cost_estimate=takes(8),
        name="merge",
    )(*rights, *lefts, x, *vectors)


def expand_kernel(chunk, count, x_ref, *refs):
    weights, biases = refs[:count], refs[count : 2 * count]
    actives, slopes = refs[2 * count : 3 * count], refs[3 * count :]
    for w_ref, b_ref, active_ref, slope_ref in zip(weights, biases, actives, slopes):
        for at in range(0, x_ref.shape[0], chunk):
            rows = slice(at, at + chunk)
            v = dot(x_ref[rows, :], w_ref[...]) + b_ref[...]
            below = 0.5 + 0.5 * lax.erf(v * ROOT_HALF)
            active_ref[rows, :] = low(v * below)
            slope_ref[rows, :] = low(below + v * jnp.exp(-0.5 * v * v) * GAUSS_NORM)


def expand(x, weights, biases, block=512, chunk=256):
    rows, depth = x.shape
    count, width = len(weights), weights[0].shape[1]
    column = lambda size: pl.BlockSpec((size, block), lambda i: (0, i))
    return pl.pallas_call(
        functools.partial(expand_kernel, chunk, count),
        grid=(width // block,),
        in_specs=[whole(x)] + [column(depth)] * count + [column(1)] * count,
        out_specs=[column(rows)] * (2 * count),
        out_shape=[jax.ShapeDtypeStruct((rows, width), jnp.bfloat16)] * (2 * count),
        compiler_params=params(),
        cost_estimate=takes(14),
        name="expand",
    )(x, *weights, *[bias[None] for bias in biases])


def reduce_kernel(count, half, side_ref, *refs):
    rights, lefts = refs[:count], refs[count : 2 * count]
    x_ref, bias_ref, send_ref, keep_ref = refs[2 * count :]
    total = x_ref[...] + bias_ref[...]
    for left, right in zip(lefts, rights):
        total = total + dot(left[...], right[...])

    @pl.when(pl.program_id(0) < half)
    def _():
        send_ref[...] = low(total)

    @pl.when(pl.program_id(0) >= half)
    def _():
        keep_ref[...] = low(total)


def reduce_rows(side, lefts, rights, x, bias, block=320):
    rows, depth = x.shape
    half = rows // 2 // block
    at = lambda i, side: jnp.where(i < half, (1 - side[0]) * half + i, side[0] * half + i - half)
    row = lambda array: pl.BlockSpec((block, array.shape[1]), lambda i, side: (at(i, side), 0))
    return pl.pallas_call(
        functools.partial(reduce_kernel, len(lefts), half),
        grid_spec=pltpu.PrefetchScalarGridSpec(
            num_scalar_prefetch=1,
            grid=(2 * half,),
            in_specs=[whole(w) for w in rights]
            + [row(a) for a in lefts]
            + [row(x), whole(bias[None])],
            out_specs=[
                pl.BlockSpec((block, depth), lambda i, side: (jnp.minimum(i, half - 1), 0)),
                pl.BlockSpec((block, depth), lambda i, side: (jnp.maximum(i - half, 0), 0)),
            ],
        ),
        out_shape=[jax.ShapeDtypeStruct((rows // 2, depth), jnp.bfloat16)] * 2,
        compiler_params=params(),
        cost_estimate=takes(0.1),
        name="reduce_rows",
    )(side, *rights, *lefts, x, bias[None])


def back_kernel(count, at_ref, *refs):
    rights, lefts = refs[:count], refs[count : 2 * count]
    base_ref, above_ref, gain_ref, out_ref, sums_ref = refs[2 * count :]

    @pl.when(pl.program_id(0) == 0)
    def _():
        sums_ref[...] = jnp.zeros_like(sums_ref)

    g = dot_nt(lefts[0][...], rights[0][...])
    for left, right in zip(lefts[1:], rights[1:]):
        g = g + dot_nt(left[...], right[...])
    normed, scale = standardize(wide(base_ref[...]))
    u = g * gain_ref[...]
    above = wide(above_ref[...])
    inner = jnp.mean(u, -1, keepdims=True) + normed * jnp.mean(u * normed, -1, keepdims=True)
    out = low(above + scale * (u - inner))
    out_ref[...] = out
    sums_ref[0] += fold(g * normed)
    sums_ref[1] += fold(g)
    sums_ref[2] += fold(wide(out))
    sums_ref[3] += fold(above)


def back_norm(at, lefts, rights, base, above, gain, block=320):
    rows, depth = base.shape
    row = lambda array: pl.BlockSpec((block, array.shape[1]), lambda i, at: (at[i], 0))
    return pl.pallas_call(
        functools.partial(back_kernel, len(lefts)),
        grid_spec=pltpu.PrefetchScalarGridSpec(
            num_scalar_prefetch=1,
            grid=(at.size,),
            in_specs=[whole(w) for w in rights]
            + [row(a) for a in lefts]
            + [row(base), row(above), whole(gain[None])],
            out_specs=[
                pl.BlockSpec((block, depth), lambda i, at: (i, 0)),
                pl.BlockSpec((4, 8, depth), lambda i, at: (0, 0, 0)),
            ],
        ),
        out_shape=[
            jax.ShapeDtypeStruct((rows, depth), jnp.bfloat16),
            jax.ShapeDtypeStruct((4, 8, depth), jnp.float32),
        ],
        compiler_params=params(),
        cost_estimate=takes(0.1 if base.dtype == jnp.float32 else 20),
        name="back_norm",
    )(at, *rights, *lefts, base, above, gain[None])


def place_kernel(steps, flag_ref, mine_ref, theirs_ref, out_ref):
    @pl.when(pl.program_id(0) < steps)
    def _():
        out_ref[...] = mine_ref[...].astype(out_ref.dtype).reshape(out_ref.shape)

    @pl.when(pl.program_id(0) >= steps)
    def _():
        out_ref[...] = theirs_ref[...].astype(out_ref.dtype).reshape(out_ref.shape)


def place(flag, mine, theirs, steps, in_block, in_index, out_shape, out_block, out_index, dtype):
    def target(i, flag):
        return out_index(jnp.where(i < steps, flag[0], 1 - flag[0]), jnp.where(i < steps, i, i - steps))

    return pl.pallas_call(
        functools.partial(place_kernel, steps),
        grid_spec=pltpu.PrefetchScalarGridSpec(
            num_scalar_prefetch=1,
            grid=(2 * steps,),
            in_specs=[
                pl.BlockSpec(in_block, lambda i, flag: in_index(jnp.minimum(i, steps - 1))),
                pl.BlockSpec(in_block, lambda i, flag: in_index(jnp.maximum(i - steps, 0))),
            ],
            out_specs=pl.BlockSpec(out_block, target),
        ),
        out_shape=jax.ShapeDtypeStruct(out_shape, dtype),
        compiler_params=params(),
        cost_estimate=takes(4),
        name="place",
    )(flag, mine, theirs)


def place_rows(flag, mine, theirs, steps, dtype):
    rows, width = mine.shape
    block = (rows // steps, width)
    return place(
        flag, mine, theirs, steps, block, lambda j: (j, 0),
        (2 * rows, width), block, lambda half, j: (half * steps + j, 0), dtype,
    )


def place_columns(flag, mine, theirs, steps, dtype):
    rows, width = mine.shape
    block = (rows // steps, width)
    return place(
        flag, mine, theirs, steps, block, lambda j: (j, 0),
        (rows, 2 * width), block, lambda half, j: (j, half), dtype,
    )


def place_heads(flag, mine, theirs, dtype):
    rows, width = mine.shape[0], mine.shape[1] // 3
    return place(
        flag, mine, theirs, 3, (rows, width), lambda j: (0, j),
        (3, rows, 2 * width), (1, rows, width), lambda half, j: (j, 0, half), dtype,
    )


def column_sums(matrix):
    unit_column = jnp.ones((matrix.shape[0],), matrix.dtype)
    return jnp.dot(unit_column, matrix, preferred_element_type=jnp.float32)


KEEP, SEND = 0, 1
OWN, FAR = 0, 1
QUARTERS = ((FAR, SEND), (FAR, KEEP), (OWN, SEND), (OWN, KEEP))


def on_device(
    spread,
    tokens,
    cotangent,
    patch_count,
    first_gain,
    first_shift,
    heads_weight,
    heads_bias,
    merge_weight,
    merge_bias,
    second_gain,
    second_shift,
    expand_weight,
    expand_bias,
    reduce_weight,
    reduce_bias,
):
    levels = spread.bit_length() - 1
    rest = list(range(1, levels))
    chunks = spread // 2
    location = lax.axis_index("dp")
    side = lax.axis_index("mp")
    sides = side[None].astype(jnp.int32)
    previous = []

    def bit(level):
        return (location >> level) & 1

    core = bit(0)[None].astype(jnp.int32)

    def tie(array, *others):
        return lax.optimization_barrier((array,) + others)[0] if others else array

    def after(array):
        return tie(array, *previous)

    def did(*arrays):
        previous[:] = arrays
        return arrays[0] if len(arrays) == 1 else arrays

    def swap(array, level):
        return lax.ppermute(array, "dp", [(i, i ^ (1 << level)) for i in range(spread)])

    def cross(array):
        return lax.ppermute(array, "mp", [(0, 1), (1, 0)])

    def half_of(array, flag, axis=0):
        size = array.shape[axis] // 2
        return lax.dynamic_slice_in_dim(array, flag * size, size, axis)

    def chunk_of(array):
        size = array.shape[0] // chunks
        return lax.dynamic_slice_in_dim(array, (location >> 1) * size, size, 0)

    def split(array, level, open_levels=None):
        left = 1 << sum(other > level for other in (open_levels or rest))
        four = array.reshape(left, 2, -1, array.shape[1])
        part = lambda flag: lax.dynamic_index_in_dim(four, flag, 1, False).reshape(-1, array.shape[1])
        return part(bit(level)), part(1 - bit(level))

    def join(mine, theirs, level, open_levels=None):
        left = 1 << sum(other > level for other in (open_levels or rest))
        four = lambda array: array.reshape(left, 1, -1, array.shape[1])
        pair = jnp.where(
            bit(level) == 0,
            jnp.concatenate([four(mine), four(theirs)], 1),
            jnp.concatenate([four(theirs), four(mine)], 1),
        )
        return pair.reshape(-1, mine.shape[1])

    def quarters_of(own, axis):
        return [half_of(own, bit(0), axis), half_of(own, 1 - bit(0), axis)]

    tokens, cotangent = tokens[:, 0], cotangent[:, 0]
    heads_three = heads_weight.transpose(1, 0, 2)
    near = rest[:2]
    piece_rows = heads_three.shape[1] >> len(near)
    piece_width = heads_three.shape[2] // 2
    piece_at = ((location >> 1) & ((1 << len(near)) - 1)) * piece_rows
    heads_piece = jnp.concatenate(
        [
            lax.dynamic_slice(
                heads_three, (n, piece_at, bit(0) * piece_width), (1, piece_rows, piece_width)
            )[0]
            for n in range(3)
        ],
        1,
    )
    heads_cross = cross(heads_piece)
    tokens_far = cross(lax.dynamic_index_in_dim(tie(tokens, heads_piece), 1 - side, 0, False))
    heads_own = [
        jnp.concatenate([half_of(heads_three[n], flag, 1) for n in range(3)], 1)
        for flag in (bit(0), 1 - bit(0))
    ]
    merge_own = quarters_of(merge_weight, 0)
    expand_own = quarters_of(expand_weight, 1)
    reduce_own = quarters_of(reduce_weight, 0)
    pack = lambda hb, eb: jnp.concatenate([hb.reshape(-1), eb])
    bias_own = [
        pack(half_of(heads_bias, flag, 1), half_of(expand_bias, flag)) for flag in (bit(0), 1 - bit(0))
    ]
    three = heads_bias.size // 2
    up_piece = jnp.concatenate([chunk_of(expand_own[KEEP]), chunk_of(merge_own[KEEP])])
    down_piece = chunk_of(reduce_own[KEEP])

    count_one = lax.dynamic_index_in_dim(patch_count[:, 0], side, 0, False)
    length = 2 * tokens.shape[1]
    first_key, past_key, frame_id, patch_row, column, segment, starts = slot_layout(count_one, length)
    tables = rotary_tables(frame_id, patch_row, column)
    lanes = segment_lanes(first_key, past_key, segment, starts)
    first_key, past_key = first_key[None], past_key[None]

    bias_pieces = jnp.concatenate(bias_own)
    did(*heads_own, *merge_own)
    heads_piece = did(after(heads_cross))
    if len(near) > 1:
        heads_next = swap(heads_piece, near[1])
        expand_own = quarters_of(after(expand_weight), 1)
        up_piece = jnp.concatenate([chunk_of(expand_own[KEEP]), chunk_of(merge_own[KEEP])])
        did(*expand_own, up_piece)
        heads_piece = did(join(after(heads_piece), heads_next, near[1], near[1:]))
    heads_next = swap(heads_piece, near[0])
    up_piece = cross(tie(up_piece, heads_piece))
    bias_both = cross(tie(bias_pieces, heads_piece))
    did(heads_piece, down_piece, *heads_own, *merge_own, *expand_own, *reduce_own, *tables, *lanes)
    bias_far = [bias_both[: bias_both.size // 2], bias_both[bias_both.size // 2 :]]
    stream, first_out = did(*enter(sides, after(tokens), tokens_far, first_gain, first_shift))
    heads, seen = {}, {}
    heads_all = [heads_own, None]
    bias_all = (bias_own, bias_far)

    def look(p):
        biases = [bias[:three] for bias in bias_all[p]]
        heads[p] = did(project(after(first_out), heads_all[p], biases, tables))

    def attention(p):
        seen[p] = did(*attend(after(heads[p]), lanes, first_key, past_key))

    def gathered(array, *splits):
        array = lax.all_gather(array, "dp", axis=0, tiled=True)
        array = array.reshape(chunks, 2, -1, array.shape[1])
        quarters, at = [], 0
        for size in splits:
            part = array[:, :, at : at + size]
            quarters.append(
                [
                    lax.dynamic_index_in_dim(part, flag, 1, False).reshape(-1, array.shape[3])
                    for flag in (bit(0), 1 - bit(0))
                ]
            )
            at += size
        return quarters

    look(OWN)
    up_sizes = (expand_own[0].shape[0] // chunks, merge_own[0].shape[0] // chunks)
    up_gathered = gathered(after(up_piece), *up_sizes)
    down_piece = cross(after(down_piece))
    heads_piece = did(join(after(heads_piece), heads_next, near[0], near))
    heads_all[FAR] = [heads_piece, swap(heads_piece, 0)]
    attention(OWN)
    cotangent_far = cross(after(lax.dynamic_index_in_dim(cotangent, 1 - side, 0, False)))
    look(FAR)
    (reduce_far,) = gathered(after(down_piece), down_piece.shape[0])
    attention(FAR)
    expand_far, merge_far = ([after(q) for q in quarters] for quarters in up_gathered)
    merge_all = (merge_own, merge_far)
    expand_all = (expand_own, expand_far)
    reduce_all = (reduce_own, reduce_far)
    width = seen[OWN][0].shape[1] // 2
    residual, second_out = did(
        *merge(
            [seen[OWN][0], seen[FAR][0]], [merge_all[p][c] for p in (OWN, FAR) for c in (KEEP, SEND)],
            after(stream), merge_bias, second_gain, second_shift,
        )
    )
    grad_two = did(collect(sides, after(cotangent), cotangent_far))

    active, slope, grad_pre = {}, {}, {}

    def widen(p):
        active[p, KEEP], active[p, SEND], slope[p, KEEP], slope[p, SEND] = did(
            *expand(after(second_out), expand_all[p], [bias[three:] for bias in bias_all[p]])
        )

    def back_active(p, c):
        grad_pre[p, c] = did(low(dot_nt(after(grad_two), reduce_all[p][c]) * wide(slope[p, c])))

    def product(left, right, *arrived):
        total = dot_tn(after(left), right)
        for array in arrived:
            total = total + wide(array)
        return did(low(total))

    def scattered(array, level, open_levels=None):
        keep, send = split(after(array), level, open_levels or rest[rest.index(level) :])
        did(send)
        return keep, swap(send, level)

    def summed(keep, arrived):
        return did(low(wide(after(keep)) + wide(arrived)))

    def rows_out(keep, arrived, dtype):
        return place_rows(sides, keep, arrived, 4, dtype).reshape(2, 1, length // 2, -1)

    widen(FAR)
    sent = swap(product(active[FAR, SEND], grad_two), 0)
    widen(OWN)
    reduce_far_sum = product(active[FAR, KEEP], grad_two, sent)
    reduce_cross = cross(reduce_far_sum)
    sent = swap(product(active[OWN, SEND], grad_two), 0)
    back_active(FAR, SEND)
    reduce_sum = product(active[OWN, KEEP], grad_two, sent)
    back_active(FAR, KEEP)
    sent = swap(product(second_out, grad_pre[FAR, SEND]), 0)
    back_active(OWN, SEND)
    expand_far_sum = product(second_out, grad_pre[FAR, KEEP], sent)
    back_active(OWN, KEEP)
    sent = swap(product(second_out, grad_pre[OWN, SEND]), 0)
    expand_sum = product(second_out, grad_pre[OWN, KEEP], sent)
    expand_cross = cross(expand_far_sum)
    blocks = jnp.arange(length // 320, dtype=jnp.int32)
    grad_one, second_sums = did(
        *back_norm(
            blocks, [grad_pre[q] for q in QUARTERS], [expand_all[p][c] for p, c in QUARTERS],
            after(residual), grad_two, second_gain,
        )
    )
    grad_mixed, grad_heads, head_sums = {}, {}, {}

    def back_mixed(p, c):
        grad_mixed[p, c] = did(low(dot_nt(after(grad_one), merge_all[p][c])))

    def back_attention(q):
        p, c = q
        grad_heads[q], sums = did(
            *attend_back(c, heads[p], after(grad_mixed[q]), *seen[p], tables)
        )
        head_sums[q] = jnp.sum(sums, 0)

    merge_far_sum = product(seen[FAR][0], grad_one)
    sent_far = swap(merge_far_sum[width:], 0)
    merge_sum = product(seen[OWN][0], grad_one)
    sent_own = swap(merge_sum[width:], 0)
    for p, c in QUARTERS:
        back_mixed(p, c)
    merge_far_sum = summed(merge_far_sum[:width], sent_far)
    merge_sum = summed(merge_sum[:width], sent_own)
    merge_cross = cross(tie(merge_far_sum, reduce_cross))
    reduce_sum = summed(reduce_sum, reduce_cross)
    reduce_keep, reduce_next = scattered(reduce_sum, rest[0])
    back_attention((FAR, SEND))
    reduce_sum = summed(reduce_keep, reduce_next)
    reduce_keep, reduce_next = scattered(reduce_sum, rest[1])
    sent = swap(product(first_out, grad_heads[FAR, SEND]), 0)
    expand_sum = summed(expand_sum, expand_cross)
    expand_keep, expand_next = scattered(expand_sum, rest[0])
    merge_sum = summed(merge_sum, merge_cross)
    merge_keep, merge_next = scattered(merge_sum, rest[0])
    reduce_sum = summed(reduce_keep, reduce_next)
    for level in rest[2:]:
        reduce_keep, reduce_next = scattered(reduce_sum, level)
        reduce_sum = low(wide(reduce_keep) + wide(reduce_next))
    back_attention((FAR, KEEP))
    reduce_total = lax.all_gather(after(reduce_sum), "dp", axis=0, tiled=True)
    heads_far_sum = product(first_out, grad_heads[FAR, KEEP], sent)
    heads_cross = cross(heads_far_sum)
    expand_sum = summed(expand_keep, expand_next)
    merge_sum = summed(merge_keep, merge_next)
    expand_keep, expand_next = scattered(expand_sum, rest[1])
    merge_keep, merge_next = scattered(merge_sum, rest[1])
    back_attention((OWN, SEND))
    expand_sum = summed(expand_keep, expand_next)
    merge_sum = summed(merge_keep, merge_next)
    for level in rest[2:]:
        expand_keep, expand_next = scattered(expand_sum, level)
        merge_keep, merge_next = scattered(merge_sum, level)
        expand_sum = low(wide(expand_keep) + wide(expand_next))
        merge_sum = low(wide(merge_keep) + wide(merge_next))
    sent = swap(product(first_out, grad_heads[OWN, SEND]), 0)
    back_attention((OWN, KEEP))
    expand_total = lax.all_gather(
        after(jnp.concatenate([expand_sum, merge_sum])), "dp", axis=0, tiled=True
    )
    heads_sum = product(first_out, grad_heads[OWN, KEEP], sent, heads_cross)
    orders = [rest[:1] + rest[2:] + rest[1:2], rest[1:2] + rest[:1] + rest[2:]]
    middle = heads_sum.shape[1] // 2
    heads_sums = [heads_sum[:, :middle], heads_sum[:, middle:]]

    def both_scattered(n):
        return [scattered(total, order[n], order[n:]) for total, order in zip(heads_sums, orders)]

    def both_summed(pairs):
        return [summed(*pair) for pair in pairs]

    def in_rows(array):
        return wide(array.transpose(1, 0, 2, 3).reshape(-1, array.shape[3]))

    reduce_total = reduce_total.reshape(chunks, 2, -1, reduce_total.shape[1])
    expand_total = expand_total.reshape(chunks, 2, -1, expand_total.shape[1])
    rows = expand_sum.shape[0]

    pairs = both_scattered(0)
    lefts = [grad_heads[q] for q in QUARTERS]
    rights = [heads_all[p][c] for p, c in QUARTERS]
    half = length // 2
    blocks = (blocks + (1 - sides) * (half // 320)) % (length // 320)
    tokens_rows, first_sums = did(
        *back_norm(blocks, lefts, rights, stream, grad_one, after(first_gain))
    )
    tokens_cross, tokens_keep = cross(tokens_rows[:half]), tokens_rows[half:]
    heads_sums = both_summed(pairs)
    pairs = both_scattered(1)

    small = {q: jnp.concatenate([head_sums[q], column_sums(grad_pre[q])]) for q in QUARTERS}
    both = jnp.concatenate(
        [
            jnp.sum(part, 0)
            for part in (
                first_sums[0], first_sums[1], second_sums[0], second_sums[1], second_sums[2], second_sums[3],
            )
        ]
    )
    far_send, own_send, both = did(*(after(v) for v in (small[FAR, SEND], small[OWN, SEND], both)))
    arrived = swap(jnp.concatenate([far_send, own_send, both]), 0)
    size = own_send.size
    layer_send, layer_keep = did(
        *reduce_rows(
            sides, [active[q] for q in QUARTERS], [reduce_all[p][c] for p, c in QUARTERS],
            after(residual), reduce_bias,
        )
    )
    heads_sums = both_summed(pairs)
    mine = jnp.concatenate([small[FAR, KEEP] + arrived[:size], small[OWN, KEEP], both])
    mine = did(
        jnp.concatenate([mine[:size], mine[size:] + after(arrived)[size:]])
    )
    for n in range(2, len(rest) - 1):
        pairs = both_scattered(n)
        small_next = swap(mine, rest[n])
        heads_sums = both_summed(pairs)
        mine = did(mine + after(small_next))
    arrived = [swap(total, order[-1]) for total, order in zip(heads_sums, orders)]
    small_next = swap(mine, rest[-1])
    reduce_out = in_rows(after(reduce_total))
    mine, reduce_out = lax.optimization_barrier((mine, reduce_out))
    did(mine)
    heads_sums = both_summed(zip(heads_sums, arrived))
    mine = did(mine + after(small_next))
    layer_far = cross(tie(layer_send, tokens_cross))
    for n in range(len(rest) - 1)[::-1]:
        arrived = [swap(total, order[n]) for total, order in zip(heads_sums, orders)]
        small_next = swap(mine, rest[n]) if n < 2 else None
        if n == len(rest) - 2:
            tokens_out = rows_out(after(tokens_keep), tokens_cross, jnp.float32)
            mine, tokens_out = lax.optimization_barrier((mine, tokens_out))
            did(mine)
        if n == 0:
            expand_out = wide(
                jnp.concatenate(
                    [
                        after(expand_total)[:, half, :rows].reshape(-1, expand_total.shape[3])
                        for half in range(2)
                    ],
                    1,
                )
            )
            mine, expand_out = lax.optimization_barrier((mine, expand_out))
            did(mine)
        heads_sums = [
            did(join(after(total), other, order[n], order[n:]))
            for total, other, order in zip(heads_sums, arrived, orders)
        ]
        if n < 2:
            mine = did(mine + after(small_next))
    layer_out = rows_out(layer_keep, layer_far, jnp.bfloat16)
    heads_sum = jnp.concatenate(heads_sums, 1)
    heads_next = swap(heads_sum, 0)
    arrived = cross(jnp.concatenate([mine[:size], mine[2 * size :]]))
    both = mine[2 * size :] + arrived[size:]
    mine = mine[size : 2 * size] + arrived[:size]
    theirs = swap(mine, 0)
    first = jnp.where(bit(0) == 0, mine, theirs)
    second = jnp.where(bit(0) == 0, theirs, mine)
    heads_bias_total = jnp.concatenate([first[:three].reshape(3, -1), second[:three].reshape(3, -1)], 1)
    expand_bias_total = jnp.concatenate([first[three:], second[three:]])
    (first_gain_total, first_shift_total, second_gain_total, second_shift_total, merge_bias_total,
     reduce_bias_total) = both.reshape(6, -1)
    heads_out = place_heads(core, heads_sum, heads_next, jnp.float32)
    return (
        layer_out,
        tokens_out,
        first_gain_total,
        first_shift_total,
        heads_out.transpose(1, 0, 2),
        heads_bias_total,
        in_rows(expand_total[:, :, rows:]),
        merge_bias_total,
        second_gain_total,
        second_shift_total,
        expand_out,
        expand_bias_total,
        reduce_out,
        reduce_bias_total,
    )


def solution(mesh):
    rows = P(None, "dp", "mp", None)
    columns = P(None, "mp")
    heads = P(None, None, "mp")
    return jax.shard_map(
        functools.partial(on_device, mesh.shape["dp"]),
        mesh=mesh,
        in_specs=(
            rows, rows, P(None, "dp"), P(), P(), heads, columns, P("mp", None), P(), P(), P(), columns,
            P("mp"), P("mp", None), P(),
        ),
        out_specs=(
            rows, rows, P(), P(), heads, columns, P("mp", None), P(), P(), P(), columns, P("mp"),
            P("mp", None), P(),
        ),
        check_vma=False,
    )
```
